128 devices in a mesh: lat: 8 (over y, core), lon: 16 (over x, z).
Axes of the slice: x: 4, y: 4, z: 4, core: 2. Of those that a mesh axis runs over, the one named last changes fastest.
Arguments:
- state: bfloat16 [64, 1024, 256], P('lat', 'lon'), may hold values from -6 to 6
- background: bfloat16 [64, 1024, 256], P('lat', 'lon'), may hold values from -6 to 6
- conv_in: bfloat16 [3, 3, 256, 256], replicated, may hold values from -0.125 to 0.125
- conv_out: bfloat16 [3, 3, 256, 256], replicated, may hold values from -0.125 to 0.125
- probe: float32 [256], replicated, may hold values from -0.375 to 0.375
- tile_ids: int32 [262144, 1], P(('lat', 'lon')), may hold values from 0 to 127; in each aligned block of 2048 rows (0 to 2047, 2048 to 4095, ...) at most 32 rows name the same one
- cell_taps: int32 [4, 262144], P(None, ('lat', 'lon')), may hold values from 0 to 511
- tap_weights: float32 [4, 262144], P(None, ('lat', 'lon')), may hold values from 0 to 1
- obs_values: float32 [262144], P(('lat', 'lon')), may hold values from -6 to 6
- obs_precision: float32 [262144], P(('lat', 'lon')), may hold values from 0.5 to 2
Outputs:
- grad_state: bfloat16 [64, 1024, 256], P('lat', 'lon')
- innovation: float32 [262144], P(('lat', 'lon'))
The draws below stay inside these ranges and needn't reach their ends.
Inputs may be any that keep to these rules, and one draw needn't show every extreme that they name: `tile_ids`: among the rows held by one device, no tile is named by more than 32 of them, a bound that some block reaches.
All inputs are finite; a program needn't handle non-finite values.
Results may differ from the reference program's by a relative error of at most 0.006.
Values may be sent and summed in bfloat16 or wider, within the bound.
A program may use at most 128 MiB of HBM per device.

```python
import math
import jax
import jax.numpy as jnp
import numpy as np

C = 256
TH = 8
TW = 64
OBS_DEV = 2048
TILES = 128
CAP = 32
CELLS = 512
NLAT = 64
NLON = 1024
OBS = 262144
N_LON = 16


def touch_ends(array, stream_key, low, high):
    longest = array.shape.index(max(array.shape))
    spots = []
    for shift in (0, 1):
        where = [jax.random.randint(jax.random.fold_in(stream_key, axis), (), 0, length) for axis, length in enumerate(array.shape)]
        where[longest] = (where[longest] + shift) % array.shape[longest]
        spots.append(tuple(where))
    return array.at[spots[0]].set(low).at[spots[1]].set(high)


def level_of(rng, extent, split, smallest, top_value):
    level = 1.0
    for dim, shards_of in split:
        draws = jax.random.uniform(jax.random.fold_in(jax.random.fold_in(rng, 6), dim), (shards_of,), jnp.float32, smallest / len(split), top_value / len(split))
        level = level * jnp.repeat(jnp.exp(draws), extent[dim] // shards_of).reshape((-1,) + (1,) * (len(extent) - 1 - dim))
    return level


def assign_block(own_key, own, number, rows, number_of, top, reach, lean):
    ranking = jax.random.permutation(own_key, number_of)
    crowded, ordinary = load_shares(number_of, rows * top, reach, lean, True), load_shares(number_of, rows * top, reach, lean, False)
    places = jnp.arange(number_of)

    def named(sizes, offset_by):
        used = int((sizes > 0).sum())
        fixed = max(1, used // 4)
        shifted = fixed + (places - fixed + offset_by * (used - fixed)) % max(1, number_of - fixed)
        return jnp.zeros((number_of,), jnp.int32).at[ranking[jnp.where(places < fixed, places, shifted)]].set(jnp.asarray(sizes, jnp.int32))

    sizes = jnp.where(number % 4 == 0, named(crowded, number // 4), named(ordinary, number - number // 4 - 1))
    mixed = jax.random.permutation(jax.random.fold_in(own, 3), number_of)
    source_of, sink = mixed[0:number_of // 2 * 2:2], mixed[1:number_of // 2 * 2:2]
    room = jnp.minimum(sizes[source_of] - 1, reach - sizes[sink]) // 2
    room = jnp.where((source_of == ranking[0]) | (sink == ranking[0]) | (sizes[sink] == 0), 0, jnp.maximum(room, 0))
    shifted = jax.random.randint(jax.random.fold_in(own, 4), (number_of // 2,), 0, 1 << 20) % (room + 1)
    sizes = sizes.at[source_of].add(-shifted).at[sink].add(shifted)
    labels = jnp.searchsorted(jnp.cumsum(sizes), jnp.arange(rows * top), side="right").astype(jnp.int32)
    listing = labels.reshape(top, rows).T
    listing = listing[jax.random.permutation(jax.random.fold_in(own, 1), rows)]
    offset_by = jax.random.randint(jax.random.fold_in(own, 2), (rows, 1), 0, top)
    return jnp.take_along_axis(listing, (jnp.arange(top)[None, :] + offset_by) % top, axis=1)


def load_shares(amount, total, reach, skew, full):
    portions = [(1 << 20) // math.isqrt(standing ** skew) + 1 for standing in range(1, amount + 1)]
    largest = reach if full else min(reach, max(-(-total // amount), total * portions[0] // sum(portions)))
    least = 1 if total - largest >= amount - 1 else 0
    counts, rest = [largest] + [least] * (amount - 1), total - largest - least * (amount - 1)
    while rest > 0:
        free = [i for i in range(1, amount) if counts[i] < largest] or [i for i in range(1, amount) if counts[i] < reach]
        mass, left = sum([portions[i] for i in free]), rest
        for i in free:
            addition = min(reach - counts[i], max(1, left * portions[i] // mass), rest)
            counts[i] = counts[i] + addition
            rest = rest - addition
    return np.array(counts)


def noise(own_key, extent, scale, bound, shards=(), held_as=jnp.bfloat16):
    entries = scale * jax.random.normal(own_key, extent, jnp.float32)
    if shards:
        entries = entries * level_of(own_key, extent, shards, -0.22, 0.18)
    return jnp.clip(entries, -bound, bound).astype(held_as)


def setup_inputs(seed: int = 0) -> dict:
    key_of = jax.random.split(jax.random.key(seed), 11)
    state = noise(key_of[0], (NLAT, NLON, C), 1.0, 6.0, ((0, 8), (1, 16)))
    background = noise(key_of[1], (NLAT, NLON, C), 1.0, 6.0, ((0, 8), (1, 16)))
    conv_in = noise(key_of[2], (3, 3, C, C), (9 * C) ** -0.5, 0.125)
    conv_out = noise(key_of[3], (3, 3, C, C), (9 * C) ** -0.5, 0.125)
    probe = noise(key_of[4], (C,), C ** -0.5, 0.375, (), jnp.float32)
    tile_ids_keys = jax.random.split(jax.random.fold_in(key_of[5], 1), OBS // OBS_DEV)
    tile_ids_turns = jax.random.permutation(jax.random.fold_in(key_of[5], 3), OBS // OBS_DEV)
    tile_ids = jax.vmap(lambda own, number: assign_block(jax.random.fold_in(key_of[5], 2), own, number, OBS_DEV, TILES, 1, CAP, 2))(tile_ids_keys, tile_ids_turns).reshape((OBS, 1))
    cell_taps = touch_ends(jax.random.randint(key_of[6], (4, OBS), 0, CELLS), jax.random.fold_in(key_of[6], 1), 0, CELLS - 1).astype(jnp.int32)
    tap_weights = jnp.clip(1.0 * jax.random.uniform(key_of[7], (4, OBS), jnp.float32) ** level_of(key_of[7], (4, OBS), ((1, 128),), -0.2, 0.2), 0.0, 1.0)
    obs_values = noise(key_of[8], (OBS,), 1.0, 6.0, ((0, 128),), jnp.float32)
    obs_precision = jnp.clip(jnp.exp(math.log(2.0) - 1.3862944 * jax.random.uniform(key_of[9], (OBS,), jnp.float32) ** level_of(key_of[9], (OBS,), ((0, 128),), -0.2, 0.2)), 0.5, 2.0)
    return {"state": state, "background": background, "conv_in": conv_in, "conv_out": conv_out, "probe": probe, "tile_ids": tile_ids, "cell_taps": cell_taps, "tap_weights": tap_weights, "obs_values": obs_values, "obs_precision": obs_precision}


def extend(field, width):
    tall = jnp.pad(field, ((width, width), (0, 0), (0, 0)))
    return jnp.concatenate([tall[:, -width:], tall, tall[:, :width]], axis=1)


def correlate(grown, kernel, flipped):
    height = grown.shape[0] - 2
    breadth = grown.shape[1] - 2
    chans = grown.shape[2]
    total = jnp.zeros((height * breadth, kernel.shape[3]), jnp.float32)
    for i in range(3):
        window = jnp.concatenate([grown[i:i + height, j:j + breadth] for j in range(3)], axis=2).reshape(height * breadth, 3 * chans)
        if flipped:
            stacked = jnp.concatenate([kernel[2 - i, 2 - j].T for j in range(3)], axis=0)
        else:
            stacked = kernel[i].reshape(3 * chans, kernel.shape[3])
        total = total + jnp.dot(window, stacked, preferred_element_type=jnp.float32)
    return total.reshape(height, breadth, kernel.shape[3])


def reference(state, background, conv_in, conv_out, probe, tile_ids, cell_taps, tap_weights, obs_values, obs_precision):
    before = correlate(extend(state, 1), conv_in, False)
    hidden = jax.nn.silu(before).astype(jnp.bfloat16)
    mixed = state.astype(jnp.float32) + correlate(extend(hidden, 1), conv_out, False)
    scalar = jnp.sum(mixed * probe, axis=-1).reshape(-1)
    tile = tile_ids[:, 0]
    lat_tile = tile // N_LON
    lon_tile = tile % N_LON
    flat = (lat_tile[None, :] * TH + cell_taps // TW) * NLON + lon_tile[None, :] * TW + cell_taps % TW
    predicted = jnp.sum(tap_weights * scalar[flat], axis=0)
    innovation = obs_precision * (predicted - obs_values)
    shares = tap_weights * (obs_precision * innovation)[None, :]
    spread = jnp.zeros((NLAT * NLON,), jnp.float32).at[flat.reshape(-1)].add(shares.reshape(-1))
    spread = spread.reshape(NLAT, NLON)
    adjoint = ((mixed - background.astype(jnp.float32)) + spread[:, :, None] * probe[None, None, :]).astype(jnp.bfloat16)
    back_hidden = correlate(extend(adjoint, 1), conv_out, True)
    sigma = jax.nn.sigmoid(before)
    back_before = (back_hidden * sigma * (1.0 + before * (1.0 - sigma))).astype(jnp.bfloat16)
    grad_state = (adjoint.astype(jnp.float32) + correlate(extend(back_before, 1), conv_in, True)).astype(jnp.bfloat16)
    return grad_state, innovation
```

```python
import functools

import jax
import jax.numpy as jnp
from jax import lax
from jax.experimental import pallas as pl
from jax.experimental.pallas import tpu as pltpu
from jax.sharding import PartitionSpec as P

MESH = pl.DeviceIdType.MESH
B16 = jnp.bfloat16
F32 = jnp.float32
I32 = jnp.int32
ROWS, COLS, CH = 8, 64, 256
WIDE = 96
PITCH = 80
LATS, LONS = 8, 16
TILES = LATS * LONS
COUNT = 2048
CAP = 32
NT = (((1,), (1,)), ((), ()))
SIDES = [(a, b) for a in (-1, 0, 1) for b in (-1, 0, 1) if (a, b) != (0, 0)]
CORNERS = [s for s in SIDES if s[1] != 0]


def iota(shape, dim):
    return lax.broadcasted_iota(I32, shape, dim)


def halves(x):
    high = x.astype(B16)
    return high, (x - high.astype(F32)).astype(B16)


def products(field, rows, pitch, weights, flipped, prod):
    count = rows * pitch
    lhs = jnp.concatenate(
        [field[i : i + rows].reshape(count, CH) for i in range(3)], axis=1
    )
    for j in range(3):
        if flipped:
            rhs = jnp.concatenate([weights[2 - i, 2 - j] for i in range(3)], axis=1)
            out = lax.dot_general(lhs, rhs, NT, preferred_element_type=F32)
        else:
            rhs = jnp.concatenate([weights[i, j] for i in range(3)], axis=0)
            out = jnp.dot(lhs, rhs, preferred_element_type=F32)
        prod[j, 0, 0:count] = out[:, :128]
        prod[j, 1, 0:count] = out[:, 128:]


def gathered(prod, start, count):
    parts = [
        prod[0, h, start : start + count]
        + prod[1, h, start + 1 : start + 1 + count]
        + prod[2, h, start + 2 : start + 2 + count]
        for h in range(2)
    ]
    return jnp.concatenate(parts, axis=1)


def pack(field, packs):
    sub = iota((16, CH), 0)
    west = jnp.zeros((16, CH), F32)
    east = jnp.zeros((16, CH), F32)
    for r in range(ROWS):
        here = (sub == 2 * r) | (sub == 2 * r + 1)
        x = field[2 + r, 16:32].astype(F32)
        west = jnp.where(here, x if r == 0 else pltpu.roll(x, 2 * r, 0), west)
        x = field[2 + r, 64:80].astype(F32)
        east = jnp.where(here, x if r == 7 else pltpu.roll(x, (2 * r - 14) % 16, 0), east)
    packs[0] = west.astype(B16)
    packs[1] = east.astype(B16)


def unpack(field, arrived):
    for n, (a, b) in enumerate(CORNERS):
        x = arrived[n].astype(F32)
        for r in {-1: (6, 7), 0: range(8), 1: (0, 1)}[a]:
            row = r + 2 + a * 8
            shift = (14 - 2 * r) % 16 if b < 0 else (-2 * r) % 16
            block = (x if shift == 0 else pltpu.roll(x, shift, 0)).astype(B16)
            if b < 0:
                field[row, 0:16] = block
            else:
                field[row, 80:96] = block


def kernel(
    ids, taps, wts, vals, prec, probe, state, background, conv_in, conv_out,
    grad, innov,
    sx, mx, ax, bg, w1, w2, before, hx, mb, prod, dt, rank_s,
    packs, arrived, sbuf, r1, tbuf, r2, qbuf, q1, qs, q2, zs, zr,
    load_sem, row_sem, pack_sem, s1_sem, s2_sem, z_sem, t1_sem, t2_sem, own_sem,
):
    la = lax.axis_index("lat")
    lo = lax.axis_index("lon")

    def near(a, b):
        return (lax.rem(la + a + LATS, LATS), lax.rem(lo + b + LONS, LONS))

    def send(src, dst, sems, to):
        return pltpu.make_async_remote_copy(
            src_ref=src, dst_ref=dst, send_sem=sems[0], recv_sem=sems[1],
            device_id=to, device_id_type=MESH,
        )

    loads = [
        pltpu.make_async_copy(state, sx.at[2:10, 16:80], load_sem.at[0]),
        pltpu.make_async_copy(conv_in, w1, load_sem.at[1]),
        pltpu.make_async_copy(conv_out, w2, load_sem.at[2]),
        pltpu.make_async_copy(background, bg, load_sem.at[3]),
    ]
    for c in loads:
        c.start()

    partners = [near(k, 0) for k in range(1, LATS)] + [near(0, k) for k in range(1, LONS)]
    partners += [near(a, b) for a in (-1, 1) for b in (-1, 1)]
    barrier = pltpu.get_barrier_semaphore()
    for p in partners:
        pl.semaphore_signal(barrier, inc=1, device_id=p, device_id_type=MESH)

    def halo(field, which):
        copies = [
            send(field.at[2:4, 16:80], field.at[10:12, 16:80],
                 (row_sem.at[which, 0, 0], row_sem.at[which, 0, 1]), near(-1, 0)),
            send(field.at[8:10, 16:80], field.at[0:2, 16:80],
                 (row_sem.at[which, 1, 0], row_sem.at[which, 1, 1]), near(1, 0)),
        ]
        for n, (a, b) in enumerate(CORNERS):
            m = CORNERS.index((-a, -b))
            copies.append(
                send(packs.at[which, 0 if b < 0 else 1], arrived.at[which, m],
                     (pack_sem.at[which, n, 0], pack_sem.at[which, m, 1]), near(a, b))
            )
        return copies

    def clear(field, low, high):
        @pl.when(la == 0)
        def _():
            field[0:low] = jnp.zeros((low,) + field.shape[1:], field.dtype)

        @pl.when(la == LATS - 1)
        def _():
            field[high:] = jnp.zeros((field.shape[0] - high,) + field.shape[1:], field.dtype)

    loads[0].wait()
    pack(sx, packs.at[0])
    pl.semaphore_wait(barrier, len(partners))
    first = halo(sx, 0)
    for c in first:
        c.start()

    upper = jnp.where(iota((128, 128), 0) <= iota((128, 128), 1), 1.0, 0.0).astype(B16)
    carry = jnp.zeros((128, 1), F32)
    ranks = []
    for c in range(16):
        hit = iota((128, 128), 0) == ids[0:1, c * 128 : (c + 1) * 128]
        one = jnp.where(hit, 1.0, 0.0).astype(B16)
        dt[:, c * 128 : (c + 1) * 128] = one
        run = jnp.dot(one, upper, preferred_element_type=F32) + carry
        ranks.append(jnp.sum(jnp.where(hit, run, 0.0), axis=0, keepdims=True) - 1.0)
        carry = run[:, 127:128]
    rank = jnp.concatenate(ranks, axis=1)
    rank_s[...] = rank
    acc = jnp.zeros((128, 512), F32)
    for c in range(8):
        cut = slice(c * 256, (c + 1) * 256)
        own = iota((CAP, 256), 0) == rank[:, cut].astype(I32)
        p = prec[0:1, cut]
        rows = [taps[k : k + 1, cut].astype(F32) - 256.0 for k in range(4)]
        scaled = [wts[k : k + 1, cut] * p for k in range(4)] + [vals[0:1, cut] * p]
        tops = [s.astype(B16).astype(F32) for s in scaled]
        lows = [s - t for s, t in zip(scaled, tops)]
        rows += tops[:4] + lows[:4] + [tops[4], lows[4]]
        spots = [jnp.where(own, r, 0.0).astype(B16) for r in rows]
        spots.append(jnp.zeros((64, 256), B16))
        x = jnp.concatenate(spots, axis=0)
        acc = acc + lax.dot_general(dt[:, cut], x, NT, preferred_element_type=F32)
    sbuf[:, 0:128] = acc[:, 0:128]
    sbuf[:, 128:256] = acc[:, 128:256] + acc[:, 256:384]
    sbuf[:, 256:384] = acc[:, 384:512]
    out1 = []
    for k in range(1, LATS):
        to = lax.rem(la + k, LATS)
        out1.append(
            send(sbuf.at[pl.ds(pl.multiple_of(to * 16, 16), 16)], r1.at[la],
                 (s1_sem.at[k, 0], s1_sem.at[k, 1]), (to, lo))
        )
        out1[-1].start()
    mine = pltpu.make_async_copy(
        sbuf.at[pl.ds(pl.multiple_of(la * 16, 16), 16)], r1.at[la], own_sem.at[0]
    )
    mine.start()

    loads[1].wait()
    for c in first:
        c.wait_recv()
    unpack(sx, arrived.at[0])
    clear(sx, 2, 10)
    products(sx, 10, WIDE, w1, False, prod)
    for r in range(10):
        b = gathered(prod, r * WIDE + 14, PITCH)
        before[r] = b
        hx[r] = (b / (1.0 + jnp.exp(-b))).astype(B16)
    clear(hx, 1, 9)

    mine.wait()
    for c in out1:
        c.wait_recv()
    for t in range(LONS):
        for j in range(LATS):
            tbuf[t, j : j + 1, :] = r1[j, t : t + 1, :]
    out2 = []
    for k in range(1, LONS):
        to = lax.rem(lo + k, LONS)
        out2.append(
            send(tbuf.at[to], r2.at[lo], (s2_sem.at[k, 0], s2_sem.at[k, 1]), (la, to))
        )
        out2[-1].start()
    mine2 = pltpu.make_async_copy(tbuf.at[lo], r2.at[lo], own_sem.at[1])
    mine2.start()

    loads[2].wait()
    loads[3].wait()
    products(hx, 8, PITCH, w2, False, prod)
    pr = probe[...]
    ph, plow = halves(pr)
    sub16 = iota((16, CH), 0)
    readout = jnp.where(
        sub16 == 0, ph.astype(F32), jnp.where(sub16 == 1, plow.astype(F32), 0.0)
    ).astype(B16)
    strips = []
    for r in range(ROWS):
        m = gathered(prod, r * PITCH, COLS) + sx[2 + r, 16:80].astype(F32)
        high, low = halves(m)
        s = lax.dot_general(readout, high, NT, preferred_element_type=F32)
        t = lax.dot_general(readout, low, NT, preferred_element_type=F32)
        strips.append(s[0:1] + s[1:2] + t[0:1])
        d = m - bg[r].astype(F32)
        mb[r] = d
        mx[2 + r, 16:80] = d.astype(B16)
    pack(mx, packs.at[1])
    second = halo(mx, 1)
    for c in second:
        c.start()
    tables = [
        jnp.broadcast_to(jnp.concatenate(strips[2 * q : 2 * q + 2], axis=1), (8, 128))
        for q in range(4)
    ]

    mine2.wait()
    for c in out2:
        c.wait_recv()
    cells, shares = [], []
    for t in range(LONS):
        cell = r2[t, :, 0:128].astype(I32) + 256
        w = r2[t, :, 128:256]
        lane = lax.bitwise_and(cell, 127)
        page = lax.shift_right_logical(cell, 7)
        got = jnp.zeros((8, 128), F32)
        for q in range(4):
            look = jnp.take_along_axis(tables[q], lane, axis=1, mode="promise_in_bounds")
            got = jnp.where(page == q, look, got)
        res = w * got - r2[t, :, 256:384]
        res = res + pltpu.roll(res, 64, 1)
        res = res + pltpu.roll(res, 32, 1)
        qbuf[t] = res
        cells.append(cell)
        shares.append(w * res)
    out3 = []
    for k in range(1, LONS):
        to = lax.rem(lo + k, LONS)
        out3.append(
            send(qbuf.at[to], q1.at[lo], (t1_sem.at[k, 0], t1_sem.at[k, 1]), (la, to))
        )
        out3[-1].start()
    mine3 = pltpu.make_async_copy(qbuf.at[lo], q1.at[lo], own_sem.at[2])
    mine3.start()

    total = jnp.zeros((256, 256), F32)
    for t in range(0, LONS, 2):
        cell = jnp.concatenate(cells[t : t + 2], axis=1)
        share = jnp.concatenate(shares[t : t + 2], axis=1)
        upper_cell = lax.shift_right_logical(cell, 5)
        lower_cell = lax.bitwise_and(cell, 31)
        top = share.astype(B16).astype(F32)
        low = share - top
        tops, lows, marks = [], [], []
        for g in range(8):
            hit = iota((16, 256), 0) == upper_cell[g : g + 1]
            tops.append(jnp.where(hit, top[g : g + 1], 0.0).astype(B16))
            lows.append(jnp.where(hit, low[g : g + 1], 0.0).astype(B16))
            marks.append(
                jnp.where(iota((32, 256), 0) == lower_cell[g : g + 1], 1.0, 0.0).astype(B16)
            )
        lhs = jnp.concatenate(tops + lows, axis=0)
        rhs = jnp.concatenate(marks, axis=0)
        total = total + lax.dot_general(lhs, rhs, NT, preferred_element_type=F32)
    total = total[0:128] + total[128:256]
    total = jnp.where(iota((128, 256), 0) // 16 == iota((128, 256), 1) // 32, total, 0.0)
    fold = total[0:16]
    for g in range(1, 8):
        fold = fold + total[g * 16 : (g + 1) * 16]
    fold = fold[:, 0:128] + fold[:, 128:256]
    fold = fold + pltpu.roll(fold, 64, 1)
    fold = fold + pltpu.roll(fold, 32, 1)
    zs[...] = fold
    out4 = []
    for n, (a, b) in enumerate(SIDES):
        m = SIDES.index((-a, -b))
        out4.append(send(zs, zr.at[m], (z_sem.at[n, 0], z_sem.at[m, 1]), near(a, b)))
        out4[-1].start()

    group = iota((16, 128), 1) // 32
    base = jnp.where(iota((128, CH), 0) // 64 == 0, ph.astype(F32), plow.astype(F32)).astype(B16)
    sub = iota((16, 128), 0)
    spot = lax.bitwise_and(iota((16, 128), 1), 31)
    marks = [spot == sub, spot == sub + 16]

    def parted(z):
        top = z.astype(B16).astype(F32)
        return jnp.where(lax.bitwise_and(group, 1) == 0, top, z - top)

    def outer(blocks):
        lhs = jnp.concatenate(
            [
                jnp.where(marks[c % 2], z[2 * r + c // 2 : 2 * r + c // 2 + 1], 0.0).astype(B16)
                for z, r, c in blocks
            ],
            axis=0,
        )
        return jnp.dot(lhs, base, preferred_element_type=F32)

    center = parted(fold)
    local = outer([(center, r, c) for r in range(ROWS) for c in range(4)])
    for r in range(ROWS):
        ax[2 + r, 16:80] = (mb[r] + local[r * 64 : (r + 1) * 64]).astype(B16)
    for c in second:
        c.wait_recv()
    unpack(mx, arrived.at[1])
    for c in out4:
        c.wait_recv()
    around = {s: parted(zr[n]) for n, s in enumerate(SIDES)}
    for a, rows in ((-1, (6, 7)), (1, (0, 1))):
        piece = outer([(around[a, 0], r, c) for r in rows for c in range(4)])
        for n, r in enumerate(rows):
            row = r + 2 + a * 8
            ax[row, 16:80] = (
                mx[row, 16:80].astype(F32) + piece[n * 64 : (n + 1) * 64]
            ).astype(B16)
    for b, c, at in ((-1, 3, 0), (1, 0, 80)):
        spots = [(a, r) for a, rows in ((-1, (6, 7)), (0, range(8)), (1, (0, 1))) for r in rows]
        piece = outer([(around[a, b], r, c) for a, r in spots])
        for n, (a, r) in enumerate(spots):
            row = r + 2 + a * 8
            ax[row, at : at + 16] = (
                mx[row, at : at + 16].astype(F32) + piece[n * 16 : (n + 1) * 16]
            ).astype(B16)
    clear(ax, 2, 10)

    mine3.wait()
    for c in out3:
        c.wait_recv()
    for j in range(LATS):
        for t in range(LONS):
            qs[j, t : t + 1, :] = q1[t, j : j + 1, :]
    out5 = []
    for k in range(1, LATS):
        to = lax.rem(la + k, LATS)
        out5.append(
            send(qs.at[to], q2.at[la], (t2_sem.at[k, 0], t2_sem.at[k, 1]), (to, lo))
        )
        out5[-1].start()
    mine5 = pltpu.make_async_copy(qs.at[la], q2.at[la], own_sem.at[3])
    mine5.start()

    products(ax, 10, WIDE, w2, True, prod)
    for r in range(10):
        x = before[r]
        sigma = 1.0 / (1.0 + jnp.exp(-x))
        y = gathered(prod, r * WIDE + 14, PITCH) * sigma * (1.0 + x * (1.0 - sigma))
        hx[r] = y.astype(B16)
    clear(hx, 1, 9)
    products(hx, 8, PITCH, w1, True, prod)
    for r in range(ROWS):
        y = gathered(prod, r * PITCH, COLS) + ax[2 + r, 16:80].astype(F32)
        grad[r] = y.astype(B16)

    mine5.wait()
    for c in out5:
        c.wait_recv()
    back = q2[...].reshape(TILES, 128).T[0:CAP]
    one = back.astype(B16)
    rest = back - one.astype(F32)
    two = rest.astype(B16)
    three = (rest - two.astype(F32)).astype(B16)
    lhs = jnp.concatenate([one, two, three], axis=0)
    for c in range(4):
        cut = slice(c * 512, (c + 1) * 512)
        got = jnp.dot(lhs, dt[:, cut], preferred_element_type=F32)
        got = got[0:32] + got[32:64] + got[64:96]
        own = iota((CAP, 512), 0) == rank_s[0:1, cut].astype(I32)
        innov[0:1, cut] = jnp.sum(jnp.where(own, got, 0.0), axis=0, keepdims=True)

    for c in first + out1 + out2 + second + out3 + out4 + out5:
        c.wait_send()


def on_device(
    state, background, conv_in, conv_out, probe,
    tile_ids, cell_taps, tap_weights, obs_values, obs_precision,
):
    vmem = pl.BlockSpec(memory_space=pltpu.VMEM)
    hbm = pl.BlockSpec(memory_space=pl.ANY)
    dma = pltpu.SemaphoreType.DMA
    wide = pltpu.VMEM((12, WIDE, CH), B16)
    kshape = (3, 3, CH, CH)
    grad, innov = pl.pallas_call(
        kernel,
        out_shape=(
            jax.ShapeDtypeStruct((ROWS, COLS, CH), B16),
            jax.ShapeDtypeStruct((1, COUNT), F32),
        ),
        in_specs=[vmem] * 6 + [hbm] * 4,
        out_specs=(vmem, vmem),
        scratch_shapes=[
            wide, wide, wide,
            pltpu.VMEM((ROWS, COLS, CH), B16),
            pltpu.VMEM(kshape, B16),
            pltpu.VMEM(kshape, B16),
            pltpu.VMEM((10, PITCH, CH), F32),
            pltpu.VMEM((10, PITCH, CH), B16),
            pltpu.VMEM((ROWS, COLS, CH), F32),
            pltpu.VMEM((3, 2, 10 * WIDE + 64, 128), F32),
            pltpu.VMEM((TILES, COUNT), B16),
            pltpu.VMEM((1, COUNT), F32),
            pltpu.VMEM((2, 2, 16, CH), B16),
            pltpu.VMEM((2, len(CORNERS), 16, CH), B16),
            pltpu.VMEM((TILES, 384), F32),
            pltpu.VMEM((LATS, LONS, 384), F32),
            pltpu.VMEM((LONS, LATS, 384), F32),
            pltpu.VMEM((LONS, LATS, 384), F32),
            pltpu.VMEM((LONS, LATS, 128), F32),
            pltpu.VMEM((LONS, LATS, 128), F32),
            pltpu.VMEM((LATS, LONS, 128), F32),
            pltpu.VMEM((LATS, LONS, 128), F32),
            pltpu.VMEM((16, 128), F32),
            pltpu.VMEM((len(SIDES), 16, 128), F32),
            dma((4,)),
            dma((2, 2, 2)),
            dma((2, len(CORNERS), 2)),
            dma((LATS, 2)),
            dma((LONS, 2)),
            dma((len(SIDES), 2)),
            dma((LONS, 2)),
            dma((LATS, 2)),
            dma((4,)),
        ],
        compiler_params=pltpu.CompilerParams(
            collective_id=0, has_side_effects=True, vmem_limit_bytes=56 * 2**20
        ),
    )(
        tile_ids.reshape(1, COUNT),
        cell_taps,
        tap_weights,
        obs_values.reshape(1, COUNT),
        obs_precision.reshape(1, COUNT),
        probe.reshape(1, CH),
        state,
        background,
        conv_in,
        conv_out,
    )
    return grad, innov.reshape(COUNT)


def solution(mesh):
    in_specs = (
        P("lat", "lon", None),
        P("lat", "lon", None),
        P(),
        P(),
        P(),
        P(("lat", "lon"), None),
        P(None, ("lat", "lon")),
        P(None, ("lat", "lon")),
        P(("lat", "lon")),
        P(("lat", "lon")),
    )
    out_specs = (P("lat", "lon", None), P(("lat", "lon")))
    return jax.shard_map(
        on_device, mesh=mesh, in_specs=in_specs, out_specs=out_specs, check_vma=False
    )
```

```python
import functools

import jax
import jax.numpy as jnp
from jax import lax
from jax.experimental import pallas as pl
from jax.experimental.pallas import tpu as pltpu
from jax.sharding import PartitionSpec as P

MESH = pl.DeviceIdType.MESH
B16 = jnp.bfloat16
F32 = jnp.float32
I32 = jnp.int32
ROWS, COLS, CH = 8, 64, 256
WIDE = 96
PITCH = 80
LATS, LONS = 8, 16
TILES = LATS * LONS
COUNT = 2048
CAP = 32
NT = (((1,), (1,)), ((), ()))
SIDES = [(a, b) for a in (-1, 0, 1) for b in (-1, 0, 1) if (a, b) != (0, 0)]
CORNERS = [s for s in SIDES if s[1] != 0]


def iota(shape, dim):
    return lax.broadcasted_iota(I32, shape, dim)


def halves(x):
    high = x.astype(B16)
    return high, (x - high.astype(F32)).astype(B16)


def products(field, rows, pitch, weights, flipped, prod):
    count = rows * pitch
    lhs = jnp.concatenate(
        [field[i : i + rows].reshape(count, CH) for i in range(3)], axis=1
    )
    for j in range(3):
        if flipped:
            rhs = jnp.concatenate([weights[2 - i, 2 - j] for i in range(3)], axis=1)
            out = lax.dot_general(lhs, rhs, NT, preferred_element_type=F32)
        else:
            rhs = jnp.concatenate([weights[i, j] for i in range(3)], axis=0)
            out = jnp.dot(lhs, rhs, preferred_element_type=F32)
        prod[j, 0, 0:count] = out[:, :128]
        prod[j, 1, 0:count] = out[:, 128:]


def gathered(prod, start, count):
    parts = [
        prod[0, h, start : start + count]
        + prod[1, h, start + 1 : start + 1 + count]
        + prod[2, h, start + 2 : start + 2 + count]
        for h in range(2)
    ]
    return jnp.concatenate(parts, axis=1)


def pack(field, packs):
    sub = iota((16, CH), 0)
    west = jnp.zeros((16, CH), F32)
    east = jnp.zeros((16, CH), F32)
    for r in range(ROWS):
        here = (sub == 2 * r) | (sub == 2 * r + 1)
        x = field[2 + r, 16:32].astype(F32)
        west = jnp.where(here, x if r == 0 else pltpu.roll(x, 2 * r, 0), west)
        x = field[2 + r, 64:80].astype(F32)
        east = jnp.where(here, x if r == 7 else pltpu.roll(x, (2 * r - 14) % 16, 0), east)
    packs[0] = west.astype(B16)
    packs[1] = east.astype(B16)


def unpack(field, arrived):
    for n, (a, b) in enumerate(CORNERS):
        x = arrived[n].astype(F32)
        for r in {-1: (6, 7), 0: range(8), 1: (0, 1)}[a]:
            row = r + 2 + a * 8
            shift = (14 - 2 * r) % 16 if b < 0 else (-2 * r) % 16
            block = (x if shift == 0 else pltpu.roll(x, shift, 0)).astype(B16)
            if b < 0:
                field[row, 0:16] = block
            else:
                field[row, 80:96] = block


def kernel(
    ids_in, taps_in, wts_in, vals_in, prec_in, probe_in, state, background, conv_in, conv_out,
    grad, innov,
    ids, taps, wts, vals, prec, probe, sx, mx, ax, bg, w1, w2, before, hx, mb, prod, dt, rank_s,
    packs, arrived, sbuf, r2, qbuf, q2, zs, zr,
    load_sem, row_sem, pack_sem, out_sem, back_sem, z_sem, own_sem,
):
    la = lax.axis_index("lat")
    lo = lax.axis_index("lon")

    def near(a, b):
        return (lax.rem(la + a + LATS, LATS), lax.rem(lo + b + LONS, LONS))

    def send(src, dst, sems, to):
        return pltpu.make_async_remote_copy(
            src_ref=src, dst_ref=dst, send_sem=sems[0], recv_sem=sems[1],
            device_id=to, device_id_type=MESH,
        )

    me = la * LONS + lo
    barrier = pltpu.get_barrier_semaphore()

    def place(k):
        t = lax.rem(me + k, TILES)
        return t, (t // LONS, lax.rem(t, LONS))

    def greet(k, c):
        pl.semaphore_signal(barrier, inc=1, device_id=place(k)[1], device_id_type=MESH)
        return c

    lax.fori_loop(1, TILES, greet, 0)
    ins = [(ids_in, ids), (taps_in, taps), (wts_in, wts), (vals_in, vals), (prec_in, prec)]
    ins += [(state, sx.at[2:10, 16:80]), (conv_in, w1), (conv_out, w2), (background, bg)]
    ins += [(probe_in, probe)]
    loads = [pltpu.make_async_copy(a, b, load_sem.at[n]) for n, (a, b) in enumerate(ins)]
    for c in loads:
        c.start()

    def scatter(src, dst, sems):
        def one(k, c):
            t, to = place(k)
            send(src.at[t], dst.at[me], (sems.at[0], sems.at[1]), to).start()
            return c

        lax.fori_loop(1, TILES, one, 0)
        own = pltpu.make_async_copy(src.at[me], dst.at[me], own_sem.at[0])
        own.start()
        own.wait()

    def settle(src, dst, sem):
        some = slice(0, TILES - 1)
        pltpu.make_async_copy(src.at[some], dst.at[some], sem).wait()

    def halo(field, which):
        copies = [
            send(field.at[2:4, 16:80], field.at[10:12, 16:80],
                 (row_sem.at[which, 0, 0], row_sem.at[which, 0, 1]), near(-1, 0)),
            send(field.at[8:10, 16:80], field.at[0:2, 16:80],
                 (row_sem.at[which, 1, 0], row_sem.at[which, 1, 1]), near(1, 0)),
        ]
        for n, (a, b) in enumerate(CORNERS):
            m = CORNERS.index((-a, -b))
            copies.append(
                send(packs.at[which, 0 if b < 0 else 1], arrived.at[which, m],
                     (pack_sem.at[which, n, 0], pack_sem.at[which, m, 1]), near(a, b))
            )
        return copies

    def clear(field, low, high):
        @pl.when(la == 0)
        def _():
            field[0:low] = jnp.zeros((low,) + field.shape[1:], field.dtype)

        @pl.when(la == LATS - 1)
        def _():
            field[high:] = jnp.zeros((field.shape[0] - high,) + field.shape[1:], field.dtype)

    for c in loads[:5]:
        c.wait()
    upper = jnp.where(iota((128, 128), 0) <= iota((128, 128), 1), 1.0, 0.0).astype(B16)
    carry = jnp.zeros((128, 1), F32)
    ranks = []
    for c in range(16):
        hit = iota((128, 128), 0) == ids[0:1, c * 128 : (c + 1) * 128]
        one = jnp.where(hit, 1.0, 0.0).astype(B16)
        dt[:, c * 128 : (c + 1) * 128] = one
        run = jnp.dot(one, upper, preferred_element_type=F32) + carry
        ranks.append(jnp.sum(jnp.where(hit, run, 0.0), axis=0, keepdims=True) - 1.0)
        carry = run[:, 127:128]
    rank = jnp.concatenate(ranks, axis=1)
    rank_s[...] = rank
    acc = jnp.zeros((128, 512), F32)
    for c in range(8):
        cut = slice(c * 256, (c + 1) * 256)
        own = iota((CAP, 256), 0) == rank[:, cut].astype(I32)
        p = prec[0:1, cut]
        rows = [taps[k : k + 1, cut].astype(F32) - 256.0 for k in range(4)]
        scaled = [wts[k : k + 1, cut] * p for k in range(4)] + [vals[0:1, cut] * p]
        tops = [s.astype(B16).astype(F32) for s in scaled]
        lows = [s - t for s, t in zip(scaled, tops)]
        rows += tops[:4] + lows[:4] + [tops[4], lows[4]]
        spots = [jnp.where(own, r, 0.0).astype(B16) for r in rows]
        spots.append(jnp.zeros((64, 256), B16))
        x = jnp.concatenate(spots, axis=0)
        acc = acc + lax.dot_general(dt[:, cut], x, NT, preferred_element_type=F32)
    sbuf[:, 0, 0:128] = acc[:, 0:128]
    sbuf[:, 0, 128:256] = acc[:, 128:256] + acc[:, 256:384]
    sbuf[:, 0, 256:384] = acc[:, 384:512]

    loads[5].wait()
    pack(sx, packs.at[0])
    pl.semaphore_wait(barrier, TILES - 1)
    first = halo(sx, 0)
    for c in first:
        c.start()
    scatter(sbuf, r2, out_sem)

    loads[6].wait()
    for c in first:
        c.wait_recv()
    unpack(sx, arrived.at[0])
    clear(sx, 2, 10)
    products(sx, 10, WIDE, w1, False, prod)
    for r in range(10):
        b = gathered(prod, r * WIDE + 14, PITCH)
        before[r] = b
        hx[r] = (b / (1.0 + jnp.exp(-b))).astype(B16)
    clear(hx, 1, 9)

    for c in loads[7:]:
        c.wait()
    products(hx, 8, PITCH, w2, False, prod)
    pr = probe[...]
    ph, plow = halves(pr)
    sub16 = iota((16, CH), 0)
    readout = jnp.where(
        sub16 == 0, ph.astype(F32), jnp.where(sub16 == 1, plow.astype(F32), 0.0)
    ).astype(B16)
    strips = []
    for r in range(ROWS):
        m = gathered(prod, r * PITCH, COLS) + sx[2 + r, 16:80].astype(F32)
        high, low = halves(m)
        s = lax.dot_general(readout, high, NT, preferred_element_type=F32)
        t = lax.dot_general(readout, low, NT, preferred_element_type=F32)
        strips.append(s[0:1] + s[1:2] + t[0:1])
        d = m - bg[r].astype(F32)
        mb[r] = d
        mx[2 + r, 16:80] = d.astype(B16)
    pack(mx, packs.at[1])
    second = halo(mx, 1)
    for c in second:
        c.start()
    tables = [
        jnp.broadcast_to(jnp.concatenate(strips[2 * q : 2 * q + 2], axis=1), (8, 128))
        for q in range(4)
    ]

    settle(sbuf, r2, out_sem.at[1])
    cells, shares = [], []
    for t in range(TILES // 8):
        own = slice(8 * t, 8 * t + 8)
        cell = r2[own, 0, 0:128].astype(I32) + 256
        w = r2[own, 0, 128:256]
        lane = lax.bitwise_and(cell, 127)
        page = lax.shift_right_logical(cell, 7)
        got = jnp.zeros((8, 128), F32)
        for q in range(4):
            look = jnp.take_along_axis(tables[q], lane, axis=1, mode="promise_in_bounds")
            got = jnp.where(page == q, look, got)
        res = w * got - r2[own, 0, 256:384]
        res = res + pltpu.roll(res, 64, 1)
        res = res + pltpu.roll(res, 32, 1)
        qbuf[own, 0, :] = res
        cells.append(cell)
        shares.append(w * res)

    total = jnp.zeros((256, 256), F32)
    for t in range(0, TILES // 8, 2):
        cell = jnp.concatenate(cells[t : t + 2], axis=1)
        share = jnp.concatenate(shares[t : t + 2], axis=1)
        upper_cell = lax.shift_right_logical(cell, 5)
        lower_cell = lax.bitwise_and(cell, 31)
        top = share.astype(B16).astype(F32)
        low = share - top
        tops, lows, marks = [], [], []
        for g in range(8):
            hit = iota((16, 256), 0) == upper_cell[g : g + 1]
            tops.append(jnp.where(hit, top[g : g + 1], 0.0).astype(B16))
            lows.append(jnp.where(hit, low[g : g + 1], 0.0).astype(B16))
            marks.append(
                jnp.where(iota((32, 256), 0) == lower_cell[g : g + 1], 1.0, 0.0).astype(B16)
            )
        lhs = jnp.concatenate(tops + lows, axis=0)
        rhs = jnp.concatenate(marks, axis=0)
        total = total + lax.dot_general(lhs, rhs, NT, preferred_element_type=F32)
    total = total[0:128] + total[128:256]
    total = jnp.where(iota((128, 256), 0) // 16 == iota((128, 256), 1) // 32, total, 0.0)
    fold = total[0:16]
    for g in range(1, 8):
        fold = fold + total[g * 16 : (g + 1) * 16]
    fold = fold[:, 0:128] + fold[:, 128:256]
    fold = fold + pltpu.roll(fold, 64, 1)
    fold = fold + pltpu.roll(fold, 32, 1)
    zs[...] = fold
    out4 = []
    for n, (a, b) in enumerate(SIDES):
        m = SIDES.index((-a, -b))
        out4.append(send(zs, zr.at[m], (z_sem.at[n, 0], z_sem.at[m, 1]), near(a, b)))
        out4[-1].start()

    scatter(qbuf, q2, back_sem)

    group = iota((16, 128), 1) // 32
    base = jnp.where(iota((128, CH), 0) // 64 == 0, ph.astype(F32), plow.astype(F32)).astype(B16)
    sub = iota((16, 128), 0)
    spot = lax.bitwise_and(iota((16, 128), 1), 31)
    marks = [spot == sub, spot == sub + 16]

    def parted(z):
        top = z.astype(B16).astype(F32)
        return jnp.where(lax.bitwise_and(group, 1) == 0, top, z - top)

    def outer(blocks):
        lhs = jnp.concatenate(
            [
                jnp.where(marks[c % 2], z[2 * r + c // 2 : 2 * r + c // 2 + 1], 0.0).astype(B16)
                for z, r, c in blocks
            ],
            axis=0,
        )
        return jnp.dot(lhs, base, preferred_element_type=F32)

    center = parted(fold)
    local = outer([(center, r, c) for r in range(ROWS) for c in range(4)])
    for r in range(ROWS):
        ax[2 + r, 16:80] = (mb[r] + local[r * 64 : (r + 1) * 64]).astype(B16)
    for c in second:
        c.wait_recv()
    unpack(mx, arrived.at[1])
    for c in out4:
        c.wait_recv()
    around = {s: parted(zr[n]) for n, s in enumerate(SIDES)}
    for a, rows in ((-1, (6, 7)), (1, (0, 1))):
        piece = outer([(around[a, 0], r, c) for r in rows for c in range(4)])
        for n, r in enumerate(rows):
            row = r + 2 + a * 8
            ax[row, 16:80] = (
                mx[row, 16:80].astype(F32) + piece[n * 64 : (n + 1) * 64]
            ).astype(B16)
    for b, c, at in ((-1, 3, 0), (1, 0, 80)):
        spots = [(a, r) for a, rows in ((-1, (6, 7)), (0, range(8)), (1, (0, 1))) for r in rows]
        piece = outer([(around[a, b], r, c) for a, r in spots])
        for n, (a, r) in enumerate(spots):
            row = r + 2 + a * 8
            ax[row, at : at + 16] = (
                mx[row, at : at + 16].astype(F32) + piece[n * 16 : (n + 1) * 16]
            ).astype(B16)
    clear(ax, 2, 10)

    products(ax, 10, WIDE, w2, True, prod)
    for r in range(10):
        x = before[r]
        sigma = 1.0 / (1.0 + jnp.exp(-x))
        y = gathered(prod, r * WIDE + 14, PITCH) * sigma * (1.0 + x * (1.0 - sigma))
        hx[r] = y.astype(B16)
    clear(hx, 1, 9)
    products(hx, 8, PITCH, w1, True, prod)
    for r in range(ROWS):
        y = gathered(prod, r * PITCH, COLS) + ax[2 + r, 16:80].astype(F32)
        grad[r] = y.astype(B16)

    settle(qbuf, q2, back_sem.at[1])
    back = q2[:, 0, :].T[0:CAP]
    one = back.astype(B16)
    rest = back - one.astype(F32)
    two = rest.astype(B16)
    three = (rest - two.astype(F32)).astype(B16)
    lhs = jnp.concatenate([one, two, three], axis=0)
    for c in range(4):
        cut = slice(c * 512, (c + 1) * 512)
        got = jnp.dot(lhs, dt[:, cut], preferred_element_type=F32)
        got = got[0:32] + got[32:64] + got[64:96]
        own = iota((CAP, 512), 0) == rank_s[0:1, cut].astype(I32)
        innov[0:1, cut] = jnp.sum(jnp.where(own, got, 0.0), axis=0, keepdims=True)

    for c in first + second + out4:
        c.wait_send()
    settle(sbuf, r2, out_sem.at[0])
    settle(qbuf, q2, back_sem.at[0])


def on_device(
    state, background, conv_in, conv_out, probe,
    tile_ids, cell_taps, tap_weights, obs_values, obs_precision,
):
    vmem = pl.BlockSpec(memory_space=pltpu.VMEM)
    hbm = pl.BlockSpec(memory_space=pl.ANY)
    dma = pltpu.SemaphoreType.DMA
    wide = pltpu.VMEM((12, WIDE, CH), B16)
    kshape = (3, 3, CH, CH)
    grad, innov = pl.pallas_call(
        kernel,
        out_shape=(
            jax.ShapeDtypeStruct((ROWS, COLS, CH), B16),
            jax.ShapeDtypeStruct((1, COUNT), F32),
        ),
        in_specs=[hbm] * 10,
        out_specs=(vmem, vmem),
        scratch_shapes=[
            pltpu.VMEM((1, COUNT), I32),
            pltpu.VMEM((4, COUNT), I32),
            pltpu.VMEM((4, COUNT), F32),
            pltpu.VMEM((1, COUNT), F32),
            pltpu.VMEM((1, COUNT), F32),
            pltpu.VMEM((1, CH), F32),
            wide, wide, wide,
            pltpu.VMEM((ROWS, COLS, CH), B16),
            pltpu.VMEM(kshape, B16),
            pltpu.VMEM(kshape, B16),
            pltpu.VMEM((10, PITCH, CH), F32),
            pltpu.VMEM((10, PITCH, CH), B16),
            pltpu.VMEM((ROWS, COLS, CH), F32),
            pltpu.VMEM((3, 2, 10 * WIDE + 64, 128), F32),
            pltpu.VMEM((TILES, COUNT), B16),
            pltpu.VMEM((1, COUNT), F32),
            pltpu.VMEM((2, 2, 16, CH), B16),
            pltpu.VMEM((2, len(CORNERS), 16, CH), B16),
            pltpu.VMEM((TILES, 1, 384), F32),
            pltpu.VMEM((TILES, 1, 384), F32),
            pltpu.VMEM((TILES, 1, 128), F32),
            pltpu.VMEM((TILES, 1, 128), F32),
            pltpu.VMEM((16, 128), F32),
            pltpu.VMEM((len(SIDES), 16, 128), F32),
            dma((10,)),
            dma((2, 2, 2)),
            dma((2, len(CORNERS), 2)),
            dma((2,)),
            dma((2,)),
            dma((len(SIDES), 2)),
            dma((1,)),
        ],
        compiler_params=pltpu.CompilerParams(
            collective_id=0, has_side_effects=True, vmem_limit_bytes=56 * 2**20
        ),
    )(
        tile_ids.reshape(1, COUNT),
        cell_taps,
        tap_weights,
        obs_values.reshape(1, COUNT),
        obs_precision.reshape(1, COUNT),
        probe.reshape(1, CH),
        state,
        background,
        conv_in,
        conv_out,
    )
    return grad, innov.reshape(COUNT)


def solution(mesh):
    in_specs = (
        P("lat", "lon", None),
        P("lat", "lon", None),
        P(),
        P(),
        P(),
        P(("lat", "lon"), None),
        P(None, ("lat", "lon")),
        P(None, ("lat", "lon")),
        P(("lat", "lon")),
        P(("lat", "lon")),
    )
    out_specs = (P("lat", "lon", None), P(("lat", "lon")))
    return jax.shard_map(
        on_device, mesh=mesh, in_specs=in_specs, out_specs=out_specs, check_vma=False
    )
```

```python
import functools

import jax
import jax.numpy as jnp
from jax import lax
from jax.experimental import pallas as pl
from jax.experimental.pallas import tpu as pltpu
from jax.sharding import PartitionSpec as P

MESH = pl.DeviceIdType.MESH
B16 = jnp.bfloat16
F32 = jnp.float32
I32 = jnp.int32
ROWS, COLS, CH = 8, 64, 256
WIDE = 96
PITCH = 80
LATS, LONS = 8, 16
TILES = LATS * LONS
COUNT = 2048
CAP = 32
NT = (((1,), (1,)), ((), ()))
SIDES = [(a, b) for a in (-1, 0, 1) for b in (-1, 0, 1) if (a, b) != (0, 0)]
CORNERS = [s for s in SIDES if s[1] != 0]


def hops(a, b):
    y, x, z = a // 2, b // 4, b % 4
    return min(y, 4 - y) + min(x, 4 - x) + min(z, 4 - z)


OTHERS = [(a, b) for a in range(LATS) for b in range(LONS) if (a, b) != (0, 0)]
OTHERS.sort(key=lambda o: -hops(*o))


def iota(shape, dim):
    return lax.broadcasted_iota(I32, shape, dim)


def halves(x):
    high = x.astype(B16)
    return high, (x - high.astype(F32)).astype(B16)


def products(field, rows, pitch, weights, flipped, prod):
    count = rows * pitch
    lhs = jnp.concatenate(
        [field[i : i + rows].reshape(count, CH) for i in range(3)], axis=1
    )
    for j in range(3):
        if flipped:
            rhs = jnp.concatenate([weights[2 - i, 2 - j] for i in range(3)], axis=1)
            out = lax.dot_general(lhs, rhs, NT, preferred_element_type=F32)
        else:
            rhs = jnp.concatenate([weights[i, j] for i in range(3)], axis=0)
            out = jnp.dot(lhs, rhs, preferred_element_type=F32)
        prod[j, 0, 0:count] = out[:, :128]
        prod[j, 1, 0:count] = out[:, 128:]


def gathered(prod, start, count):
    parts = [
        prod[0, h, start : start + count]
        + prod[1, h, start + 1 : start + 1 + count]
        + prod[2, h, start + 2 : start + 2 + count]
        for h in range(2)
    ]
    return jnp.concatenate(parts, axis=1)


def pack(field, packs):
    sub = iota((16, CH), 0)
    west = jnp.zeros((16, CH), F32)
    east = jnp.zeros((16, CH), F32)
    for r in range(ROWS):
        here = (sub == 2 * r) | (sub == 2 * r + 1)
        x = field[2 + r, 16:32].astype(F32)
        west = jnp.where(here, x if r == 0 else pltpu.roll(x, 2 * r, 0), west)
        x = field[2 + r, 64:80].astype(F32)
        east = jnp.where(here, x if r == 7 else pltpu.roll(x, (2 * r - 14) % 16, 0), east)
    packs[0] = west.astype(B16)
    packs[1] = east.astype(B16)


def unpack(field, arrived):
    for n, (a, b) in enumerate(CORNERS):
        x = arrived[n].astype(F32)
        for r in {-1: (6, 7), 0: range(8), 1: (0, 1)}[a]:
            row = r + 2 + a * 8
            shift = (14 - 2 * r) % 16 if b < 0 else (-2 * r) % 16
            block = (x if shift == 0 else pltpu.roll(x, shift, 0)).astype(B16)
            if b < 0:
                field[row, 0:16] = block
            else:
                field[row, 80:96] = block


def kernel(
    ids_in, taps_in, wts_in, vals_in, prec_in, probe_in, state, background, conv_in, conv_out,
    grad, innov,
    ids, taps, wts, vals, prec, probe, sx, mx, ax, bg, w1, w2, before, hx, mb, prod, dt, rank_s,
    packs, arrived, sbuf, r2, qbuf, q2, zs, zr,
    load_sem, row_sem, pack_sem, out_sem, back_sem, z_sem, own_sem,
):
    la = lax.axis_index("lat")
    lo = lax.axis_index("lon")

    def near(a, b):
        return place(a, b)[1]

    def send(src, dst, sems, to):
        return pltpu.make_async_remote_copy(
            src_ref=src, dst_ref=dst, send_sem=sems[0], recv_sem=sems[1],
            device_id=to, device_id_type=MESH,
        )

    me = la * LONS + lo
    barrier = pltpu.get_barrier_semaphore()

    def place(a, b):
        to = (lax.bitwise_and(la + a, LATS - 1), lax.bitwise_and(lo + b, LONS - 1))
        return to[0] * LONS + to[1], to

    ins = [(ids_in, ids), (prec_in, prec), (taps_in, taps), (wts_in, wts), (vals_in, vals)]
    ins += [(state, sx.at[2:10, 16:80]), (conv_in, w1), (conv_out, w2), (background, bg)]
    ins += [(probe_in, probe)]
    loads = [pltpu.make_async_copy(a, b, load_sem.at[n]) for n, (a, b) in enumerate(ins)]
    for c in loads:
        c.start()
    for a, b in OTHERS:
        pl.semaphore_signal(barrier, inc=1, device_id=place(a, b)[1], device_id_type=MESH)

    def scatter(src, dst, sems):
        for a, b in OTHERS:
            t, to = place(a, b)
            send(src.at[t], dst.at[me], (sems.at[0], sems.at[1]), to).start()
        own = pltpu.make_async_copy(src.at[me], dst.at[me], own_sem.at[0])
        own.start()
        own.wait()

    def settle(src, dst, sems, which):
        some = slice(0, TILES - 1)
        pltpu.make_async_copy(src.at[some], dst.at[some], sems.at[which]).wait()

    def halo(field, which):
        copies = [
            send(field.at[2:4, 16:80], field.at[10:12, 16:80],
                 (row_sem.at[which, 0, 0], row_sem.at[which, 0, 1]), near(-1, 0)),
            send(field.at[8:10, 16:80], field.at[0:2, 16:80],
                 (row_sem.at[which, 1, 0], row_sem.at[which, 1, 1]), near(1, 0)),
        ]
        for n, (a, b) in enumerate(CORNERS):
            m = CORNERS.index((-a, -b))
            copies.append(
                send(packs.at[which, 0 if b < 0 else 1], arrived.at[which, m],
                     (pack_sem.at[which, n, 0], pack_sem.at[which, m, 1]), near(a, b))
            )
        return copies

    def clear(field, low, high):
        @pl.when(la == 0)
        def _():
            field[0:low] = jnp.zeros((low,) + field.shape[1:], field.dtype)

        @pl.when(la == LATS - 1)
        def _():
            field[high:] = jnp.zeros((field.shape[0] - high,) + field.shape[1:], field.dtype)

    for c in loads[:5]:
        c.wait()
    upper = jnp.where(iota((128, 128), 0) <= iota((128, 128), 1), 1.0, 0.0).astype(B16)
    carry = jnp.zeros((128, 1), F32)
    ranks = []
    for c in range(16):
        hit = iota((128, 128), 0) == ids[0:1, c * 128 : (c + 1) * 128]
        one = jnp.where(hit, 1.0, 0.0).astype(B16)
        dt[:, c * 128 : (c + 1) * 128] = one
        run = jnp.dot(one, upper, preferred_element_type=F32) + carry
        ranks.append(jnp.sum(jnp.where(hit, run, 0.0), axis=0, keepdims=True) - 1.0)
        carry = run[:, 127:128]
    rank = jnp.concatenate(ranks, axis=1)
    rank_s[...] = rank
    acc = jnp.zeros((128, 512), F32)
    for c in range(8):
        cut = slice(c * 256, (c + 1) * 256)
        own = iota((CAP, 256), 0) == rank[:, cut].astype(I32)
        p = prec[0:1, cut]
        rows = [taps[k : k + 1, cut].astype(F32) - 256.0 for k in range(4)]
        scaled = [wts[k : k + 1, cut] * p for k in range(4)] + [vals[0:1, cut] * p]
        tops = [s.astype(B16).astype(F32) for s in scaled]
        lows = [s - t for s, t in zip(scaled, tops)]
        rows += tops[:4] + lows[:4] + [tops[4], lows[4]]
        spots = [jnp.where(own, r, 0.0).astype(B16) for r in rows]
        spots.append(jnp.zeros((64, 256), B16))
        x = jnp.concatenate(spots, axis=0)
        acc = acc + lax.dot_general(dt[:, cut], x, NT, preferred_element_type=F32)
    sbuf[:, 0, 0:128] = acc[:, 0:128]
    sbuf[:, 0, 128:256] = acc[:, 128:256] + acc[:, 256:384]
    sbuf[:, 0, 256:384] = acc[:, 384:512]

    loads[5].wait()
    pack(sx, packs.at[0])
    pl.semaphore_wait(barrier, TILES - 1)
    first = halo(sx, 0)
    for c in first:
        c.start()
    scatter(sbuf, r2, out_sem)

    loads[6].wait()
    for c in first:
        c.wait_recv()
    unpack(sx, arrived.at[0])
    clear(sx, 2, 10)
    products(sx, 10, WIDE, w1, False, prod)
    for r in range(10):
        b = gathered(prod, r * WIDE + 14, PITCH)
        before[r] = b
        hx[r] = (b / (1.0 + jnp.exp(-b))).astype(B16)
    clear(hx, 1, 9)

    for c in loads[7:]:
        c.wait()
    products(hx, 8, PITCH, w2, False, prod)
    pr = probe[...]
    ph, plow = halves(pr)
    sub16 = iota((16, CH), 0)
    readout = jnp.where(
        sub16 == 0, ph.astype(F32), jnp.where(sub16 == 1, plow.astype(F32), 0.0)
    ).astype(B16)
    strips = []
    for r in range(ROWS):
        m = gathered(prod, r * PITCH, COLS) + sx[2 + r, 16:80].astype(F32)
        high, low = halves(m)
        s = lax.dot_general(readout, high, NT, preferred_element_type=F32)
        t = lax.dot_general(readout, low, NT, preferred_element_type=F32)
        strips.append(s[0:1] + s[1:2] + t[0:1])
        d = m - bg[r].astype(F32)
        mb[r] = d
        mx[2 + r, 16:80] = d.astype(B16)
    pack(mx, packs.at[1])
    second = halo(mx, 1)
    for c in second:
        c.start()
    tables = [
        jnp.broadcast_to(jnp.concatenate(strips[2 * q : 2 * q + 2], axis=1), (8, 128))
        for q in range(4)
    ]

    settle(sbuf, r2, out_sem, 1)
    cells, shares = [], []
    for t in range(TILES // 8):
        own = slice(8 * t, 8 * t + 8)
        cell = r2[own, 0, 0:128].astype(I32) + 256
        w = r2[own, 0, 128:256]
        lane = lax.bitwise_and(cell, 127)
        page = lax.shift_right_logical(cell, 7)
        got = jnp.zeros((8, 128), F32)
        for q in range(4):
            look = jnp.take_along_axis(tables[q], lane, axis=1, mode="promise_in_bounds")
            got = jnp.where(page == q, look, got)
        res = w * got - r2[own, 0, 256:384]
        res = res + pltpu.roll(res, 64, 1)
        res = res + pltpu.roll(res, 32, 1)
        qbuf[own, 0, :] = res
        cells.append(cell)
        shares.append(w * res)

    total = jnp.zeros((256, 256), F32)
    for t in range(0, TILES // 8, 2):
        cell = jnp.concatenate(cells[t : t + 2], axis=1)
        share = jnp.concatenate(shares[t : t + 2], axis=1)
        upper_cell = lax.shift_right_logical(cell, 5)
        lower_cell = lax.bitwise_and(cell, 31)
        top = share.astype(B16).astype(F32)
        low = share - top
        tops, lows, marks = [], [], []
        for g in range(8):
            hit = iota((16, 256), 0) == upper_cell[g : g + 1]
            tops.append(jnp.where(hit, top[g : g + 1], 0.0).astype(B16))
            lows.append(jnp.where(hit, low[g : g + 1], 0.0).astype(B16))
            marks.append(
                jnp.where(iota((32, 256), 0) == lower_cell[g : g + 1], 1.0, 0.0).astype(B16)
            )
        lhs = jnp.concatenate(tops + lows, axis=0)
        rhs = jnp.concatenate(marks, axis=0)
        total = total + lax.dot_general(lhs, rhs, NT, preferred_element_type=F32)
    total = total[0:128] + total[128:256]
    total = jnp.where(iota((128, 256), 0) // 16 == iota((128, 256), 1) // 32, total, 0.0)
    fold = total[0:16]
    for g in range(1, 8):
        fold = fold + total[g * 16 : (g + 1) * 16]
    fold = fold[:, 0:128] + fold[:, 128:256]
    fold = fold + pltpu.roll(fold, 64, 1)
    fold = fold + pltpu.roll(fold, 32, 1)
    zs[...] = fold
    out4 = []
    for n, (a, b) in enumerate(SIDES):
        m = SIDES.index((-a, -b))
        out4.append(send(zs, zr.at[m], (z_sem.at[n, 0], z_sem.at[m, 1]), near(a, b)))
        out4[-1].start()

    scatter(qbuf, q2, back_sem)

    group = iota((16, 128), 1) // 32
    base = jnp.where(iota((128, CH), 0) // 64 == 0, ph.astype(F32), plow.astype(F32)).astype(B16)
    sub = iota((16, 128), 0)
    spot = lax.bitwise_and(iota((16, 128), 1), 31)
    marks = [spot == sub, spot == sub + 16]

    def parted(z):
        top = z.astype(B16).astype(F32)
        return jnp.where(lax.bitwise_and(group, 1) == 0, top, z - top)

    def outer(blocks):
        lhs = jnp.concatenate(
            [
                jnp.where(marks[c % 2], z[2 * r + c // 2 : 2 * r + c // 2 + 1], 0.0).astype(B16)
                for z, r, c in blocks
            ],
            axis=0,
        )
        return jnp.dot(lhs, base, preferred_element_type=F32)

    center = parted(fold)
    local = outer([(center, r, c) for r in range(ROWS) for c in range(4)])
    for r in range(ROWS):
        ax[2 + r, 16:80] = (mb[r] + local[r * 64 : (r + 1) * 64]).astype(B16)
    for c in second:
        c.wait_recv()
    unpack(mx, arrived.at[1])
    for c in out4:
        c.wait_recv()
    around = {s: parted(zr[n]) for n, s in enumerate(SIDES)}
    for a, rows in ((-1, (6, 7)), (1, (0, 1))):
        piece = outer([(around[a, 0], r, c) for r in rows for c in range(4)])
        for n, r in enumerate(rows):
            row = r + 2 + a * 8
            ax[row, 16:80] = (
                mx[row, 16:80].astype(F32) + piece[n * 64 : (n + 1) * 64]
            ).astype(B16)
    for b, c, at in ((-1, 3, 0), (1, 0, 80)):
        spots = [(a, r) for a, rows in ((-1, (6, 7)), (0, range(8)), (1, (0, 1))) for r in rows]
        piece = outer([(around[a, b], r, c) for a, r in spots])
        for n, (a, r) in enumerate(spots):
            row = r + 2 + a * 8
            ax[row, at : at + 16] = (
                mx[row, at : at + 16].astype(F32) + piece[n * 16 : (n + 1) * 16]
            ).astype(B16)
    clear(ax, 2, 10)

    products(ax, 10, WIDE, w2, True, prod)
    for r in range(10):
        x = before[r]
        sigma = 1.0 / (1.0 + jnp.exp(-x))
        y = gathered(prod, r * WIDE + 14, PITCH) * sigma * (1.0 + x * (1.0 - sigma))
        hx[r] = y.astype(B16)
    clear(hx, 1, 9)
    products(hx, 8, PITCH, w1, True, prod)
    for r in range(ROWS):
        y = gathered(prod, r * PITCH, COLS) + ax[2 + r, 16:80].astype(F32)
        grad[r] = y.astype(B16)

    settle(qbuf, q2, back_sem, 1)
    back = q2[:, 0, :].T[0:CAP]
    one = back.astype(B16)
    rest = back - one.astype(F32)
    two = rest.astype(B16)
    three = (rest - two.astype(F32)).astype(B16)
    lhs = jnp.concatenate([one, two, three], axis=0)
    for c in range(4):
        cut = slice(c * 512, (c + 1) * 512)
        got = jnp.dot(lhs, dt[:, cut], preferred_element_type=F32)
        got = got[0:32] + got[32:64] + got[64:96]
        own = iota((CAP, 512), 0) == rank_s[0:1, cut].astype(I32)
        innov[0:1, cut] = jnp.sum(jnp.where(own, got, 0.0), axis=0, keepdims=True)

    for c in first + second + out4:
        c.wait_send()
    settle(sbuf, r2, out_sem, 0)
    settle(qbuf, q2, back_sem, 0)


def on_device(
    state, background, conv_in, conv_out, probe,
    tile_ids, cell_taps, tap_weights, obs_values, obs_precision,
):
    vmem = pl.BlockSpec(memory_space=pltpu.VMEM)
    hbm = pl.BlockSpec(memory_space=pl.ANY)
    dma = pltpu.SemaphoreType.DMA
    wide = pltpu.VMEM((12, WIDE, CH), B16)
    kshape = (3, 3, CH, CH)
    grad, innov = pl.pallas_call(
        kernel,
        out_shape=(
            pltpu.VMEM((ROWS, COLS, CH), B16),
            pltpu.VMEM((1, COUNT), F32),
        ),
        in_specs=[hbm] * 10,
        out_specs=(vmem, vmem),
        scratch_shapes=[
            pltpu.VMEM((1, COUNT), I32),
            pltpu.VMEM((4, COUNT), I32),
            pltpu.VMEM((4, COUNT), F32),
            pltpu.VMEM((1, COUNT), F32),
            pltpu.VMEM((1, COUNT), F32),
            pltpu.VMEM((1, CH), F32),
            wide, wide, wide,
            pltpu.VMEM((ROWS, COLS, CH), B16),
            pltpu.VMEM(kshape, B16),
            pltpu.VMEM(kshape, B16),
            pltpu.VMEM((10, PITCH, CH), F32),
            pltpu.VMEM((10, PITCH, CH), B16),
            pltpu.VMEM((ROWS, COLS, CH), F32),
            pltpu.VMEM((3, 2, 10 * WIDE + 64, 128), F32),
            pltpu.VMEM((TILES, COUNT), B16),
            pltpu.VMEM((1, COUNT), F32),
            pltpu.VMEM((2, 2, 16, CH), B16),
            pltpu.VMEM((2, len(CORNERS), 16, CH), B16),
            pltpu.VMEM((TILES, 1, 384), F32),
            pltpu.VMEM((TILES, 1, 384), F32),
            pltpu.VMEM((TILES, 1, 128), F32),
            pltpu.VMEM((TILES, 1, 128), F32),
            pltpu.VMEM((16, 128), F32),
            pltpu.VMEM((len(SIDES), 16, 128), F32),
            dma((10,)),
            dma((2, 2, 2)),
            dma((2, len(CORNERS), 2)),
            dma((2,)),
            dma((2,)),
            dma((len(SIDES), 2)),
            dma((1,)),
        ],
        compiler_params=pltpu.CompilerParams(
            collective_id=0, has_side_effects=True, vmem_limit_bytes=56 * 2**20
        ),
    )(
        tile_ids.reshape(1, COUNT),
        cell_taps,
        tap_weights,
        obs_values.reshape(1, COUNT),
        obs_precision.reshape(1, COUNT),
        probe.reshape(1, CH),
        state,
        background,
        conv_in,
        conv_out,
    )
    return grad, innov.reshape(COUNT)


def solution(mesh):
    in_specs = (
        P("lat", "lon", None),
        P("lat", "lon", None),
        P(),
        P(),
        P(),
        P(("lat", "lon"), None),
        P(None, ("lat", "lon")),
        P(None, ("lat", "lon")),
        P(("lat", "lon")),
        P(("lat", "lon")),
    )
    out_specs = (P("lat", "lon", None), P(("lat", "lon")))
    return jax.shard_map(
        on_device, mesh=mesh, in_specs=in_specs, out_specs=out_specs, check_vma=False
    )
```

```python
import functools

import jax
import jax.numpy as jnp
from jax import lax
from jax.experimental import pallas as pl
from jax.experimental.pallas import tpu as pltpu
from jax.sharding import PartitionSpec as P

MESH = pl.DeviceIdType.MESH
B16 = jnp.bfloat16
F32 = jnp.float32
I32 = jnp.int32
ROWS, COLS, CH = 8, 64, 256
WIDE = 96
PITCH = 80
LATS, LONS = 8, 16
TILES = LATS * LONS
COUNT = 2048
CAP = 32
NT = (((1,), (1,)), ((), ()))
SIDES = [(a, b) for a in (-1, 0, 1) for b in (-1, 0, 1) if (a, b) != (0, 0)]
CORNERS = [s for s in SIDES if s[1] != 0]


def hops(a, b):
    y, x, z = a // 2, b // 4, b % 4
    return min(y, 4 - y) + min(x, 4 - x) + min(z, 4 - z)


OTHERS = [(a, b) for a in range(LATS) for b in range(LONS) if (a, b) != (0, 0)]
OTHERS.sort(key=lambda o: -hops(*o))
LINES = [o for o in OTHERS if 0 in o]


def iota(shape, dim):
    return lax.broadcasted_iota(I32, shape, dim)


def halves(x):
    high = x.astype(B16)
    return high, (x - high.astype(F32)).astype(B16)


def products(field, rows, pitch, weights, flipped, prod):
    count = rows * pitch
    lhs = jnp.concatenate(
        [field[i : i + rows].reshape(count, CH) for i in range(3)], axis=1
    )
    for j in range(3):
        if flipped:
            rhs = jnp.concatenate([weights[2 - i, 2 - j] for i in range(3)], axis=1)
            out = lax.dot_general(lhs, rhs, NT, preferred_element_type=F32)
        else:
            rhs = jnp.concatenate([weights[i, j] for i in range(3)], axis=0)
            out = jnp.dot(lhs, rhs, preferred_element_type=F32)
        prod[j, 0, 0:count] = out[:, :128]
        prod[j, 1, 0:count] = out[:, 128:]


def gathered(prod, start, count):
    parts = [
        prod[0, h, start : start + count]
        + prod[1, h, start + 1 : start + 1 + count]
        + prod[2, h, start + 2 : start + 2 + count]
        for h in range(2)
    ]
    return jnp.concatenate(parts, axis=1)


def pack(field, packs):
    sub = iota((16, CH), 0)
    west = jnp.zeros((16, CH), F32)
    east = jnp.zeros((16, CH), F32)
    for r in range(ROWS):
        here = (sub == 2 * r) | (sub == 2 * r + 1)
        x = field[2 + r, 16:32].astype(F32)
        west = jnp.where(here, x if r == 0 else pltpu.roll(x, 2 * r, 0), west)
        x = field[2 + r, 64:80].astype(F32)
        east = jnp.where(here, x if r == 7 else pltpu.roll(x, (2 * r - 14) % 16, 0), east)
    packs[0] = west.astype(B16)
    packs[1] = east.astype(B16)


def unpack(field, arrived):
    for n, (a, b) in enumerate(CORNERS):
        x = arrived[n].astype(F32)
        for r in {-1: (6, 7), 0: range(8), 1: (0, 1)}[a]:
            row = r + 2 + a * 8
            shift = (14 - 2 * r) % 16 if b < 0 else (-2 * r) % 16
            block = (x if shift == 0 else pltpu.roll(x, shift, 0)).astype(B16)
            if b < 0:
                field[row, 0:16] = block
            else:
                field[row, 80:96] = block


def kernel(
    ids_in, taps_in, wts_in, vals_in, prec_in, probe_in, state, background, conv_in, conv_out,
    grad, innov,
    ids, taps, wts, vals, prec, probe, sx, mx, ax, bg, w1, w2, before, hx, mb, prod, dt, rank_s,
    packs, arrived, sbuf, r2, qbuf, q2, zs, zr,
    load_sem, row_sem, pack_sem, out_sem, back_sem, z_sem, own_sem, ready,
):
    la = lax.axis_index("lat")
    lo = lax.axis_index("lon")

    def near(a, b):
        return place(a, b)[1]

    def send(src, dst, sems, to):
        return pltpu.make_async_remote_copy(
            src_ref=src, dst_ref=dst, send_sem=sems[0], recv_sem=sems[1],
            device_id=to, device_id_type=MESH,
        )

    me = la * LONS + lo
    barrier = pltpu.get_barrier_semaphore()

    def place(a, b):
        to = (lax.bitwise_and(la + a, LATS - 1), lax.bitwise_and(lo + b, LONS - 1))
        return to[0] * LONS + to[1], to

    ins = [(ids_in, ids), (prec_in, prec), (taps_in, taps), (wts_in, wts), (vals_in, vals)]
    ins += [(state, sx.at[2:10, 16:80]), (conv_in, w1), (conv_out, w2), (background, bg)]
    ins += [(probe_in, probe)]
    loads = [pltpu.make_async_copy(a, b, load_sem.at[n]) for n, (a, b) in enumerate(ins)]
    for c in loads:
        c.start()

    def greet(a, b):
        pl.semaphore_signal(barrier, inc=1, device_id=place(a, b)[1], device_id_type=MESH)

    def where(a, run, things):
        def body():
            for t in things:
                run(t)

        if a == 0:
            body()
        else:
            pl.when(la > 0 if a < 0 else la < LATS - 1)(body)

    for a in (-1, 1):
        where(a, lambda b: greet(a, b), (-1, 1))
    for a, b in LINES:
        greet(a, b)

    def each(copies, act):
        for a in (-1, 1, 0):
            where(a, act, [c for s, c in copies if s[0] == a])

    def scatter(src, dst, sems):
        for a, b in OTHERS:
            t, to = place(a, b)
            send(src.at[t], dst.at[me], (sems.at[0], sems.at[1]), to).start()
        own = pltpu.make_async_copy(src.at[me], dst.at[me], own_sem.at[0])
        own.start()
        own.wait()

    def settle(src, dst, sems, which):
        some = slice(0, TILES - 1)
        pltpu.make_async_copy(src.at[some], dst.at[some], sems.at[which]).wait()

    def halo(field, which):
        copies = [
            ((-1, 0), send(field.at[2:4, 16:80], field.at[10:12, 16:80],
                           (row_sem.at[which, 0, 0], row_sem.at[which, 1, 1]), near(-1, 0))),
            ((1, 0), send(field.at[8:10, 16:80], field.at[0:2, 16:80],
                          (row_sem.at[which, 1, 0], row_sem.at[which, 0, 1]), near(1, 0))),
        ]
        for n, (a, b) in enumerate(CORNERS):
            m = CORNERS.index((-a, -b))
            copies.append(
                ((a, b), send(packs.at[which, 0 if b < 0 else 1], arrived.at[which, m],
                              (pack_sem.at[which, n, 0], pack_sem.at[which, m, 1]), near(a, b)))
            )
        return copies

    def arrive(copies):
        back = {s: c for s, c in copies}
        each([(s, back[-s[0], -s[1]]) for s in back], lambda c: c.wait_recv())

    def clear(field, low, high):
        @pl.when(la == 0)
        def _():
            field[0:low] = jnp.zeros((low,) + field.shape[1:], field.dtype)

        @pl.when(la == LATS - 1)
        def _():
            field[high:] = jnp.zeros((field.shape[0] - high,) + field.shape[1:], field.dtype)

    for c in loads[:5]:
        c.wait()
    upper = jnp.where(iota((128, 128), 0) <= iota((128, 128), 1), 1.0, 0.0).astype(B16)
    carry = jnp.zeros((128, 1), F32)
    ranks = []
    for c in range(16):
        hit = iota((128, 128), 0) == ids[0:1, c * 128 : (c + 1) * 128]
        one = jnp.where(hit, 1.0, 0.0).astype(B16)
        dt[:, c * 128 : (c + 1) * 128] = one
        run = jnp.dot(one, upper, preferred_element_type=F32) + carry
        ranks.append(jnp.sum(jnp.where(hit, run, 0.0), axis=0, keepdims=True) - 1.0)
        carry = run[:, 127:128]
    rank = jnp.concatenate(ranks, axis=1)
    rank_s[...] = rank
    acc = jnp.zeros((128, 512), F32)
    for c in range(8):
        cut = slice(c * 256, (c + 1) * 256)
        own = iota((CAP, 256), 0) == rank[:, cut].astype(I32)
        p = prec[0:1, cut]
        rows = [taps[k : k + 1, cut].astype(F32) - 256.0 for k in range(4)]
        scaled = [wts[k : k + 1, cut] * p for k in range(4)] + [vals[0:1, cut] * p]
        tops = [s.astype(B16).astype(F32) for s in scaled]
        lows = [s - t for s, t in zip(scaled, tops)]
        rows += tops[:4] + lows[:4] + [tops[4], lows[4]]
        spots = [jnp.where(own, r, 0.0).astype(B16) for r in rows]
        spots.append(jnp.zeros((64, 256), B16))
        x = jnp.concatenate(spots, axis=0)
        acc = acc + lax.dot_general(dt[:, cut], x, NT, preferred_element_type=F32)
    sbuf[:, 0, 0:128] = acc[:, 0:128]
    sbuf[:, 0, 128:256] = acc[:, 128:256] + acc[:, 256:384]
    sbuf[:, 0, 256:384] = acc[:, 384:512]

    loads[5].wait()
    pack(sx, packs.at[0])
    ends = jnp.where((la == 0) | (la == LATS - 1), 2, 4)
    pl.semaphore_wait(barrier, len(LINES) + ends)
    for a in range(1, LATS):
        pl.semaphore_signal(ready, inc=1, device_id=place(a, 0)[1], device_id_type=MESH)
    first = halo(sx, 0)
    each(first, lambda c: c.start())
    pl.semaphore_wait(ready, LATS - 1)
    scatter(sbuf, r2, out_sem)

    loads[6].wait()
    arrive(first)
    unpack(sx, arrived.at[0])
    clear(sx, 2, 10)
    products(sx, 10, WIDE, w1, False, prod)
    for r in range(10):
        b = gathered(prod, r * WIDE + 14, PITCH)
        before[r] = b
        hx[r] = (b / (1.0 + jnp.exp(-b))).astype(B16)
    clear(hx, 1, 9)

    for c in loads[7:]:
        c.wait()
    products(hx, 8, PITCH, w2, False, prod)
    pr = probe[...]
    ph, plow = halves(pr)
    sub16 = iota((16, CH), 0)
    readout = jnp.where(
        sub16 == 0, ph.astype(F32), jnp.where(sub16 == 1, plow.astype(F32), 0.0)
    ).astype(B16)
    strips = []
    for r in range(ROWS):
        m = gathered(prod, r * PITCH, COLS) + sx[2 + r, 16:80].astype(F32)
        high, low = halves(m)
        s = lax.dot_general(readout, high, NT, preferred_element_type=F32)
        t = lax.dot_general(readout, low, NT, preferred_element_type=F32)
        strips.append(s[0:1] + s[1:2] + t[0:1])
        d = m - bg[r].astype(F32)
        mb[r] = d
        mx[2 + r, 16:80] = d.astype(B16)
    pack(mx, packs.at[1])
    second = halo(mx, 1)
    each(second, lambda c: c.start())
    tables = [
        jnp.broadcast_to(jnp.concatenate(strips[2 * q : 2 * q + 2], axis=1), (8, 128))
        for q in range(4)
    ]

    settle(sbuf, r2, out_sem, 1)
    cells, shares = [], []
    for t in range(TILES // 8):
        own = slice(8 * t, 8 * t + 8)
        cell = r2[own, 0, 0:128].astype(I32) + 256
        w = r2[own, 0, 128:256]
        lane = lax.bitwise_and(cell, 127)
        page = lax.shift_right_logical(cell, 7)
        got = jnp.zeros((8, 128), F32)
        for q in range(4):
            look = jnp.take_along_axis(tables[q], lane, axis=1, mode="promise_in_bounds")
            got = jnp.where(page == q, look, got)
        res = w * got - r2[own, 0, 256:384]
        res = res + pltpu.roll(res, 64, 1)
        res = res + pltpu.roll(res, 32, 1)
        qbuf[own, 0, :] = res
        cells.append(cell)
        shares.append(w * res)

    total = jnp.zeros((256, 256), F32)
    for t in range(0, TILES // 8, 2):
        cell = jnp.concatenate(cells[t : t + 2], axis=1)
        share = jnp.concatenate(shares[t : t + 2], axis=1)
        upper_cell = lax.shift_right_logical(cell, 5)
        lower_cell = lax.bitwise_and(cell, 31)
        top = share.astype(B16).astype(F32)
        low = share - top
        tops, lows, marks = [], [], []
        for g in range(8):
            hit = iota((16, 256), 0) == upper_cell[g : g + 1]
            tops.append(jnp.where(hit, top[g : g + 1], 0.0).astype(B16))
            lows.append(jnp.where(hit, low[g : g + 1], 0.0).astype(B16))
            marks.append(
                jnp.where(iota((32, 256), 0) == lower_cell[g : g + 1], 1.0, 0.0).astype(B16)
            )
        lhs = jnp.concatenate(tops + lows, axis=0)
        rhs = jnp.concatenate(marks, axis=0)
        total = total + lax.dot_general(lhs, rhs, NT, preferred_element_type=F32)
    total = total[0:128] + total[128:256]
    total = jnp.where(iota((128, 256), 0) // 16 == iota((128, 256), 1) // 32, total, 0.0)
    fold = total[0:16]
    for g in range(1, 8):
        fold = fold + total[g * 16 : (g + 1) * 16]
    fold = fold[:, 0:128] + fold[:, 128:256]
    fold = fold + pltpu.roll(fold, 64, 1)
    fold = fold + pltpu.roll(fold, 32, 1)
    zs[...] = fold
    out4 = []
    for n, (a, b) in enumerate(SIDES):
        m = SIDES.index((-a, -b))
        out4.append(((a, b), send(zs, zr.at[m], (z_sem.at[n, 0], z_sem.at[m, 1]), near(a, b))))
    each(out4, lambda c: c.start())

    scatter(qbuf, q2, back_sem)

    group = iota((16, 128), 1) // 32
    base = jnp.where(iota((128, CH), 0) // 64 == 0, ph.astype(F32), plow.astype(F32)).astype(B16)
    sub = iota((16, 128), 0)
    spot = lax.bitwise_and(iota((16, 128), 1), 31)
    marks = [spot == sub, spot == sub + 16]

    def parted(z):
        top = z.astype(B16).astype(F32)
        return jnp.where(lax.bitwise_and(group, 1) == 0, top, z - top)

    def outer(blocks):
        lhs = jnp.concatenate(
            [
                jnp.where(marks[c % 2], z[2 * r + c // 2 : 2 * r + c // 2 + 1], 0.0).astype(B16)
                for z, r, c in blocks
            ],
            axis=0,
        )
        return jnp.dot(lhs, base, preferred_element_type=F32)

    center = parted(fold)
    local = outer([(center, r, c) for r in range(ROWS) for c in range(4)])
    for r in range(ROWS):
        ax[2 + r, 16:80] = (mb[r] + local[r * 64 : (r + 1) * 64]).astype(B16)
    arrive(second)
    unpack(mx, arrived.at[1])
    arrive(out4)
    around = {s: parted(zr[n]) for n, s in enumerate(SIDES)}
    for a, rows in ((-1, (6, 7)), (1, (0, 1))):
        piece = outer([(around[a, 0], r, c) for r in rows for c in range(4)])
        for n, r in enumerate(rows):
            row = r + 2 + a * 8
            ax[row, 16:80] = (
                mx[row, 16:80].astype(F32) + piece[n * 64 : (n + 1) * 64]
            ).astype(B16)
    for b, c, at in ((-1, 3, 0), (1, 0, 80)):
        spots = [(a, r) for a, rows in ((-1, (6, 7)), (0, range(8)), (1, (0, 1))) for r in rows]
        piece = outer([(around[a, b], r, c) for a, r in spots])
        for n, (a, r) in enumerate(spots):
            row = r + 2 + a * 8
            ax[row, at : at + 16] = (
                mx[row, at : at + 16].astype(F32) + piece[n * 16 : (n + 1) * 16]
            ).astype(B16)
    clear(ax, 2, 10)

    products(ax, 10, WIDE, w2, True, prod)
    for r in range(10):
        x = before[r]
        sigma = 1.0 / (1.0 + jnp.exp(-x))
        y = gathered(prod, r * WIDE + 14, PITCH) * sigma * (1.0 + x * (1.0 - sigma))
        hx[r] = y.astype(B16)
    clear(hx, 1, 9)
    products(hx, 8, PITCH, w1, True, prod)
    for r in range(ROWS):
        y = gathered(prod, r * PITCH, COLS) + ax[2 + r, 16:80].astype(F32)
        grad[r] = y.astype(B16)

    settle(qbuf, q2, back_sem, 1)
    back = q2[:, 0, :].T[0:CAP]
    one = back.astype(B16)
    rest = back - one.astype(F32)
    two = rest.astype(B16)
    three = (rest - two.astype(F32)).astype(B16)
    lhs = jnp.concatenate([one, two, three], axis=0)
    for c in range(4):
        cut = slice(c * 512, (c + 1) * 512)
        got = jnp.dot(lhs, dt[:, cut], preferred_element_type=F32)
        got = got[0:32] + got[32:64] + got[64:96]
        own = iota((CAP, 512), 0) == rank_s[0:1, cut].astype(I32)
        innov[0:1, cut] = jnp.sum(jnp.where(own, got, 0.0), axis=0, keepdims=True)

    each(first + second + out4, lambda c: c.wait_send())
    settle(sbuf, r2, out_sem, 0)
    settle(qbuf, q2, back_sem, 0)


def on_device(
    state, background, conv_in, conv_out, probe,
    tile_ids, cell_taps, tap_weights, obs_values, obs_precision,
):
    vmem = pl.BlockSpec(memory_space=pltpu.VMEM)
    hbm = pl.BlockSpec(memory_space=pl.ANY)
    dma = pltpu.SemaphoreType.DMA
    wide = pltpu.VMEM((12, WIDE, CH), B16)
    kshape = (3, 3, CH, CH)
    grad, innov = pl.pallas_call(
        kernel,
        out_shape=(
            pltpu.VMEM((ROWS, COLS, CH), B16),
            pltpu.VMEM((1, COUNT), F32),
        ),
        in_specs=[hbm] * 10,
        out_specs=(vmem, vmem),
        scratch_shapes=[
            pltpu.VMEM((1, COUNT), I32),
            pltpu.VMEM((4, COUNT), I32),
            pltpu.VMEM((4, COUNT), F32),
            pltpu.VMEM((1, COUNT), F32),
            pltpu.VMEM((1, COUNT), F32),
            pltpu.VMEM((1, CH), F32),
            wide, wide, wide,
            pltpu.VMEM((ROWS, COLS, CH), B16),
            pltpu.VMEM(kshape, B16),
            pltpu.VMEM(kshape, B16),
            pltpu.VMEM((10, PITCH, CH), F32),
            pltpu.VMEM((10, PITCH, CH), B16),
            pltpu.VMEM((ROWS, COLS, CH), F32),
            pltpu.VMEM((3, 2, 10 * WIDE + 64, 128), F32),
            pltpu.VMEM((TILES, COUNT), B16),
            pltpu.VMEM((1, COUNT), F32),
            pltpu.VMEM((2, 2, 16, CH), B16),
            pltpu.VMEM((2, len(CORNERS), 16, CH), B16),
            pltpu.VMEM((TILES, 1, 384), F32),
            pltpu.VMEM((TILES, 1, 384), F32),
            pltpu.VMEM((TILES, 1, 128), F32),
            pltpu.VMEM((TILES, 1, 128), F32),
            pltpu.VMEM((16, 128), F32),
            pltpu.VMEM((len(SIDES), 16, 128), F32),
            dma((10,)),
            dma((2, 2, 2)),
            dma((2, len(CORNERS), 2)),
            dma((2,)),
            dma((2,)),
            dma((len(SIDES), 2)),
            dma((1,)),
            pltpu.SemaphoreType.REGULAR,
        ],
        compiler_params=pltpu.CompilerParams(
            collective_id=0, has_side_effects=True, vmem_limit_bytes=56 * 2**20
        ),
    )(
        tile_ids.reshape(1, COUNT),
        cell_taps,
        tap_weights,
        obs_values.reshape(1, COUNT),
        obs_precision.reshape(1, COUNT),
        probe.reshape(1, CH),
        state,
        background,
        conv_in,
        conv_out,
    )
    return grad, innov.reshape(COUNT)


def solution(mesh):
    in_specs = (
        P("lat", "lon", None),
        P("lat", "lon", None),
        P(),
        P(),
        P(),
        P(("lat", "lon"), None),
        P(None, ("lat", "lon")),
        P(None, ("lat", "lon")),
        P(("lat", "lon")),
        P(("lat", "lon")),
    )
    out_specs = (P("lat", "lon", None), P(("lat", "lon")))
    return jax.shard_map(
        on_device, mesh=mesh, in_specs=in_specs, out_specs=out_specs, check_vma=False
    )
```

```python
import functools

import jax
import jax.numpy as jnp
from jax import lax
from jax.experimental import pallas as pl
from jax.experimental.pallas import tpu as pltpu
from jax.sharding import PartitionSpec as P

MESH = pl.DeviceIdType.MESH
B16 = jnp.bfloat16
F32 = jnp.float32
I32 = jnp.int32
ROWS, COLS, CH = 8, 64, 256
PITCH = 80
LATS, LONS = 8, 16
TILES = LATS * LONS
COUNT = 2048
CAP = 32
NT = (((1,), (1,)), ((), ()))
SIDES = [(a, b) for a in (-1, 0, 1) for b in (-1, 0, 1) if (a, b) != (0, 0)]
CORNERS = [s for s in SIDES if s[1] != 0]


def hops(a, b):
    y, x, z = a // 2, b // 4, b % 4
    return min(y, 4 - y) + min(x, 4 - x) + min(z, 4 - z)


OTHERS = [(a, b) for a in range(LATS) for b in range(LONS) if (a, b) != (0, 0)]
OTHERS.sort(key=lambda o: -hops(*o))
LINES = [o for o in OTHERS if 0 in o]


def iota(shape, dim):
    return lax.broadcasted_iota(I32, shape, dim)


def halves(x):
    high = x.astype(B16)
    return high, (x - high.astype(F32)).astype(B16)


def weighted(lhs, weights, flipped, j):
    if flipped:
        rhs = jnp.concatenate([weights[2 - i, 2 - j] for i in range(3)], axis=1)
        return lax.dot_general(lhs, rhs, NT, preferred_element_type=F32)
    rhs = jnp.concatenate([weights[i, j] for i in range(3)], axis=0)
    return jnp.dot(lhs, rhs, preferred_element_type=F32)


def windows(field, first, rows):
    count = rows * field.shape[1]
    return jnp.concatenate(
        [field[first + i : first + i + rows].reshape(count, CH) for i in range(3)], axis=1
    )


def products(field, weights, flipped, prod):
    lhs = windows(field, 0, ROWS)
    for j in range(3):
        out = weighted(lhs, weights, flipped, j)
        prod[j, 0, 0 : ROWS * PITCH] = out[:, :128]
        prod[j, 1, 0 : ROWS * PITCH] = out[:, 128:]


def put(prod, j, row, out):
    start = row * PITCH + 8
    prod[j, 0, start : start + COLS] = out[:, :128]
    prod[j, 1, start : start + COLS] = out[:, 128:]


def inner(field, weights, flipped, prod, j):
    out = weighted(windows(field, 2, 6), weights, flipped, j)
    for n in range(6):
        put(prod, j, 2 + n, out[n * COLS : (n + 1) * COLS])


def border(field, edge, weights, flipped, prod):
    sides = [
        jnp.concatenate([edge[b, 2 * i : 2 * i + 24] for i in range(3)], axis=1) for b in range(2)
    ]
    lhs = jnp.concatenate(
        [windows(field, 0, 2), windows(field, 8, 2), jnp.concatenate(sides, axis=0).astype(B16)],
        axis=0,
    )
    for j in range(3):
        out = weighted(lhs, weights, flipped, j)
        for n, row in enumerate((0, 1, 8, 9)):
            put(prod, j, row, out[n * COLS : (n + 1) * COLS])
        for b in range(2):
            for row in range(10):
                at = 4 * COLS + 24 * b + 2 * row
                start = row * PITCH + (72 if b else 6)
                prod[j, 0, start : start + 2] = out[at : at + 2, :128]
                prod[j, 1, start : start + 2] = out[at : at + 2, 128:]


def gathered(prod, start, count):
    parts = [
        prod[0, h, start : start + count]
        + prod[1, h, start + 1 : start + 1 + count]
        + prod[2, h, start + 2 : start + 2 + count]
        for h in range(2)
    ]
    return jnp.concatenate(parts, axis=1)


def pack(field, packs):
    sub = iota((16, CH), 0)
    west = jnp.zeros((16, CH), F32)
    east = jnp.zeros((16, CH), F32)
    for r in range(ROWS):
        here = (sub == 2 * r) | (sub == 2 * r + 1)
        x = field[2 + r, 0:16].astype(F32)
        west = jnp.where(here, x if r == 0 else pltpu.roll(x, 2 * r, 0), west)
        x = field[2 + r, 48:64].astype(F32)
        east = jnp.where(here, x if r == 7 else pltpu.roll(x, (2 * r - 14) % 16, 0), east)
    packs[0] = west.astype(B16)
    packs[1] = east.astype(B16)


def assemble(edge, parts, north, south):
    for n, (a, b) in enumerate(CORNERS):
        x = parts[n]
        side = 0 if b < 0 else 1
        if a < 0:
            edge[side, 0:4] = jnp.where(north, x[12:16], 0.0)
        elif a == 0:
            edge[side, 4:20] = x
        else:
            edge[side, 20:24] = jnp.where(south, x[0:4], 0.0)


def kernel(
    ids_in, taps_in, wts_in, vals_in, prec_in, probe_in, state, background, conv_in, conv_out,
    grad, innov,
    ids, taps, wts, vals, prec, probe, edge, sx, mx, ax, bg, w1, w2, before, hx, mb, prod, dt, rank_s,
    packs, arrived, sbuf, r2, qbuf, q2, zs, zr,
    load_sem, row_sem, pack_sem, out_sem, back_sem, z_sem, own_sem, ready,
):
    la = lax.axis_index("lat")
    lo = lax.axis_index("lon")

    def near(a, b):
        return place(a, b)[1]

    def send(src, dst, sems, to):
        return pltpu.make_async_remote_copy(
            src_ref=src, dst_ref=dst, send_sem=sems[0], recv_sem=sems[1],
            device_id=to, device_id_type=MESH,
        )

    me = la * LONS + lo
    barrier = pltpu.get_barrier_semaphore()

    def place(a, b):
        to = (lax.bitwise_and(la + a, LATS - 1), lax.bitwise_and(lo + b, LONS - 1))
        return to[0] * LONS + to[1], to

    ins = [(ids_in, ids), (prec_in, prec), (taps_in, taps), (wts_in, wts), (vals_in, vals)]
    ins += [(state, sx.at[2:10]), (conv_in, w1), (conv_out, w2), (background, bg)]
    ins += [(probe_in, probe)]
    loads = [pltpu.make_async_copy(a, b, load_sem.at[n]) for n, (a, b) in enumerate(ins)]
    for c in loads:
        c.start()

    def greet(a, b):
        pl.semaphore_signal(barrier, inc=1, device_id=place(a, b)[1], device_id_type=MESH)

    def where(a, run, things):
        def body():
            for t in things:
                run(t)

        if a == 0:
            body()
        else:
            pl.when(la > 0 if a < 0 else la < LATS - 1)(body)

    for a in (-1, 1):
        where(a, lambda b: greet(a, b), (-1, 1))
    for a, b in LINES:
        greet(a, b)

    def each(copies, act):
        for a in (-1, 1, 0):
            where(a, act, [c for s, c in copies if s[0] == a])

    def depart(src, dst, sems, offsets):
        for a, b in offsets:
            t, to = place(a, b)
            send(src.at[t], dst.at[me], (sems.at[0], sems.at[1]), to).start()

    def stay(src, dst):
        own = pltpu.make_async_copy(src.at[me], dst.at[me], own_sem.at[0])
        own.start()
        own.wait()

    def settle(src, dst, sems, which):
        some = slice(0, TILES - 1)
        pltpu.make_async_copy(src.at[some], dst.at[some], sems.at[which]).wait()

    def halo(field, which):
        copies = [
            ((-1, 0), send(field.at[2:4], field.at[10:12],
                           (row_sem.at[which, 0, 0], row_sem.at[which, 1, 1]), near(-1, 0))),
            ((1, 0), send(field.at[8:10], field.at[0:2],
                          (row_sem.at[which, 1, 0], row_sem.at[which, 0, 1]), near(1, 0))),
        ]
        for n, (a, b) in enumerate(CORNERS):
            m = CORNERS.index((-a, -b))
            copies.append(
                ((a, b), send(packs.at[which, 0 if b < 0 else 1], arrived.at[which, m],
                              (pack_sem.at[which, n, 0], pack_sem.at[which, m, 1]), near(a, b)))
            )
        return copies

    def arrive(copies):
        back = {s: c for s, c in copies}
        each([(s, back[-s[0], -s[1]]) for s in back], lambda c: c.wait_recv())

    def clear(field, low, high):
        @pl.when(la == 0)
        def _():
            field[0:low] = jnp.zeros((low,) + field.shape[1:], field.dtype)

        @pl.when(la == LATS - 1)
        def _():
            field[high:] = jnp.zeros((field.shape[0] - high,) + field.shape[1:], field.dtype)

    for c in loads[:5]:
        c.wait()
    upper = jnp.where(iota((128, 128), 0) <= iota((128, 128), 1), 1.0, 0.0).astype(B16)
    carry = jnp.zeros((128, 1), F32)
    ranks = []
    for c in range(16):
        hit = iota((128, 128), 0) == ids[0:1, c * 128 : (c + 1) * 128]
        one = jnp.where(hit, 1.0, 0.0).astype(B16)
        dt[:, c * 128 : (c + 1) * 128] = one
        run = jnp.dot(one, upper, preferred_element_type=F32) + carry
        ranks.append(jnp.sum(jnp.where(hit, run, 0.0), axis=0, keepdims=True) - 1.0)
        carry = run[:, 127:128]
    rank = jnp.concatenate(ranks, axis=1)
    rank_s[...] = rank
    acc = jnp.zeros((128, 512), F32)
    for c in range(8):
        cut = slice(c * 256, (c + 1) * 256)
        own = iota((CAP, 256), 0) == rank[:, cut].astype(I32)
        p = prec[0:1, cut]
        rows = [taps[k : k + 1, cut].astype(F32) - 256.0 for k in range(4)]
        scaled = [wts[k : k + 1, cut] * p for k in range(4)] + [vals[0:1, cut] * p]
        tops = [s.astype(B16).astype(F32) for s in scaled]
        lows = [s - t for s, t in zip(scaled, tops)]
        rows += tops[:4] + lows[:4] + [tops[4], lows[4]]
        spots = [jnp.where(own, r, 0.0).astype(B16) for r in rows]
        spots.append(jnp.zeros((64, 256), B16))
        x = jnp.concatenate(spots, axis=0)
        acc = acc + lax.dot_general(dt[:, cut], x, NT, preferred_element_type=F32)
    sbuf[:, 0, 0:128] = acc[:, 0:128]
    sbuf[:, 0, 128:256] = acc[:, 128:256] + acc[:, 256:384]
    sbuf[:, 0, 256:384] = acc[:, 384:512]

    loads[5].wait()
    pack(sx, packs.at[0])
    ends = jnp.where((la == 0) | (la == LATS - 1), 2, 4)
    pl.semaphore_wait(barrier, len(LINES) + ends)
    for a in range(1, LATS):
        pl.semaphore_signal(ready, inc=1, device_id=place(a, 0)[1], device_id_type=MESH)
    first = halo(sx, 0)
    each(first, lambda c: c.start())
    pl.semaphore_wait(ready, LATS - 1)
    depart(sbuf, r2, out_sem, OTHERS)
    stay(sbuf, r2)

    loads[6].wait()
    for j in range(3):
        inner(sx, w1, False, prod, j)
    arrive(first)
    assemble(edge, [arrived[0, n].astype(F32) for n in range(6)], la > 0, la < LATS - 1)
    clear(sx, 2, 10)
    border(sx, edge, w1, False, prod)
    for r in range(10):
        b = gathered(prod, r * PITCH + 6, PITCH)
        before[r] = b
        hx[r] = (b / (1.0 + jnp.exp(-b))).astype(B16)
    clear(hx, 1, 9)

    for c in loads[7:]:
        c.wait()
    products(hx, w2, False, prod)
    pr = probe[...]
    ph, plow = halves(pr)
    sub16 = iota((16, CH), 0)
    readout = jnp.where(
        sub16 == 0, ph.astype(F32), jnp.where(sub16 == 1, plow.astype(F32), 0.0)
    ).astype(B16)
    strips = []
    for r in range(ROWS):
        m = gathered(prod, r * PITCH, COLS) + sx[2 + r].astype(F32)
        high, low = halves(m)
        s = lax.dot_general(readout, high, NT, preferred_element_type=F32)
        t = lax.dot_general(readout, low, NT, preferred_element_type=F32)
        strips.append(s[0:1] + s[1:2] + t[0:1])
        d = m - bg[r].astype(F32)
        mb[r] = d
        mx[2 + r] = d.astype(B16)
    pack(mx, packs.at[1])
    second = halo(mx, 1)
    each(second, lambda c: c.start())
    tables = [
        jnp.broadcast_to(jnp.concatenate(strips[2 * q : 2 * q + 2], axis=1), (8, 128))
        for q in range(4)
    ]

    settle(sbuf, r2, out_sem, 1)
    cells, shares = [], []
    for t in range(TILES // 8):
        own = slice(8 * t, 8 * t + 8)
        cell = r2[own, 0, 0:128].astype(I32) + 256
        w = r2[own, 0, 128:256]
        lane = lax.bitwise_and(cell, 127)
        page = lax.shift_right_logical(cell, 7)
        got = jnp.zeros((8, 128), F32)
        for q in range(4):
            look = jnp.take_along_axis(tables[q], lane, axis=1, mode="promise_in_bounds")
            got = jnp.where(page == q, look, got)
        res = w * got - r2[own, 0, 256:384]
        res = res + pltpu.roll(res, 64, 1)
        res = res + pltpu.roll(res, 32, 1)
        qbuf[own, 0, :] = res
        cells.append(cell)
        shares.append(w * res)

    total = jnp.zeros((256, 256), F32)
    for t in range(0, TILES // 8, 2):
        cell = jnp.concatenate(cells[t : t + 2], axis=1)
        share = jnp.concatenate(shares[t : t + 2], axis=1)
        upper_cell = lax.shift_right_logical(cell, 5)
        lower_cell = lax.bitwise_and(cell, 31)
        top = share.astype(B16).astype(F32)
        low = share - top
        tops, lows, marks = [], [], []
        for g in range(8):
            hit = iota((16, 256), 0) == upper_cell[g : g + 1]
            tops.append(jnp.where(hit, top[g : g + 1], 0.0).astype(B16))
            lows.append(jnp.where(hit, low[g : g + 1], 0.0).astype(B16))
            marks.append(
                jnp.where(iota((32, 256), 0) == lower_cell[g : g + 1], 1.0, 0.0).astype(B16)
            )
        lhs = jnp.concatenate(tops + lows, axis=0)
        rhs = jnp.concatenate(marks, axis=0)
        total = total + lax.dot_general(lhs, rhs, NT, preferred_element_type=F32)
    total = total[0:128] + total[128:256]
    total = jnp.where(iota((128, 256), 0) // 16 == iota((128, 256), 1) // 32, total, 0.0)
    fold = total[0:16]
    for g in range(1, 8):
        fold = fold + total[g * 16 : (g + 1) * 16]
    fold = fold[:, 0:128] + fold[:, 128:256]
    fold = fold + pltpu.roll(fold, 64, 1)
    fold = fold + pltpu.roll(fold, 32, 1)
    zs[...] = fold
    out4 = []
    for n, (a, b) in enumerate(SIDES):
        m = SIDES.index((-a, -b))
        out4.append(((a, b), send(zs, zr.at[m], (z_sem.at[n, 0], z_sem.at[m, 1]), near(a, b))))
    each(out4, lambda c: c.start())

    stay(qbuf, q2)
    group = iota((16, 128), 1) // 32
    base = jnp.where(iota((128, CH), 0) // 64 == 0, ph.astype(F32), plow.astype(F32)).astype(B16)
    sub = iota((16, 128), 0)
    odd = lax.bitwise_and(sub, 1)
    spot = lax.bitwise_and(iota((16, 128), 1), 31)
    marks = [spot == sub, spot == sub + 16]

    def parted(z):
        top = z.astype(B16).astype(F32)
        return jnp.where(lax.bitwise_and(group, 1) == 0, top, z - top)

    def outer(blocks):
        lhs = jnp.concatenate(
            [
                jnp.where(marks[c % 2], z[2 * r + c // 2 : 2 * r + c // 2 + 1], 0.0).astype(B16)
                for z, r, c in blocks
            ],
            axis=0,
        )
        return jnp.dot(lhs, base, preferred_element_type=F32)

    center = parted(fold)
    for r in range(ROWS):
        local = outer([(center, r, c) for c in range(4)])
        ax[2 + r] = (mb[r] + local).astype(B16)
        depart(qbuf, q2, back_sem, OTHERS[r * 10 : r * 10 + 10])
    for j in range(3):
        inner(ax, w2, True, prod, j)
        depart(qbuf, q2, back_sem, OTHERS[80 + 16 * j : 96 + 16 * j])

    arrive(second)
    arrive(out4)
    around = {s: parted(zr[n]) for n, s in enumerate(SIDES)}
    for a, rows in ((-1, (6, 7)), (1, (0, 1))):
        piece = outer([(around[a, 0], r, c) for r in rows for c in range(4)])
        for n, r in enumerate(rows):
            row = r + 2 + a * 8
            ax[row] = (mx[row].astype(F32) + piece[n * 64 : (n + 1) * 64]).astype(B16)
    strips = []
    for a, b in CORNERS:
        z = around[a, b]
        if b < 0:
            z = jnp.where(odd == 1, z, pltpu.roll(z, 15, 0))
            hit = spot == odd + 30
        else:
            z = jnp.where(odd == 0, z, pltpu.roll(z, 1, 0))
            hit = spot == odd
        strips.append(jnp.where(hit, z, 0.0).astype(B16))
    piece = jnp.dot(jnp.concatenate(strips, axis=0), base, preferred_element_type=F32)
    parts = [
        (arrived[1, n].astype(F32) + piece[16 * n : 16 * n + 16]).astype(B16).astype(F32)
        for n in range(6)
    ]
    assemble(edge, parts, la > 0, la < LATS - 1)
    clear(ax, 2, 10)

    border(ax, edge, w2, True, prod)
    for r in range(10):
        x = before[r]
        sigma = 1.0 / (1.0 + jnp.exp(-x))
        y = gathered(prod, r * PITCH + 6, PITCH) * sigma * (1.0 + x * (1.0 - sigma))
        hx[r] = y.astype(B16)
    clear(hx, 1, 9)
    products(hx, w1, True, prod)
    for r in range(ROWS):
        y = gathered(prod, r * PITCH, COLS) + ax[2 + r].astype(F32)
        grad[r] = y.astype(B16)

    settle(qbuf, q2, back_sem, 1)
    back = q2[:, 0, :].T[0:CAP]
    one = back.astype(B16)
    rest = back - one.astype(F32)
    two = rest.astype(B16)
    three = (rest - two.astype(F32)).astype(B16)
    lhs = jnp.concatenate([one, two, three], axis=0)
    for c in range(4):
        cut = slice(c * 512, (c + 1) * 512)
        got = jnp.dot(lhs, dt[:, cut], preferred_element_type=F32)
        got = got[0:32] + got[32:64] + got[64:96]
        own = iota((CAP, 512), 0) == rank_s[0:1, cut].astype(I32)
        innov[0:1, cut] = jnp.sum(jnp.where(own, got, 0.0), axis=0, keepdims=True)

    each(first + second + out4, lambda c: c.wait_send())
    settle(sbuf, r2, out_sem, 0)
    settle(qbuf, q2, back_sem, 0)


def on_device(
    state, background, conv_in, conv_out, probe,
    tile_ids, cell_taps, tap_weights, obs_values, obs_precision,
):
    vmem = pl.BlockSpec(memory_space=pltpu.VMEM)
    hbm = pl.BlockSpec(memory_space=pl.ANY)
    dma = pltpu.SemaphoreType.DMA
    wide = pltpu.VMEM((12, COLS, CH), B16)
    kshape = (3, 3, CH, CH)
    grad, innov = pl.pallas_call(
        kernel,
        out_shape=(
            pltpu.VMEM((ROWS, COLS, CH), B16),
            pltpu.VMEM((1, COUNT), F32),
        ),
        in_specs=[hbm] * 10,
        out_specs=(vmem, vmem),
        scratch_shapes=[
            pltpu.VMEM((1, COUNT), I32),
            pltpu.VMEM((4, COUNT), I32),
            pltpu.VMEM((4, COUNT), F32),
            pltpu.VMEM((1, COUNT), F32),
            pltpu.VMEM((1, COUNT), F32),
            pltpu.VMEM((1, CH), F32),
            pltpu.VMEM((2, 32, CH), F32),
            wide, wide, wide,
            pltpu.VMEM((ROWS, COLS, CH), B16),
            pltpu.VMEM(kshape, B16),
            pltpu.VMEM(kshape, B16),
            pltpu.VMEM((10, PITCH, CH), F32),
            pltpu.VMEM((10, PITCH, CH), B16),
            pltpu.VMEM((ROWS, COLS, CH), F32),
            pltpu.VMEM((3, 2, 10 * PITCH + 64, 128), F32),
            pltpu.VMEM((TILES, COUNT), B16),
            pltpu.VMEM((1, COUNT), F32),
            pltpu.VMEM((2, 2, 16, CH), B16),
            pltpu.VMEM((2, len(CORNERS), 16, CH), B16),
            pltpu.VMEM((TILES, 1, 384), F32),
            pltpu.VMEM((TILES, 1, 384), F32),
            pltpu.VMEM((TILES, 1, 128), F32),
            pltpu.VMEM((TILES, 1, 128), F32),
            pltpu.VMEM((16, 128), F32),
            pltpu.VMEM((len(SIDES), 16, 128), F32),
            dma((10,)),
            dma((2, 2, 2)),
            dma((2, len(CORNERS), 2)),
            dma((2,)),
            dma((2,)),
            dma((len(SIDES), 2)),
            dma((1,)),
            pltpu.SemaphoreType.REGULAR,
        ],
        compiler_params=pltpu.CompilerParams(
            collective_id=0, has_side_effects=True, vmem_limit_bytes=56 * 2**20
        ),
    )(
        tile_ids.reshape(1, COUNT),
        cell_taps,
        tap_weights,
        obs_values.reshape(1, COUNT),
        obs_precision.reshape(1, COUNT),
        probe.reshape(1, CH),
        state,
        background,
        conv_in,
        conv_out,
    )
    return grad, innov.reshape(COUNT)


def solution(mesh):
    in_specs = (
        P("lat", "lon", None),
        P("lat", "lon", None),
        P(),
        P(),
        P(),
        P(("lat", "lon"), None),
        P(None, ("lat", "lon")),
        P(None, ("lat", "lon")),
        P(("lat", "lon")),
        P(("lat", "lon")),
    )
    out_specs = (P("lat", "lon", None), P(("lat", "lon")))
    return jax.shard_map(
        on_device, mesh=mesh, in_specs=in_specs, out_specs=out_specs, check_vma=False
    )
```

```python
import functools

import jax
import jax.numpy as jnp
from jax import lax
from jax.experimental import pallas as pl
from jax.experimental.pallas import tpu as pltpu
from jax.sharding import PartitionSpec as P

MESH = pl.DeviceIdType.MESH
B16 = jnp.bfloat16
F32 = jnp.float32
I32 = jnp.int32
ROWS, COLS, CH = 8, 64, 256
PITCH = 80
LATS, LONS = 8, 16
TILES = LATS * LONS
COUNT = 2048
CAP = 32
NT = (((1,), (1,)), ((), ()))
SIDES = [(a, b) for a in (-1, 0, 1) for b in (-1, 0, 1) if (a, b) != (0, 0)]
CORNERS = [s for s in SIDES if s[1] != 0]


def hops(a, b):
    y, x, z = a // 2, b // 4, b % 4
    return min(y, 4 - y) + min(x, 4 - x) + min(z, 4 - z)


OTHERS = [(a, b) for a in range(LATS) for b in range(LONS) if (a, b) != (0, 0)]
OTHERS.sort(key=lambda o: -hops(*o))
FIRST = 0
ROUND = sorted(range(1, LONS), key=lambda b: -hops(0, b))
LINES = [o for o in OTHERS if 0 in o]


def iota(shape, dim):
    return lax.broadcasted_iota(I32, shape, dim)


def halves(x):
    high = x.astype(B16)
    return high, (x - high.astype(F32)).astype(B16)


def weighted(lhs, weights, flipped, j):
    if flipped:
        rhs = jnp.concatenate([weights[2 - i, 2 - j] for i in range(3)], axis=1)
        return lax.dot_general(lhs, rhs, NT, preferred_element_type=F32)
    rhs = jnp.concatenate([weights[i, j] for i in range(3)], axis=0)
    return jnp.dot(lhs, rhs, preferred_element_type=F32)


def windows(field, first, rows):
    count = rows * field.shape[1]
    return jnp.concatenate(
        [field[first + i : first + i + rows].reshape(count, CH) for i in range(3)], axis=1
    )


def products(field, weights, flipped, prod):
    lhs = windows(field, 0, ROWS)
    for j in range(3):
        out = weighted(lhs, weights, flipped, j)
        prod[j, 0, 0 : ROWS * PITCH] = out[:, :128]
        prod[j, 1, 0 : ROWS * PITCH] = out[:, 128:]


def put(prod, j, row, out):
    start = row * PITCH + 8
    prod[j, 0, start : start + COLS] = out[:, :128]
    prod[j, 1, start : start + COLS] = out[:, 128:]


def inner(field, weights, flipped, prod, j):
    out = weighted(windows(field, 2, 6), weights, flipped, j)
    for n in range(6):
        put(prod, j, 2 + n, out[n * COLS : (n + 1) * COLS])


def border(field, edge, weights, flipped, prod):
    sides = [
        jnp.concatenate([edge[b, 2 * i : 2 * i + 24] for i in range(3)], axis=1) for b in range(2)
    ]
    lhs = jnp.concatenate(
        [windows(field, 0, 2), windows(field, 8, 2), jnp.concatenate(sides, axis=0).astype(B16)],
        axis=0,
    )
    for j in range(3):
        out = weighted(lhs, weights, flipped, j)
        for n, row in enumerate((0, 1, 8, 9)):
            put(prod, j, row, out[n * COLS : (n + 1) * COLS])
        for b in range(2):
            for row in range(10):
                at = 4 * COLS + 24 * b + 2 * row
                start = row * PITCH + (72 if b else 6)
                prod[j, 0, start : start + 2] = out[at : at + 2, :128]
                prod[j, 1, start : start + 2] = out[at : at + 2, 128:]


def gathered(prod, start, count):
    parts = [
        prod[0, h, start : start + count]
        + prod[1, h, start + 1 : start + 1 + count]
        + prod[2, h, start + 2 : start + 2 + count]
        for h in range(2)
    ]
    return jnp.concatenate(parts, axis=1)


def pack(field, packs):
    sub = iota((16, CH), 0)
    west = jnp.zeros((16, CH), F32)
    east = jnp.zeros((16, CH), F32)
    for r in range(ROWS):
        here = (sub == 2 * r) | (sub == 2 * r + 1)
        x = field[2 + r, 0:16].astype(F32)
        west = jnp.where(here, x if r == 0 else pltpu.roll(x, 2 * r, 0), west)
        x = field[2 + r, 48:64].astype(F32)
        east = jnp.where(here, x if r == 7 else pltpu.roll(x, (2 * r - 14) % 16, 0), east)
    packs[0] = west.astype(B16)
    packs[1] = east.astype(B16)


def assemble(edge, parts, north, south):
    for n, (a, b) in enumerate(CORNERS):
        x = parts[n]
        side = 0 if b < 0 else 1
        if a < 0:
            edge[side, 0:4] = jnp.where(north, x[12:16], 0.0)
        elif a == 0:
            edge[side, 4:20] = x
        else:
            edge[side, 20:24] = jnp.where(south, x[0:4], 0.0)


def kernel(
    ids_in, taps_in, wts_in, vals_in, prec_in, probe_in, state, background, conv_in, conv_out,
    grad, innov,
    ids, taps, wts, vals, prec, probe, edge, sx, mx, ax, bg, w1, w2, slope, hx, mb, prod, dt, rank_s,
    packs, arrived, sbuf, r2, qbuf, q2, zs, zr,
    load_sem, row_sem, pack_sem, out_sem, back_sem, z_sem, own_sem, ready,
):
    la = lax.axis_index("lat")
    lo = lax.axis_index("lon")

    def near(a, b):
        return place(a, b)[1]

    def send(src, dst, sems, to):
        return pltpu.make_async_remote_copy(
            src_ref=src, dst_ref=dst, send_sem=sems[0], recv_sem=sems[1],
            device_id=to, device_id_type=MESH,
        )

    me = la * LONS + lo
    barrier = pltpu.get_barrier_semaphore()

    def place(a, b):
        to = (lax.bitwise_and(la + a, LATS - 1), lax.bitwise_and(lo + b, LONS - 1))
        return to[0] * LONS + to[1], to

    ins = [(ids_in, ids), (prec_in, prec), (taps_in, taps), (wts_in, wts), (vals_in, vals)]
    ins += [(state, sx.at[2:10]), (conv_in, w1), (conv_out, w2), (background, bg)]
    ins += [(probe_in, probe)]
    loads = [pltpu.make_async_copy(a, b, load_sem.at[n]) for n, (a, b) in enumerate(ins)]
    for c in loads[:5]:
        c.start()

    def greet(a, b):
        pl.semaphore_signal(barrier, inc=1, device_id=place(a, b)[1], device_id_type=MESH)

    def where(a, run, things):
        def body():
            for t in things:
                run(t)

        if a == 0:
            body()
        else:
            pl.when(la > 0 if a < 0 else la < LATS - 1)(body)

    for a in (-1, 1):
        where(a, lambda b: greet(a, b), (-1, 1))
    for a, b in LINES:
        greet(a, b)
    for c in loads[5:]:
        c.start()

    def each(copies, act):
        for a in (-1, 1, 0):
            where(a, act, [c for s, c in copies if s[0] == a])

    def give(src, dst, sems, row, b):
        to = (row, lax.bitwise_and(lo + b, LONS - 1))
        send(src.at[row * LONS + to[1]], dst.at[me], (sems.at[0], sems.at[1]), to).start()

    def depart(src, dst, sems, offsets):
        for a, b in offsets:
            t, to = place(a, b)
            send(src.at[t], dst.at[me], (sems.at[0], sems.at[1]), to).start()

    def stay(src, dst, n):
        own = pltpu.make_async_copy(src.at[me], dst.at[me], own_sem.at[n])
        own.start()
        return own

    def settle(src, dst, sems, which):
        some = slice(0, TILES - 1)
        pltpu.make_async_copy(src.at[some], dst.at[some], sems.at[which]).wait()

    def halo(field, which):
        copies = [
            ((-1, 0), send(field.at[2:4], field.at[10:12],
                           (row_sem.at[which, 0, 0], row_sem.at[which, 1, 1]), near(-1, 0))),
            ((1, 0), send(field.at[8:10], field.at[0:2],
                          (row_sem.at[which, 1, 0], row_sem.at[which, 0, 1]), near(1, 0))),
        ]
        for n, (a, b) in enumerate(CORNERS):
            m = CORNERS.index((-a, -b))
            copies.append(
                ((a, b), send(packs.at[which, 0 if b < 0 else 1], arrived.at[which, m],
                              (pack_sem.at[which, n, 0], pack_sem.at[which, m, 1]), near(a, b)))
            )
        return copies

    def arrive(copies):
        back = {s: c for s, c in copies}
        each([(s, back[-s[0], -s[1]]) for s in back], lambda c: c.wait_recv())

    def clear(field, low, high):
        @pl.when(la == 0)
        def _():
            field[0:low] = jnp.zeros((low,) + field.shape[1:], field.dtype)

        @pl.when(la == LATS - 1)
        def _():
            field[high:] = jnp.zeros((field.shape[0] - high,) + field.shape[1:], field.dtype)

    for c in loads[:5]:
        c.wait()
    upper = jnp.where(iota((128, 128), 0) <= iota((128, 128), 1), 1.0, 0.0).astype(B16)
    carry = jnp.zeros((128, 1), F32)
    ranks = []
    for c in range(16):
        hit = iota((128, 128), 0) == ids[0:1, c * 128 : (c + 1) * 128]
        one = jnp.where(hit, 1.0, 0.0).astype(B16)
        dt[:, c * 128 : (c + 1) * 128] = one
        run = jnp.dot(one, upper, preferred_element_type=F32) + carry
        ranks.append(jnp.sum(jnp.where(hit, run, 0.0), axis=0, keepdims=True) - 1.0)
        carry = run[:, 127:128]
    rank = jnp.concatenate(ranks, axis=1)
    rank_s[...] = rank
    acc = jnp.zeros((128, 512), F32)
    for c in range(8):
        cut = slice(c * 256, (c + 1) * 256)
        own = iota((CAP, 256), 0) == rank[:, cut].astype(I32)
        p = prec[0:1, cut]
        rows = [taps[k : k + 1, cut].astype(F32) - 256.0 for k in range(4)]
        scaled = [wts[k : k + 1, cut] * p for k in range(4)] + [vals[0:1, cut] * p]
        tops = [s.astype(B16).astype(F32) for s in scaled]
        lows = [s - t for s, t in zip(scaled, tops)]
        rows += tops[:4] + lows[:4] + [tops[4], lows[4]]
        spots = [jnp.where(own, r, 0.0).astype(B16) for r in rows]
        spots.append(jnp.zeros((64, 256), B16))
        x = jnp.concatenate(spots, axis=0)
        acc = acc + lax.dot_general(dt[:, cut], x, NT, preferred_element_type=F32)
    sbuf[:, 0, 0:128] = acc[:, 0:128]
    sbuf[:, 0, 128:256] = acc[:, 128:256] + acc[:, 256:384]
    sbuf[:, 0, 256:384] = acc[:, 384:512]

    loads[5].wait()
    pack(sx, packs.at[0])
    ends = jnp.where((la == 0) | (la == LATS - 1), 2, 4)
    pl.semaphore_wait(barrier, len(LINES) + ends)
    for a in range(1, LATS):
        pl.semaphore_signal(
            ready.at[la], inc=1, device_id=place(a, 0)[1], device_id_type=MESH
        )
    first = halo(sx, 0)
    each(first, lambda c: c.start())
    loads[6].wait()
    for j in range(3):
        inner(sx, w1, False, prod, j)
    for row in range(LATS):

        @pl.when(la != row)
        def _(row=row):
            pl.semaphore_wait(ready.at[row], 1)
            give(sbuf, r2, out_sem, row, 0)

        for b in ROUND:
            give(sbuf, r2, out_sem, row, b)
    kept = stay(sbuf, r2, 0)

    arrive(first)
    assemble(edge, [arrived[0, n].astype(F32) for n in range(6)], la > 0, la < LATS - 1)
    clear(sx, 2, 10)
    border(sx, edge, w1, False, prod)
    for r in range(10):
        b = gathered(prod, r * PITCH + 6, PITCH)
        sigma = 1.0 / (1.0 + jnp.exp(-b))
        slope[r] = sigma * (1.0 + b * (1.0 - sigma))
        hx[r] = (b * sigma).astype(B16)
    clear(hx, 1, 9)

    for c in loads[7:]:
        c.wait()
    products(hx, w2, False, prod)
    pr = probe[...]
    ph, plow = halves(pr)
    sub16 = iota((16, CH), 0)
    readout = jnp.where(
        sub16 == 0, ph.astype(F32), jnp.where(sub16 == 1, plow.astype(F32), 0.0)
    ).astype(B16)
    strips = []
    for r in range(ROWS):
        m = gathered(prod, r * PITCH, COLS) + sx[2 + r].astype(F32)
        high, low = halves(m)
        s = lax.dot_general(readout, high, NT, preferred_element_type=F32)
        t = lax.dot_general(readout, low, NT, preferred_element_type=F32)
        strips.append(s[0:1] + s[1:2] + t[0:1])
        d = m - bg[r].astype(F32)
        mb[r] = d
        mx[2 + r] = d.astype(B16)
    pack(mx, packs.at[1])
    second = halo(mx, 1)
    each(second, lambda c: c.start())
    tables = [
        jnp.broadcast_to(jnp.concatenate(strips[2 * q : 2 * q + 2], axis=1), (8, 128))
        for q in range(4)
    ]

    kept.wait()
    settle(sbuf, r2, out_sem, 1)
    cells, shares = [], []
    for t in range(TILES // 8):
        own = slice(8 * t, 8 * t + 8)
        cell = r2[own, 0, 0:128].astype(I32) + 256
        w = r2[own, 0, 128:256]
        lane = lax.bitwise_and(cell, 127)
        page = lax.shift_right_logical(cell, 7)
        got = jnp.zeros((8, 128), F32)
        for q in range(4):
            look = jnp.take_along_axis(tables[q], lane, axis=1, mode="promise_in_bounds")
            got = jnp.where(page == q, look, got)
        res = w * got - r2[own, 0, 256:384]
        res = res + pltpu.roll(res, 64, 1)
        res = res + pltpu.roll(res, 32, 1)
        qbuf[own, 0, :] = res
        cells.append(cell)
        shares.append(w * res)

    depart(qbuf, q2, back_sem, OTHERS[:FIRST])
    total = jnp.zeros((256, 256), F32)
    for t in range(0, TILES // 8, 2):
        cell = jnp.concatenate(cells[t : t + 2], axis=1)
        share = jnp.concatenate(shares[t : t + 2], axis=1)
        upper_cell = lax.shift_right_logical(cell, 5)
        lower_cell = lax.bitwise_and(cell, 31)
        top = share.astype(B16).astype(F32)
        low = share - top
        tops, lows, marks = [], [], []
        for g in range(8):
            hit = iota((16, 256), 0) == upper_cell[g : g + 1]
            tops.append(jnp.where(hit, top[g : g + 1], 0.0).astype(B16))
            lows.append(jnp.where(hit, low[g : g + 1], 0.0).astype(B16))
            marks.append(
                jnp.where(iota((32, 256), 0) == lower_cell[g : g + 1], 1.0, 0.0).astype(B16)
            )
        lhs = jnp.concatenate(tops + lows, axis=0)
        rhs = jnp.concatenate(marks, axis=0)
        total = total + lax.dot_general(lhs, rhs, NT, preferred_element_type=F32)
    total = total[0:128] + total[128:256]
    total = jnp.where(iota((128, 256), 0) // 16 == iota((128, 256), 1) // 32, total, 0.0)
    fold = total[0:16]
    for g in range(1, 8):
        fold = fold + total[g * 16 : (g + 1) * 16]
    fold = fold[:, 0:128] + fold[:, 128:256]
    fold = fold + pltpu.roll(fold, 64, 1)
    fold = fold + pltpu.roll(fold, 32, 1)
    zs[...] = fold
    out4 = []
    for n, (a, b) in enumerate(SIDES):
        m = SIDES.index((-a, -b))
        out4.append(((a, b), send(zs, zr.at[m], (z_sem.at[n, 0], z_sem.at[m, 1]), near(a, b))))
    each(out4, lambda c: c.start())

    depart(qbuf, q2, back_sem, OTHERS[FIRST:])
    kept = stay(qbuf, q2, 1)
    group = iota((16, 128), 1) // 32
    base = jnp.where(iota((128, CH), 0) // 64 == 0, ph.astype(F32), plow.astype(F32)).astype(B16)
    sub = iota((16, 128), 0)
    odd = lax.bitwise_and(sub, 1)
    spot = lax.bitwise_and(iota((16, 128), 1), 31)
    marks = [spot == sub, spot == sub + 16]

    def parted(z):
        top = z.astype(B16).astype(F32)
        return jnp.where(lax.bitwise_and(group, 1) == 0, top, z - top)

    def outer(blocks):
        lhs = jnp.concatenate(
            [
                jnp.where(marks[c % 2], z[2 * r + c // 2 : 2 * r + c // 2 + 1], 0.0).astype(B16)
                for z, r, c in blocks
            ],
            axis=0,
        )
        return jnp.dot(lhs, base, preferred_element_type=F32)

    center = parted(fold)
    for r in range(ROWS):
        local = outer([(center, r, c) for c in range(4)])
        ax[2 + r] = (mb[r] + local).astype(B16)
    for j in range(3):
        inner(ax, w2, True, prod, j)

    arrive(second)
    arrive(out4)
    around = {s: parted(zr[n]) for n, s in enumerate(SIDES)}
    for a, rows in ((-1, (6, 7)), (1, (0, 1))):
        piece = outer([(around[a, 0], r, c) for r in rows for c in range(4)])
        for n, r in enumerate(rows):
            row = r + 2 + a * 8
            ax[row] = (mx[row].astype(F32) + piece[n * 64 : (n + 1) * 64]).astype(B16)
    strips = []
    for a, b in CORNERS:
        z = around[a, b]
        if b < 0:
            z = jnp.where(odd == 1, z, pltpu.roll(z, 15, 0))
            hit = spot == odd + 30
        else:
            z = jnp.where(odd == 0, z, pltpu.roll(z, 1, 0))
            hit = spot == odd
        strips.append(jnp.where(hit, z, 0.0).astype(B16))
    piece = jnp.dot(jnp.concatenate(strips, axis=0), base, preferred_element_type=F32)
    parts = [
        (arrived[1, n].astype(F32) + piece[16 * n : 16 * n + 16]).astype(B16).astype(F32)
        for n in range(6)
    ]
    assemble(edge, parts, la > 0, la < LATS - 1)
    clear(ax, 2, 10)

    border(ax, edge, w2, True, prod)
    for r in range(10):
        hx[r] = (gathered(prod, r * PITCH + 6, PITCH) * slope[r]).astype(B16)
    clear(hx, 1, 9)
    products(hx, w1, True, prod)
    for r in range(ROWS):
        y = gathered(prod, r * PITCH, COLS) + ax[2 + r].astype(F32)
        grad[r] = y.astype(B16)

    kept.wait()
    settle(qbuf, q2, back_sem, 1)
    back = q2[:, 0, :].T[0:CAP]
    one = back.astype(B16)
    rest = back - one.astype(F32)
    two = rest.astype(B16)
    three = (rest - two.astype(F32)).astype(B16)
    lhs = jnp.concatenate([one, two, three], axis=0)
    for c in range(4):
        cut = slice(c * 512, (c + 1) * 512)
        got = jnp.dot(lhs, dt[:, cut], preferred_element_type=F32)
        got = got[0:32] + got[32:64] + got[64:96]
        own = iota((CAP, 512), 0) == rank_s[0:1, cut].astype(I32)
        innov[0:1, cut] = jnp.sum(jnp.where(own, got, 0.0), axis=0, keepdims=True)

    each(first + second + out4, lambda c: c.wait_send())
    settle(sbuf, r2, out_sem, 0)
    settle(qbuf, q2, back_sem, 0)


def on_device(
    state, background, conv_in, conv_out, probe,
    tile_ids, cell_taps, tap_weights, obs_values, obs_precision,
):
    vmem = pl.BlockSpec(memory_space=pltpu.VMEM)
    hbm = pl.BlockSpec(memory_space=pl.ANY)
    dma = pltpu.SemaphoreType.DMA
    wide = pltpu.VMEM((12, COLS, CH), B16)
    kshape = (3, 3, CH, CH)
    grad, innov = pl.pallas_call(
        kernel,
        out_shape=(
            pltpu.VMEM((ROWS, COLS, CH), B16),
            pltpu.VMEM((1, COUNT), F32),
        ),
        in_specs=[hbm] * 10,
        out_specs=(vmem, vmem),
        scratch_shapes=[
            pltpu.VMEM((1, COUNT), I32),
            pltpu.VMEM((4, COUNT), I32),
            pltpu.VMEM((4, COUNT), F32),
            pltpu.VMEM((1, COUNT), F32),
            pltpu.VMEM((1, COUNT), F32),
            pltpu.VMEM((1, CH), F32),
            pltpu.VMEM((2, 32, CH), F32),
            wide, wide, wide,
            pltpu.VMEM((ROWS, COLS, CH), B16),
            pltpu.VMEM(kshape, B16),
            pltpu.VMEM(kshape, B16),
            pltpu.VMEM((10, PITCH, CH), F32),
            pltpu.VMEM((10, PITCH, CH), B16),
            pltpu.VMEM((ROWS, COLS, CH), F32),
            pltpu.VMEM((3, 2, 10 * PITCH + 64, 128), F32),
            pltpu.VMEM((TILES, COUNT), B16),
            pltpu.VMEM((1, COUNT), F32),
            pltpu.VMEM((2, 2, 16, CH), B16),
            pltpu.VMEM((2, len(CORNERS), 16, CH), B16),
            pltpu.VMEM((TILES, 1, 384), F32),
            pltpu.VMEM((TILES, 1, 384), F32),
            pltpu.VMEM((TILES, 1, 128), F32),
            pltpu.VMEM((TILES, 1, 128), F32),
            pltpu.VMEM((16, 128), F32),
            pltpu.VMEM((len(SIDES), 16, 128), F32),
            dma((10,)),
            dma((2, 2, 2)),
            dma((2, len(CORNERS), 2)),
            dma((2,)),
            dma((2,)),
            dma((len(SIDES), 2)),
            dma((2,)),
            pltpu.SemaphoreType.REGULAR((LATS,)),
        ],
        compiler_params=pltpu.CompilerParams(
            collective_id=0, has_side_effects=True, vmem_limit_bytes=56 * 2**20
        ),
    )(
        tile_ids.reshape(1, COUNT),
        cell_taps,
        tap_weights,
        obs_values.reshape(1, COUNT),
        obs_precision.reshape(1, COUNT),
        probe.reshape(1, CH),
        state,
        background,
        conv_in,
        conv_out,
    )
    return grad, innov.reshape(COUNT)


def solution(mesh):
    in_specs = (
        P("lat", "lon", None),
        P("lat", "lon", None),
        P(),
        P(),
        P(),
        P(("lat", "lon"), None),
        P(None, ("lat", "lon")),
        P(None, ("lat", "lon")),
        P(("lat", "lon")),
        P(("lat", "lon")),
    )
    out_specs = (P("lat", "lon", None), P(("lat", "lon")))
    return jax.shard_map(
        on_device, mesh=mesh, in_specs=in_specs, out_specs=out_specs, check_vma=False
    )
```

```python
import functools

import jax
import jax.numpy as jnp
from jax import lax
from jax.experimental import pallas as pl
from jax.experimental.pallas import tpu as pltpu
from jax.sharding import PartitionSpec as P

MESH = pl.DeviceIdType.MESH
B16 = jnp.bfloat16
F32 = jnp.float32
I32 = jnp.int32
ROWS, COLS, CH = 8, 64, 256
PITCH = 80
LATS, LONS = 8, 16
TILES = LATS * LONS
COUNT = 2048
CAP = 32
NT = (((1,), (1,)), ((), ()))
SIDES = [(a, b) for a in (-1, 0, 1) for b in (-1, 0, 1) if (a, b) != (0, 0)]
CORNERS = [s for s in SIDES if s[1] != 0]


def hops(a, b):
    y, x, z = a // 2, b // 4, b % 4
    return min(y, 4 - y) + min(x, 4 - x) + min(z, 4 - z)


OTHERS = [(a, b) for a in range(LATS) for b in range(LONS) if (a, b) != (0, 0)]
OTHERS.sort(key=lambda o: -hops(*o))
FIRST = 0
ROUND = sorted(range(1, LONS), key=lambda b: -hops(0, b))
LINES = [o for o in OTHERS if 0 in o]


def iota(shape, dim):
    return lax.broadcasted_iota(I32, shape, dim)


def halves(x):
    high = x.astype(B16)
    return high, (x - high.astype(F32)).astype(B16)


def weighted(lhs, weights, flipped, j):
    if flipped:
        rhs = jnp.concatenate([weights[2 - i, 2 - j] for i in range(3)], axis=1)
        return lax.dot_general(lhs, rhs, NT, preferred_element_type=F32)
    rhs = jnp.concatenate([weights[i, j] for i in range(3)], axis=0)
    return jnp.dot(lhs, rhs, preferred_element_type=F32)


def windows(field, first, rows):
    count = rows * field.shape[1]
    return jnp.concatenate(
        [field[first + i : first + i + rows].reshape(count, CH) for i in range(3)], axis=1
    )


def products(field, sides, weights, flipped, prod):
    ends = [jnp.concatenate([sides[b, i : i + ROWS] for i in range(3)], axis=1) for b in range(2)]
    lhs = jnp.concatenate(
        [windows(field, 0, ROWS), jnp.concatenate(ends, axis=0).astype(B16)], axis=0
    )
    for j in range(3):
        out = weighted(lhs, weights, flipped, j)
        for row in range(ROWS):
            put(prod, j, row, out[row * COLS : (row + 1) * COLS])
        at = ROWS * COLS
        place_column(prod, j, 7, out[at : at + ROWS])
        place_column(prod, j, 72, out[at + ROWS : at + 2 * ROWS])


def place_column(prod, j, start, out):
    rows = pl.ds(start, out.shape[0], stride=PITCH)
    prod[j, 0, rows, :] = out[:, :128]
    prod[j, 1, rows, :] = out[:, 128:]


def put(prod, j, row, out):
    start = row * PITCH + 8
    prod[j, 0, start : start + COLS] = out[:, :128]
    prod[j, 1, start : start + COLS] = out[:, 128:]


def inner(field, weights, flipped, prod, j):
    out = weighted(windows(field, 2, 6), weights, flipped, j)
    for n in range(6):
        put(prod, j, 2 + n, out[n * COLS : (n + 1) * COLS])


def border(field, edge, weights, flipped, prod):
    sides = [
        jnp.concatenate(
            [edge[b, h, pl.ds(2 * i + c, 16, stride=2), :] for i in range(3) for h in range(2)],
            axis=1,
        )
        for b in range(2)
        for c in range(2)
    ]
    lhs = jnp.concatenate(
        [windows(field, 0, 2), windows(field, 8, 2), jnp.concatenate(sides, axis=0).astype(B16)],
        axis=0,
    )
    for j in range(3):
        out = weighted(lhs, weights, flipped, j)
        for n, row in enumerate((0, 1, 8, 9)):
            put(prod, j, row, out[n * COLS : (n + 1) * COLS])
        for n, start in enumerate((6, 7, 72, 73)):
            at = 4 * COLS + 16 * n
            place_column(prod, j, start, out[at : at + 10])


def columns(prod, start):
    parts = [
        prod[0, h, pl.ds(start, 10, stride=PITCH), :]
        + prod[1, h, pl.ds(start + 1, 10, stride=PITCH), :]
        + prod[2, h, pl.ds(start + 2, 10, stride=PITCH), :]
        for h in range(2)
    ]
    return jnp.concatenate(parts, axis=1)


def silu_parts(x):
    sigma = 1.0 / (1.0 + jnp.exp(-x))
    return x * sigma, sigma * (1.0 + x * (1.0 - sigma))


def gathered(prod, start, count):
    parts = [
        prod[0, h, start : start + count]
        + prod[1, h, start + 1 : start + 1 + count]
        + prod[2, h, start + 2 : start + 2 + count]
        for h in range(2)
    ]
    return jnp.concatenate(parts, axis=1)


def pack(field, packs):
    sub = iota((16, CH), 0)
    west = jnp.zeros((16, CH), F32)
    east = jnp.zeros((16, CH), F32)
    for r in range(ROWS):
        here = (sub == 2 * r) | (sub == 2 * r + 1)
        x = field[2 + r, 0:16].astype(F32)
        west = jnp.where(here, x if r == 0 else pltpu.roll(x, 2 * r, 0), west)
        x = field[2 + r, 48:64].astype(F32)
        east = jnp.where(here, x if r == 7 else pltpu.roll(x, (2 * r - 14) % 16, 0), east)
    packs[0] = west.astype(B16)
    packs[1] = east.astype(B16)


def assemble(edge, parts, north, south):
    for n, (a, b) in enumerate(CORNERS):
        x = parts[n]
        side = 0 if b < 0 else 1
        for h in range(2):
            y = x[:, h * 128 : (h + 1) * 128]
            if a < 0:
                edge[side, h, 0:4] = jnp.where(north, y[12:16], 0.0)
            elif a == 0:
                edge[side, h, 4:20] = y
            else:
                edge[side, h, 20:24] = jnp.where(south, y[0:4], 0.0)


def kernel(
    ids_in, taps_in, wts_in, vals_in, prec_in, probe_in, state, background, conv_in, conv_out,
    grad, innov,
    ids, taps, wts, vals, prec, probe, edge, sx, mx, ax, bg, w1, w2, slope, slope_side, hx, side, mb, prod, dt, rank_s,
    packs, arrived, sbuf, r2, qbuf, q2, zs, zr,
    load_sem, row_sem, pack_sem, out_sem, back_sem, z_sem, own_sem, ready,
):
    la = lax.axis_index("lat")
    lo = lax.axis_index("lon")

    def near(a, b):
        return place(a, b)[1]

    def send(src, dst, sems, to):
        return pltpu.make_async_remote_copy(
            src_ref=src, dst_ref=dst, send_sem=sems[0], recv_sem=sems[1],
            device_id=to, device_id_type=MESH,
        )

    me = la * LONS + lo
    barrier = pltpu.get_barrier_semaphore()

    def place(a, b):
        to = (lax.bitwise_and(la + a, LATS - 1), lax.bitwise_and(lo + b, LONS - 1))
        return to[0] * LONS + to[1], to

    ins = [(ids_in, ids), (prec_in, prec), (taps_in, taps), (wts_in, wts), (vals_in, vals)]
    ins += [(state, sx.at[2:10]), (conv_in, w1), (conv_out, w2), (background, bg)]
    ins += [(probe_in, probe)]
    loads = [pltpu.make_async_copy(a, b, load_sem.at[n]) for n, (a, b) in enumerate(ins)]
    for c in loads[:5]:
        c.start()

    def greet(a, b):
        pl.semaphore_signal(barrier, inc=1, device_id=place(a, b)[1], device_id_type=MESH)

    def where(a, run, things):
        def body():
            for t in things:
                run(t)

        if a == 0:
            body()
        else:
            pl.when(la > 0 if a < 0 else la < LATS - 1)(body)

    for a in (-1, 1):
        where(a, lambda b: greet(a, b), (-1, 1))
    for a, b in LINES:
        greet(a, b)
    for c in loads[5:]:
        c.start()

    def each(copies, act):
        for a in (-1, 1, 0):
            where(a, act, [c for s, c in copies if s[0] == a])

    def give(src, dst, sems, row, b):
        to = (row, lax.bitwise_and(lo + b, LONS - 1))
        send(src.at[row * LONS + to[1]], dst.at[me], (sems.at[0], sems.at[1]), to).start()

    def depart(src, dst, sems, offsets):
        for a, b in offsets:
            t, to = place(a, b)
            send(src.at[t], dst.at[me], (sems.at[0], sems.at[1]), to).start()

    def stay(src, dst, n):
        own = pltpu.make_async_copy(src.at[me], dst.at[me], own_sem.at[n])
        own.start()
        return own

    def settle(src, dst, sems, which):
        some = slice(0, TILES - 1)
        pltpu.make_async_copy(src.at[some], dst.at[some], sems.at[which]).wait()

    def halo(field, which):
        copies = [
            ((-1, 0), send(field.at[2:4], field.at[10:12],
                           (row_sem.at[which, 0, 0], row_sem.at[which, 1, 1]), near(-1, 0))),
            ((1, 0), send(field.at[8:10], field.at[0:2],
                          (row_sem.at[which, 1, 0], row_sem.at[which, 0, 1]), near(1, 0))),
        ]
        for n, (a, b) in enumerate(CORNERS):
            m = CORNERS.index((-a, -b))
            copies.append(
                ((a, b), send(packs.at[which, 0 if b < 0 else 1], arrived.at[which, m],
                              (pack_sem.at[which, n, 0], pack_sem.at[which, m, 1]), near(a, b)))
            )
        return copies

    def arrive(copies):
        back = {s: c for s, c in copies}
        each([(s, back[-s[0], -s[1]]) for s in back], lambda c: c.wait_recv())

    def clear(field, low, high):
        @pl.when(la == 0)
        def _():
            field[0:low] = jnp.zeros((low,) + field.shape[1:], field.dtype)

        @pl.when(la == LATS - 1)
        def _():
            field[high:] = jnp.zeros((field.shape[0] - high,) + field.shape[1:], field.dtype)

    for c in loads[:5]:
        c.wait()
    upper = jnp.where(iota((128, 128), 0) <= iota((128, 128), 1), 1.0, 0.0).astype(B16)
    carry = jnp.zeros((128, 1), F32)
    ranks = []
    for c in range(16):
        hit = iota((128, 128), 0) == ids[0:1, c * 128 : (c + 1) * 128]
        one = jnp.where(hit, 1.0, 0.0).astype(B16)
        dt[:, c * 128 : (c + 1) * 128] = one
        run = jnp.dot(one, upper, preferred_element_type=F32) + carry
        ranks.append(jnp.sum(jnp.where(hit, run, 0.0), axis=0, keepdims=True) - 1.0)
        carry = run[:, 127:128]
    rank = jnp.concatenate(ranks, axis=1)
    rank_s[...] = rank
    acc = jnp.zeros((128, 512), F32)
    for c in range(8):
        cut = slice(c * 256, (c + 1) * 256)
        own = iota((CAP, 256), 0) == rank[:, cut].astype(I32)
        p = prec[0:1, cut]
        rows = [taps[k : k + 1, cut].astype(F32) - 256.0 for k in range(4)]
        scaled = [wts[k : k + 1, cut] * p for k in range(4)] + [vals[0:1, cut] * p]
        tops = [s.astype(B16).astype(F32) for s in scaled]
        lows = [s - t for s, t in zip(scaled, tops)]
        rows += tops[:4] + lows[:4] + [tops[4], lows[4]]
        spots = [jnp.where(own, r, 0.0).astype(B16) for r in rows]
        spots.append(jnp.zeros((64, 256), B16))
        x = jnp.concatenate(spots, axis=0)
        acc = acc + lax.dot_general(dt[:, cut], x, NT, preferred_element_type=F32)
    sbuf[:, 0, 0:128] = acc[:, 0:128]
    sbuf[:, 0, 128:256] = acc[:, 128:256] + acc[:, 256:384]
    sbuf[:, 0, 256:384] = acc[:, 384:512]

    loads[5].wait()
    pack(sx, packs.at[0])
    ends = jnp.where((la == 0) | (la == LATS - 1), 2, 4)
    pl.semaphore_wait(barrier, len(LINES) + ends)
    for a in range(1, LATS):
        pl.semaphore_signal(
            ready.at[la], inc=1, device_id=place(a, 0)[1], device_id_type=MESH
        )
    first = halo(sx, 0)
    each(first, lambda c: c.start())
    loads[6].wait()
    for j in range(3):
        inner(sx, w1, False, prod, j)
    for row in range(LATS):

        @pl.when(la != row)
        def _(row=row):
            pl.semaphore_wait(ready.at[row], 1)
            give(sbuf, r2, out_sem, row, 0)

        for b in ROUND:
            give(sbuf, r2, out_sem, row, b)
    kept = stay(sbuf, r2, 0)

    arrive(first)
    assemble(edge, [arrived[0, n].astype(F32) for n in range(6)], la > 0, la < LATS - 1)
    clear(sx, 2, 10)
    border(sx, edge, w1, False, prod)
    for r in range(10):
        y, slope[r] = silu_parts(gathered(prod, r * PITCH + 7, COLS))
        hx[r] = y.astype(B16)
    row10 = iota((10, CH), 0)
    outside = ((row10 == 0) & (la == 0)) | ((row10 == 9) & (la == LATS - 1))
    for b in range(2):
        y, slope_side[b, 0:10] = silu_parts(columns(prod, 71 * b + 6 * (1 - b)))
        side[b, 0:10] = jnp.where(outside, 0.0, y)
    clear(hx, 1, 9)

    for c in loads[7:]:
        c.wait()
    products(hx, side, w2, False, prod)
    pr = probe[...]
    ph, plow = halves(pr)
    sub16 = iota((16, CH), 0)
    readout = jnp.where(
        sub16 == 0, ph.astype(F32), jnp.where(sub16 == 1, plow.astype(F32), 0.0)
    ).astype(B16)
    highs, lows = [], []
    for r in range(ROWS):
        m = gathered(prod, r * PITCH + 7, COLS) + sx[2 + r].astype(F32)
        high, low = halves(m)
        highs.append(high)
        lows.append(low)
        d = m - bg[r].astype(F32)
        mb[r] = d
        mx[2 + r] = d.astype(B16)
    pack(mx, packs.at[1])
    second = halo(mx, 1)
    each(second, lambda c: c.start())
    s = lax.dot_general(readout, jnp.concatenate(highs, axis=0), NT, preferred_element_type=F32)
    t = lax.dot_general(readout, jnp.concatenate(lows, axis=0), NT, preferred_element_type=F32)
    scalar = s[0:1] + s[1:2] + t[0:1]
    tables = [jnp.broadcast_to(scalar[:, q * 128 : (q + 1) * 128], (8, 128)) for q in range(4)]

    kept.wait()
    settle(sbuf, r2, out_sem, 1)
    cells, shares = [], []
    for t in range(TILES // 8):
        own = slice(8 * t, 8 * t + 8)
        cell = r2[own, 0, 0:128].astype(I32) + 256
        w = r2[own, 0, 128:256]
        lane = lax.bitwise_and(cell, 127)
        page = lax.shift_right_logical(cell, 7)
        got = jnp.zeros((8, 128), F32)
        for q in range(4):
            look = jnp.take_along_axis(tables[q], lane, axis=1, mode="promise_in_bounds")
            got = jnp.where(page == q, look, got)
        res = w * got - r2[own, 0, 256:384]
        res = res + pltpu.roll(res, 64, 1)
        res = res + pltpu.roll(res, 32, 1)
        qbuf[own, 0, :] = res
        cells.append(cell)
        shares.append(w * res)

    depart(qbuf, q2, back_sem, OTHERS[:FIRST])
    total = jnp.zeros((128, 256), F32)
    for t in range(0, TILES // 8, 2):
        cell = jnp.concatenate(cells[t : t + 2], axis=1)
        share = jnp.concatenate(shares[t : t + 2], axis=1)
        upper_cell = lax.shift_right_logical(cell, 5)
        lower_cell = lax.bitwise_and(cell, 31)
        tops, marks = [], []
        for g in range(8):
            hit = iota((16, 256), 0) == upper_cell[g : g + 1]
            tops.append(jnp.where(hit, share[g : g + 1], 0.0).astype(B16))
            marks.append(
                jnp.where(iota((32, 256), 0) == lower_cell[g : g + 1], 1.0, 0.0).astype(B16)
            )
        lhs = jnp.concatenate(tops, axis=0)
        rhs = jnp.concatenate(marks, axis=0)
        total = total + lax.dot_general(lhs, rhs, NT, preferred_element_type=F32)
    total = jnp.where(iota((128, 256), 0) // 16 == iota((128, 256), 1) // 32, total, 0.0)
    fold = total[0:16]
    for g in range(1, 8):
        fold = fold + total[g * 16 : (g + 1) * 16]
    fold = fold[:, 0:128] + fold[:, 128:256]
    fold = fold + pltpu.roll(fold, 64, 1)
    fold = fold + pltpu.roll(fold, 32, 1)
    zs[...] = fold
    out4 = []
    for n, (a, b) in enumerate(SIDES):
        m = SIDES.index((-a, -b))
        out4.append(((a, b), send(zs, zr.at[m], (z_sem.at[n, 0], z_sem.at[m, 1]), near(a, b))))
    each(out4, lambda c: c.start())

    depart(qbuf, q2, back_sem, OTHERS[FIRST:])
    kept = stay(qbuf, q2, 1)
    group = iota((16, 128), 1) // 32
    base = jnp.where(iota((128, CH), 0) // 64 == 0, ph.astype(F32), plow.astype(F32)).astype(B16)
    sub = iota((16, 128), 0)
    odd = lax.bitwise_and(sub, 1)
    spot = lax.bitwise_and(iota((16, 128), 1), 31)
    marks = [spot == sub, spot == sub + 16]

    def parted(z):
        top = z.astype(B16).astype(F32)
        return jnp.where(lax.bitwise_and(group, 1) == 0, top, z - top)

    def outer(blocks):
        lhs = jnp.concatenate(
            [
                jnp.where(marks[c % 2], z[2 * r + c // 2 : 2 * r + c // 2 + 1], 0.0).astype(B16)
                for z, r, c in blocks
            ],
            axis=0,
        )
        return jnp.dot(lhs, base, preferred_element_type=F32)

    center = parted(fold)
    for r in range(ROWS):
        local = outer([(center, r, c) for c in range(4)])
        ax[2 + r] = (mb[r] + local).astype(B16)
    for j in range(3):
        inner(ax, w2, True, prod, j)

    arrive(second)
    arrive(out4)
    around = {s: parted(zr[n]) for n, s in enumerate(SIDES)}
    for a, rows in ((-1, (6, 7)), (1, (0, 1))):
        piece = outer([(around[a, 0], r, c) for r in rows for c in range(4)])
        for n, r in enumerate(rows):
            row = r + 2 + a * 8
            ax[row] = (mx[row].astype(F32) + piece[n * 64 : (n + 1) * 64]).astype(B16)
    strips = []
    for a, b in CORNERS:
        z = around[a, b]
        if b < 0:
            z = jnp.where(odd == 1, z, pltpu.roll(z, 15, 0))
            hit = spot == odd + 30
        else:
            z = jnp.where(odd == 0, z, pltpu.roll(z, 1, 0))
            hit = spot == odd
        strips.append(jnp.where(hit, z, 0.0).astype(B16))
    piece = jnp.dot(jnp.concatenate(strips, axis=0), base, preferred_element_type=F32)
    parts = [
        (arrived[1, n].astype(F32) + piece[16 * n : 16 * n + 16]).astype(B16).astype(F32)
        for n in range(6)
    ]
    assemble(edge, parts, la > 0, la < LATS - 1)
    clear(ax, 2, 10)

    border(ax, edge, w2, True, prod)
    for r in range(10):
        hx[r] = (gathered(prod, r * PITCH + 7, COLS) * slope[r]).astype(B16)
    for b in range(2):
        y = columns(prod, 71 * b + 6 * (1 - b)) * slope_side[b, 0:10]
        side[b, 0:10] = jnp.where(outside, 0.0, y)
    clear(hx, 1, 9)
    products(hx, side, w1, True, prod)
    for r in range(ROWS):
        y = gathered(prod, r * PITCH + 7, COLS) + ax[2 + r].astype(F32)
        grad[r] = y.astype(B16)

    kept.wait()
    settle(qbuf, q2, back_sem, 1)
    back = q2[:, 0, :].T[0:CAP]
    one = back.astype(B16)
    rest = back - one.astype(F32)
    two = rest.astype(B16)
    three = (rest - two.astype(F32)).astype(B16)
    lhs = jnp.concatenate([one, two, three], axis=0)
    for c in range(4):
        cut = slice(c * 512, (c + 1) * 512)
        got = jnp.dot(lhs, dt[:, cut], preferred_element_type=F32)
        got = got[0:32] + got[32:64] + got[64:96]
        own = iota((CAP, 512), 0) == rank_s[0:1, cut].astype(I32)
        innov[0:1, cut] = jnp.sum(jnp.where(own, got, 0.0), axis=0, keepdims=True)

    each(first + second + out4, lambda c: c.wait_send())
    settle(sbuf, r2, out_sem, 0)
    settle(qbuf, q2, back_sem, 0)


def on_device(
    state, background, conv_in, conv_out, probe,
    tile_ids, cell_taps, tap_weights, obs_values, obs_precision,
):
    vmem = pl.BlockSpec(memory_space=pltpu.VMEM)
    hbm = pl.BlockSpec(memory_space=pl.ANY)
    dma = pltpu.SemaphoreType.DMA
    wide = pltpu.VMEM((12, COLS, CH), B16)
    kshape = (3, 3, CH, CH)
    grad, innov = pl.pallas_call(
        kernel,
        out_shape=(
            pltpu.VMEM((ROWS, COLS, CH), B16),
            pltpu.VMEM((1, COUNT), F32),
        ),
        in_specs=[hbm] * 10,
        out_specs=(vmem, vmem),
        scratch_shapes=[
            pltpu.VMEM((1, COUNT), I32),
            pltpu.VMEM((4, COUNT), I32),
            pltpu.VMEM((4, COUNT), F32),
            pltpu.VMEM((1, COUNT), F32),
            pltpu.VMEM((1, COUNT), F32),
            pltpu.VMEM((1, CH), F32),
            pltpu.VMEM((2, 2, 40, 128), F32),
            wide, wide, wide,
            pltpu.VMEM((ROWS, COLS, CH), B16),
            pltpu.VMEM(kshape, B16),
            pltpu.VMEM(kshape, B16),
            pltpu.VMEM((10, COLS, CH), F32),
            pltpu.VMEM((2, 16, CH), F32),
            pltpu.VMEM((10, COLS, CH), B16),
            pltpu.VMEM((2, 16, CH), F32),
            pltpu.VMEM((ROWS, COLS, CH), F32),
            pltpu.VMEM((3, 2, 10 * PITCH + 64, 128), F32),
            pltpu.VMEM((TILES, COUNT), B16),
            pltpu.VMEM((1, COUNT), F32),
            pltpu.VMEM((2, 2, 16, CH), B16),
            pltpu.VMEM((2, len(CORNERS), 16, CH), B16),
            pltpu.VMEM((TILES, 1, 384), F32),
            pltpu.VMEM((TILES, 1, 384), F32),
            pltpu.VMEM((TILES, 1, 128), F32),
            pltpu.VMEM((TILES, 1, 128), F32),
            pltpu.VMEM((16, 128), F32),
            pltpu.VMEM((len(SIDES), 16, 128), F32),
            dma((10,)),
            dma((2, 2, 2)),
            dma((2, len(CORNERS), 2)),
            dma((2,)),
            dma((2,)),
            dma((len(SIDES), 2)),
            dma((2,)),
            pltpu.SemaphoreType.REGULAR((LATS,)),
        ],
        compiler_params=pltpu.CompilerParams(
            collective_id=0, has_side_effects=True, vmem_limit_bytes=56 * 2**20
        ),
    )(
        tile_ids.reshape(1, COUNT),
        cell_taps,
        tap_weights,
        obs_values.reshape(1, COUNT),
        obs_precision.reshape(1, COUNT),
        probe.reshape(1, CH),
        state,
        background,
        conv_in,
        conv_out,
    )
    return grad, innov.reshape(COUNT)


def solution(mesh):
    in_specs = (
        P("lat", "lon", None),
        P("lat", "lon", None),
        P(),
        P(),
        P(),
        P(("lat", "lon"), None),
        P(None, ("lat", "lon")),
        P(None, ("lat", "lon")),
        P(("lat", "lon")),
        P(("lat", "lon")),
    )
    out_specs = (P("lat", "lon", None), P(("lat", "lon")))
    return jax.shard_map(
        on_device, mesh=mesh, in_specs=in_specs, out_specs=out_specs, check_vma=False
    )
```

```python
import functools

import jax
import jax.numpy as jnp
from jax import lax
from jax.experimental import pallas as pl
from jax.experimental.pallas import tpu as pltpu
from jax.sharding import PartitionSpec as P

MESH = pl.DeviceIdType.MESH
B16 = jnp.bfloat16
F32 = jnp.float32
I32 = jnp.int32
ROWS, COLS, CH = 8, 64, 256
PITCH = 80
LATS, LONS = 8, 16
TILES = LATS * LONS
COUNT = 2048
CAP = 32
NT = (((1,), (1,)), ((), ()))
SIDES = [(a, b) for a in (-1, 0, 1) for b in (-1, 0, 1) if (a, b) != (0, 0)]
CORNERS = [s for s in SIDES if s[1] != 0]


def hops(a, b):
    y, x, z = a // 2, b // 4, b % 4
    return min(y, 4 - y) + min(x, 4 - x) + min(z, 4 - z)


OTHERS = [(a, b) for a in range(LATS) for b in range(LONS) if (a, b) != (0, 0)]
OTHERS.sort(key=lambda o: -hops(*o))
ROUND = sorted(range(1, LONS), key=lambda b: -hops(0, b))
LINES = [o for o in OTHERS if 0 in o]


def iota(shape, dim):
    return lax.broadcasted_iota(I32, shape, dim)


def halves(x):
    high = x.astype(B16)
    return high, (x - high.astype(F32)).astype(B16)


def weighted(lhs, weights, flipped, j):
    if flipped:
        rhs = jnp.concatenate([weights[2 - i, 2 - j] for i in range(3)], axis=1)
        return lax.dot_general(lhs, rhs, NT, preferred_element_type=F32)
    rhs = jnp.concatenate([weights[i, j] for i in range(3)], axis=0)
    return jnp.dot(lhs, rhs, preferred_element_type=F32)


def windows(field, first, rows):
    count = rows * field.shape[1]
    return jnp.concatenate(
        [field[first + i : first + i + rows].reshape(count, CH) for i in range(3)], axis=1
    )


def products(field, sides, weights, flipped, prod):
    ends = [jnp.concatenate([sides[b, i : i + ROWS] for i in range(3)], axis=1) for b in range(2)]
    lhs = jnp.concatenate(
        [windows(field, 0, ROWS), jnp.concatenate(ends, axis=0).astype(B16)], axis=0
    )
    for j in range(3):
        out = weighted(lhs, weights, flipped, j)
        for row in range(ROWS):
            put(prod, j, row, out[row * COLS : (row + 1) * COLS])
        at = ROWS * COLS
        place_column(prod, j, 7, out[at : at + ROWS])
        place_column(prod, j, 72, out[at + ROWS : at + 2 * ROWS])


def place_column(prod, j, start, out):
    rows = pl.ds(start, out.shape[0], stride=PITCH)
    prod[j, 0, rows, :] = out[:, :128]
    prod[j, 1, rows, :] = out[:, 128:]


def put(prod, j, row, out):
    start = row * PITCH + 8
    prod[j, 0, start : start + COLS] = out[:, :128]
    prod[j, 1, start : start + COLS] = out[:, 128:]


def inner(field, weights, flipped, prod, j):
    out = weighted(windows(field, 2, 6), weights, flipped, j)
    for n in range(6):
        put(prod, j, 2 + n, out[n * COLS : (n + 1) * COLS])


def border(field, edge, weights, flipped, prod):
    sides = [
        jnp.concatenate(
            [edge[b, h, pl.ds(2 * i + c, 16, stride=2), :] for i in range(3) for h in range(2)],
            axis=1,
        )
        for b in range(2)
        for c in range(2)
    ]
    lhs = jnp.concatenate(
        [windows(field, 0, 2), windows(field, 8, 2), jnp.concatenate(sides, axis=0).astype(B16)],
        axis=0,
    )
    for j in range(3):
        out = weighted(lhs, weights, flipped, j)
        for n, row in enumerate((0, 1, 8, 9)):
            put(prod, j, row, out[n * COLS : (n + 1) * COLS])
        for n, start in enumerate((6, 7, 72, 73)):
            at = 4 * COLS + 16 * n
            place_column(prod, j, start, out[at : at + 10])


def columns(prod, start):
    parts = [
        prod[0, h, pl.ds(start, 10, stride=PITCH), :]
        + prod[1, h, pl.ds(start + 1, 10, stride=PITCH), :]
        + prod[2, h, pl.ds(start + 2, 10, stride=PITCH), :]
        for h in range(2)
    ]
    return jnp.concatenate(parts, axis=1)


def silu_parts(x):
    sigma = 1.0 / (1.0 + jnp.exp(-x))
    return x * sigma, sigma * (1.0 + x * (1.0 - sigma))


def gathered(prod, start, count):
    parts = [
        prod[0, h, start : start + count]
        + prod[1, h, start + 1 : start + 1 + count]
        + prod[2, h, start + 2 : start + 2 + count]
        for h in range(2)
    ]
    return jnp.concatenate(parts, axis=1)


def pack(field, packs):
    sub = iota((16, CH), 0)
    west = jnp.zeros((16, CH), F32)
    east = jnp.zeros((16, CH), F32)
    for r in range(ROWS):
        here = (sub == 2 * r) | (sub == 2 * r + 1)
        x = field[2 + r, 0:16].astype(F32)
        west = jnp.where(here, x if r == 0 else pltpu.roll(x, 2 * r, 0), west)
        x = field[2 + r, 48:64].astype(F32)
        east = jnp.where(here, x if r == 7 else pltpu.roll(x, (2 * r - 14) % 16, 0), east)
    packs[0] = west.astype(B16)
    packs[1] = east.astype(B16)


def assemble(edge, parts, north, south):
    for n, (a, b) in enumerate(CORNERS):
        x = parts[n]
        side = 0 if b < 0 else 1
        for h in range(2):
            y = x[:, h * 128 : (h + 1) * 128]
            if a < 0:
                edge[side, h, 0:4] = jnp.where(north, y[12:16], 0.0)
            elif a == 0:
                edge[side, h, 4:20] = y
            else:
                edge[side, h, 20:24] = jnp.where(south, y[0:4], 0.0)


def kernel(
    ids_in, taps_in, wts_in, vals_in, prec_in, probe_in, state, background, conv_in, conv_out,
    grad, innov,
    ids, taps, wts, vals, prec, probe, edge, sx, mx, ax, bg, w1, w2, slope, slope_side, hx, side, mb, prod, dt, rank_s,
    packs, arrived, sbuf, r2, qbuf, q2, zs, zr,
    load_sem, row_sem, pack_sem, out_sem, back_sem, z_sem, own_sem, ready,
):
    la = lax.axis_index("lat")
    lo = lax.axis_index("lon")

    def near(a, b):
        return place(a, b)[1]

    def send(src, dst, sems, to):
        return pltpu.make_async_remote_copy(
            src_ref=src, dst_ref=dst, send_sem=sems[0], recv_sem=sems[1],
            device_id=to, device_id_type=MESH,
        )

    me = la * LONS + lo
    barrier = pltpu.get_barrier_semaphore()

    def place(a, b):
        to = (lax.bitwise_and(la + a, LATS - 1), lax.bitwise_and(lo + b, LONS - 1))
        return to[0] * LONS + to[1], to

    ins = [(ids_in, ids), (prec_in, prec), (taps_in, taps), (wts_in, wts), (vals_in, vals)]
    ins += [(state, sx.at[2:10]), (conv_in, w1), (conv_out, w2), (background, bg)]
    ins += [(probe_in, probe)]
    loads = [pltpu.make_async_copy(a, b, load_sem.at[n]) for n, (a, b) in enumerate(ins)]
    for c in loads[:5]:
        c.start()

    def greet(a, b):
        pl.semaphore_signal(barrier, inc=1, device_id=place(a, b)[1], device_id_type=MESH)

    def where(a, run, things):
        def body():
            for t in things:
                run(t)

        if a == 0:
            body()
        else:
            pl.when(la > 0 if a < 0 else la < LATS - 1)(body)

    for a in (-1, 1):
        where(a, lambda b: greet(a, b), (-1, 1))
    for a, b in LINES:
        greet(a, b)
    for c in loads[5:]:
        c.start()

    def each(copies, act):
        for a in (-1, 1, 0):
            where(a, act, [c for s, c in copies if s[0] == a])

    def give(src, dst, sems, row, b):
        to = (row, lax.bitwise_and(lo + b, LONS - 1))
        send(src.at[row * LONS + to[1]], dst.at[me], (sems.at[0], sems.at[1]), to).start()

    def depart(src, dst, sems, offsets):
        for a, b in offsets:
            t, to = place(a, b)
            send(src.at[t], dst.at[me], (sems.at[0], sems.at[1]), to).start()

    def stay(src, dst, n):
        own = pltpu.make_async_copy(src.at[me], dst.at[me], own_sem.at[n])
        own.start()
        return own

    def settle(src, dst, sems, which):
        some = slice(0, TILES - 1)
        pltpu.make_async_copy(src.at[some], dst.at[some], sems.at[which]).wait()

    def halo(field, which):
        copies = [
            ((-1, 0), send(field.at[2:4], field.at[10:12],
                           (row_sem.at[which, 0, 0], row_sem.at[which, 1, 1]), near(-1, 0))),
            ((1, 0), send(field.at[8:10], field.at[0:2],
                          (row_sem.at[which, 1, 0], row_sem.at[which, 0, 1]), near(1, 0))),
        ]
        for n, (a, b) in enumerate(CORNERS):
            m = CORNERS.index((-a, -b))
            copies.append(
                ((a, b), send(packs.at[which, 0 if b < 0 else 1], arrived.at[which, m],
                              (pack_sem.at[which, n, 0], pack_sem.at[which, m, 1]), near(a, b)))
            )
        return copies

    def arrive(copies):
        back = {s: c for s, c in copies}
        each([(s, back[-s[0], -s[1]]) for s in back], lambda c: c.wait_recv())

    inside = {-1: la > 0, 0: True, 1: la < LATS - 1}

    def kept_in(r, x):
        a = -1 if r < 1 else (1 if r > 8 else 0)
        return jnp.where(inside[a], x, 0.0) if a else x

    for c in loads[:5]:
        c.wait()
    upper = jnp.where(iota((128, 128), 0) <= iota((128, 128), 1), 1.0, 0.0).astype(B16)
    carry = jnp.zeros((128, 1), F32)
    ranks = []
    for c in range(16):
        hit = iota((128, 128), 0) == ids[0:1, c * 128 : (c + 1) * 128]
        one = jnp.where(hit, 1.0, 0.0).astype(B16)
        dt[:, c * 128 : (c + 1) * 128] = one
        run = jnp.dot(one, upper, preferred_element_type=F32) + carry
        ranks.append(jnp.sum(jnp.where(hit, run, 0.0), axis=0, keepdims=True) - 1.0)
        carry = run[:, 127:128]
    rank = jnp.concatenate(ranks, axis=1)
    rank_s[...] = rank
    acc = jnp.zeros((128, 512), F32)
    for c in range(8):
        cut = slice(c * 256, (c + 1) * 256)
        own = iota((CAP, 256), 0) == rank[:, cut].astype(I32)
        p = prec[0:1, cut]
        rows = [taps[k : k + 1, cut].astype(F32) - 256.0 for k in range(4)]
        scaled = [wts[k : k + 1, cut] * p for k in range(4)] + [vals[0:1, cut] * p]
        tops = [s.astype(B16).astype(F32) for s in scaled]
        lows = [s - t for s, t in zip(scaled, tops)]
        rows += tops[:4] + lows[:4] + [tops[4], lows[4]]
        spots = [jnp.where(own, r, 0.0).astype(B16) for r in rows]
        spots.append(jnp.zeros((64, 256), B16))
        x = jnp.concatenate(spots, axis=0)
        acc = acc + lax.dot_general(dt[:, cut], x, NT, preferred_element_type=F32)
    sbuf[:, 0, 0:128] = acc[:, 0:128]
    sbuf[:, 0, 128:256] = acc[:, 128:256] + acc[:, 256:384]
    sbuf[:, 0, 256:384] = acc[:, 384:512]

    loads[5].wait()
    pack(sx, packs.at[0])
    ends = jnp.where((la == 0) | (la == LATS - 1), 2, 4)
    pl.semaphore_wait(barrier, len(LINES) + ends)
    for a in range(1, LATS):
        pl.semaphore_signal(
            ready.at[la], inc=1, device_id=place(a, 0)[1], device_id_type=MESH
        )
    first = halo(sx, 0)
    each(first, lambda c: c.start())
    loads[6].wait()
    for j in range(3):
        inner(sx, w1, False, prod, j)
    for row in range(LATS):

        @pl.when(la != row)
        def _(row=row):
            pl.semaphore_wait(ready.at[row], 1)
            give(sbuf, r2, out_sem, row, 0)

        for b in ROUND:
            give(sbuf, r2, out_sem, row, b)
    kept = stay(sbuf, r2, 0)

    arrive(first)
    assemble(edge, [arrived[0, n].astype(F32) for n in range(6)], la > 0, la < LATS - 1)
    sx[0:2] = jnp.where(inside[-1], sx[0:2], jnp.zeros((2, COLS, CH), B16))
    sx[10:12] = jnp.where(inside[1], sx[10:12], jnp.zeros((2, COLS, CH), B16))
    border(sx, edge, w1, False, prod)
    for r in range(10):
        y, slope[r] = silu_parts(gathered(prod, r * PITCH + 7, COLS))
        hx[r] = kept_in(r, y).astype(B16)
    row10 = iota((10, CH), 0)
    outside = ((row10 == 0) & (la == 0)) | ((row10 == 9) & (la == LATS - 1))
    for b in range(2):
        y, slope_side[b, 0:10] = silu_parts(columns(prod, 71 * b + 6 * (1 - b)))
        side[b, 0:10] = jnp.where(outside, 0.0, y)

    for c in loads[7:]:
        c.wait()
    products(hx, side, w2, False, prod)
    pr = probe[...]
    ph, plow = halves(pr)
    sub16 = iota((16, CH), 0)
    readout = jnp.where(
        sub16 == 0, ph.astype(F32), jnp.where(sub16 == 1, plow.astype(F32), 0.0)
    ).astype(B16)
    highs, lows = [], []
    for r in range(ROWS):
        m = gathered(prod, r * PITCH + 7, COLS) + sx[2 + r].astype(F32)
        high, low = halves(m)
        highs.append(high)
        lows.append(low)
        d = m - bg[r].astype(F32)
        mb[r] = d
        mx[2 + r] = d.astype(B16)
    pack(mx, packs.at[1])
    second = halo(mx, 1)
    each(second, lambda c: c.start())
    s = lax.dot_general(readout, jnp.concatenate(highs, axis=0), NT, preferred_element_type=F32)
    t = lax.dot_general(readout, jnp.concatenate(lows, axis=0), NT, preferred_element_type=F32)
    scalar = s[0:1] + s[1:2] + t[0:1]
    tables = [jnp.broadcast_to(scalar[:, q * 128 : (q + 1) * 128], (8, 128)) for q in range(4)]

    kept.wait()
    settle(sbuf, r2, out_sem, 1)
    cells, shares = [], []
    for t in range(TILES // 8):
        own = slice(8 * t, 8 * t + 8)
        cell = r2[own, 0, 0:128].astype(I32) + 256
        w = r2[own, 0, 128:256]
        lane = lax.bitwise_and(cell, 127)
        page = lax.shift_right_logical(cell, 7)
        got = jnp.zeros((8, 128), F32)
        for q in range(4):
            look = jnp.take_along_axis(tables[q], lane, axis=1, mode="promise_in_bounds")
            got = jnp.where(page == q, look, got)
        res = w * got - r2[own, 0, 256:384]
        res = res + pltpu.roll(res, 64, 1)
        res = res + pltpu.roll(res, 32, 1)
        qbuf[own, 0, :] = res
        cells.append(cell)
        shares.append(w * res)

    total = jnp.zeros((128, 256), F32)
    for t in range(0, TILES // 8, 2):
        cell = jnp.concatenate(cells[t : t + 2], axis=1)
        share = jnp.concatenate(shares[t : t + 2], axis=1)
        upper_cell = lax.shift_right_logical(cell, 5)
        lower_cell = lax.bitwise_and(cell, 31)
        tops, marks = [], []
        for g in range(8):
            hit = iota((16, 256), 0) == upper_cell[g : g + 1]
            tops.append(jnp.where(hit, share[g : g + 1], 0.0).astype(B16))
            marks.append(
                jnp.where(iota((32, 256), 0) == lower_cell[g : g + 1], 1.0, 0.0).astype(B16)
            )
        lhs = jnp.concatenate(tops, axis=0)
        rhs = jnp.concatenate(marks, axis=0)
        total = total + lax.dot_general(lhs, rhs, NT, preferred_element_type=F32)
    total = jnp.where(iota((128, 256), 0) // 16 == iota((128, 256), 1) // 32, total, 0.0)
    fold = total[0:16]
    for g in range(1, 8):
        fold = fold + total[g * 16 : (g + 1) * 16]
    fold = fold[:, 0:128] + fold[:, 128:256]
    fold = fold + pltpu.roll(fold, 64, 1)
    fold = fold + pltpu.roll(fold, 32, 1)
    zs[...] = fold
    out4 = []
    for n, (a, b) in enumerate(SIDES):
        m = SIDES.index((-a, -b))
        out4.append(((a, b), send(zs, zr.at[m], (z_sem.at[n, 0], z_sem.at[m, 1]), near(a, b))))
    each(out4, lambda c: c.start())

    group = iota((16, 128), 1) // 32
    base = jnp.where(iota((128, CH), 0) // 64 == 0, ph.astype(F32), plow.astype(F32)).astype(B16)
    sub = iota((16, 128), 0)
    odd = lax.bitwise_and(sub, 1)
    spot = lax.bitwise_and(iota((16, 128), 1), 31)
    marks = [spot == sub, spot == sub + 16]

    def parted(z):
        top = z.astype(B16).astype(F32)
        return jnp.where(lax.bitwise_and(group, 1) == 0, top, z - top)

    def outer(blocks):
        lhs = jnp.concatenate(
            [
                jnp.where(marks[c % 2], z[2 * r + c // 2 : 2 * r + c // 2 + 1], 0.0).astype(B16)
                for z, r, c in blocks
            ],
            axis=0,
        )
        return jnp.dot(lhs, base, preferred_element_type=F32)

    center = parted(fold)
    for r in range(ROWS):
        local = outer([(center, r, c) for c in range(4)])
        ax[2 + r] = (mb[r] + local).astype(B16)
    depart(qbuf, q2, back_sem, OTHERS)
    kept = stay(qbuf, q2, 1)
    for j in range(3):
        inner(ax, w2, True, prod, j)

    arrive(second)
    arrive(out4)
    around = {s: parted(zr[n]) for n, s in enumerate(SIDES)}
    for a, rows in ((-1, (6, 7)), (1, (0, 1))):
        piece = outer([(around[a, 0], r, c) for r in rows for c in range(4)])
        for n, r in enumerate(rows):
            row = r + 2 + a * 8
            x = mx[row].astype(F32) + piece[n * 64 : (n + 1) * 64]
            ax[row] = jnp.where(inside[a], x, 0.0).astype(B16)
    strips = []
    for a, b in CORNERS:
        z = around[a, b]
        if b < 0:
            z = jnp.where(odd == 1, z, pltpu.roll(z, 15, 0))
            hit = spot == odd + 30
        else:
            z = jnp.where(odd == 0, z, pltpu.roll(z, 1, 0))
            hit = spot == odd
        strips.append(jnp.where(hit, z, 0.0).astype(B16))
    piece = jnp.dot(jnp.concatenate(strips, axis=0), base, preferred_element_type=F32)
    parts = [
        (arrived[1, n].astype(F32) + piece[16 * n : 16 * n + 16]).astype(B16).astype(F32)
        for n in range(6)
    ]
    assemble(edge, parts, la > 0, la < LATS - 1)

    border(ax, edge, w2, True, prod)
    for r in range(10):
        hx[r] = kept_in(r, gathered(prod, r * PITCH + 7, COLS) * slope[r]).astype(B16)
    for b in range(2):
        y = columns(prod, 71 * b + 6 * (1 - b)) * slope_side[b, 0:10]
        side[b, 0:10] = jnp.where(outside, 0.0, y)
    products(hx, side, w1, True, prod)
    kept.wait()
    settle(qbuf, q2, back_sem, 1)
    back = q2[:, 0, :].T[0:CAP]
    one = back.astype(B16)
    rest = back - one.astype(F32)
    two = rest.astype(B16)
    three = (rest - two.astype(F32)).astype(B16)
    lhs = jnp.concatenate([one, two, three], axis=0)
    for r in range(ROWS):
        y = gathered(prod, r * PITCH + 7, COLS) + ax[2 + r].astype(F32)
        grad[r] = y.astype(B16)
    for c in range(4):
        cut = slice(c * 512, (c + 1) * 512)
        got = jnp.dot(lhs, dt[:, cut], preferred_element_type=F32)
        got = got[0:32] + got[32:64] + got[64:96]
        own = iota((CAP, 512), 0) == rank_s[0:1, cut].astype(I32)
        innov[0:1, cut] = jnp.sum(jnp.where(own, got, 0.0), axis=0, keepdims=True)

    each(first + second + out4, lambda c: c.wait_send())
    settle(sbuf, r2, out_sem, 0)
    settle(qbuf, q2, back_sem, 0)


def on_device(
    state, background, conv_in, conv_out, probe,
    tile_ids, cell_taps, tap_weights, obs_values, obs_precision,
):
    vmem = pl.BlockSpec(memory_space=pltpu.VMEM)
    hbm = pl.BlockSpec(memory_space=pl.ANY)
    dma = pltpu.SemaphoreType.DMA
    wide = pltpu.VMEM((12, COLS, CH), B16)
    kshape = (3, 3, CH, CH)
    grad, innov = pl.pallas_call(
        kernel,
        out_shape=(
            pltpu.VMEM((ROWS, COLS, CH), B16),
            pltpu.VMEM((1, COUNT), F32),
        ),
        in_specs=[hbm] * 10,
        out_specs=(vmem, vmem),
        scratch_shapes=[
            pltpu.VMEM((1, COUNT), I32),
            pltpu.VMEM((4, COUNT), I32),
            pltpu.VMEM((4, COUNT), F32),
            pltpu.VMEM((1, COUNT), F32),
            pltpu.VMEM((1, COUNT), F32),
            pltpu.VMEM((1, CH), F32),
            pltpu.VMEM((2, 2, 40, 128), F32),
            wide, wide, wide,
            pltpu.VMEM((ROWS, COLS, CH), B16),
            pltpu.VMEM(kshape, B16),
            pltpu.VMEM(kshape, B16),
            pltpu.VMEM((10, COLS, CH), F32),
            pltpu.VMEM((2, 16, CH), F32),
            pltpu.VMEM((10, COLS, CH), B16),
            pltpu.VMEM((2, 16, CH), F32),
            pltpu.VMEM((ROWS, COLS, CH), F32),
            pltpu.VMEM((3, 2, 10 * PITCH + 64, 128), F32),
            pltpu.VMEM((TILES, COUNT), B16),
            pltpu.VMEM((1, COUNT), F32),
            pltpu.VMEM((2, 2, 16, CH), B16),
            pltpu.VMEM((2, len(CORNERS), 16, CH), B16),
            pltpu.VMEM((TILES, 1, 384), F32),
            pltpu.VMEM((TILES, 1, 384), F32),
            pltpu.VMEM((TILES, 1, 128), F32),
            pltpu.VMEM((TILES, 1, 128), F32),
            pltpu.VMEM((16, 128), F32),
            pltpu.VMEM((len(SIDES), 16, 128), F32),
            dma((10,)),
            dma((2, 2, 2)),
            dma((2, len(CORNERS), 2)),
            dma((2,)),
            dma((2,)),
            dma((len(SIDES), 2)),
            dma((2,)),
            pltpu.SemaphoreType.REGULAR((LATS,)),
        ],
        compiler_params=pltpu.CompilerParams(
            collective_id=0, has_side_effects=True, vmem_limit_bytes=56 * 2**20
        ),
    )(
        tile_ids.reshape(1, COUNT),
        cell_taps,
        tap_weights,
        obs_values.reshape(1, COUNT),
        obs_precision.reshape(1, COUNT),
        probe.reshape(1, CH),
        state,
        background,
        conv_in,
        conv_out,
    )
    return grad, innov.reshape(COUNT)


def solution(mesh):
    in_specs = (
        P("lat", "lon", None),
        P("lat", "lon", None),
        P(),
        P(),
        P(),
        P(("lat", "lon"), None),
        P(None, ("lat", "lon")),
        P(None, ("lat", "lon")),
        P(("lat", "lon")),
        P(("lat", "lon")),
    )
    out_specs = (P("lat", "lon", None), P(("lat", "lon")))
    return jax.shard_map(
        on_device, mesh=mesh, in_specs=in_specs, out_specs=out_specs, check_vma=False
    )
```

```python
import functools

import jax
import jax.numpy as jnp
from jax import lax
from jax.experimental import pallas as pl
from jax.experimental.pallas import tpu as pltpu
from jax.sharding import PartitionSpec as P

MESH = pl.DeviceIdType.MESH
B16 = jnp.bfloat16
F32 = jnp.float32
I32 = jnp.int32
ROWS, COLS, CH = 8, 64, 256
PITCH = 80
LATS, LONS = 8, 16
TILES = LATS * LONS
COUNT = 2048
CAP = 32
NT = (((1,), (1,)), ((), ()))
SIDES = [(a, b) for a in (-1, 0, 1) for b in (-1, 0, 1) if (a, b) != (0, 0)]
CORNERS = [s for s in SIDES if s[1] != 0]


def hops(a, b):
    y, x, z = a // 2, b // 4, b % 4
    return min(y, 4 - y) + min(x, 4 - x) + min(z, 4 - z)


OTHERS = [(a, b) for a in range(LATS) for b in range(LONS) if (a, b) != (0, 0)]
OTHERS.sort(key=lambda o: -hops(*o))
ROUND = sorted(range(1, LONS), key=lambda b: -hops(0, b))
LINES = [o for o in OTHERS if 0 in o]


def iota(shape, dim):
    return lax.broadcasted_iota(I32, shape, dim)


def halves(x):
    high = x.astype(B16)
    return high, (x - high.astype(F32)).astype(B16)


def weighted(lhs, weights, flipped, j):
    if flipped:
        rhs = jnp.concatenate([weights[2 - i, 2 - j] for i in range(3)], axis=1)
        return lax.dot_general(lhs, rhs, NT, preferred_element_type=F32)
    rhs = jnp.concatenate([weights[i, j] for i in range(3)], axis=0)
    return jnp.dot(lhs, rhs, preferred_element_type=F32)


def windows(field, first, rows):
    count = rows * field.shape[1]
    return jnp.concatenate(
        [field[first + i : first + i + rows].reshape(count, CH) for i in range(3)], axis=1
    )


def products(field, sides, weights, flipped, prod):
    ends = [jnp.concatenate([sides[b, i : i + ROWS] for i in range(3)], axis=1) for b in range(2)]
    lhs = jnp.concatenate(
        [windows(field, 0, ROWS), jnp.concatenate(ends, axis=0).astype(B16)], axis=0
    )
    for j in range(3):
        out = weighted(lhs, weights, flipped, j)
        for row in range(ROWS):
            put(prod, j, row, out[row * COLS : (row + 1) * COLS])
        at = ROWS * COLS
        place_column(prod, j, 7, out[at : at + ROWS])
        place_column(prod, j, 72, out[at + ROWS : at + 2 * ROWS])


def place_column(prod, j, start, out):
    rows = pl.ds(start, out.shape[0], stride=PITCH)
    prod[j, 0, rows, :] = out[:, :128]
    prod[j, 1, rows, :] = out[:, 128:]


def put(prod, j, row, out):
    start = row * PITCH + 8
    prod[j, 0, start : start + COLS] = out[:, :128]
    prod[j, 1, start : start + COLS] = out[:, 128:]


def inner(field, weights, flipped, prod, j):
    out = weighted(windows(field, 2, 6), weights, flipped, j)
    for n in range(6):
        put(prod, j, 2 + n, out[n * COLS : (n + 1) * COLS])


def border(field, edge, weights, flipped, prod):
    sides = [
        jnp.concatenate(
            [edge[b, h, pl.ds(2 * i + c, 16, stride=2), :] for i in range(3) for h in range(2)],
            axis=1,
        )
        for b in range(2)
        for c in range(2)
    ]
    lhs = jnp.concatenate(
        [windows(field, 0, 2), windows(field, 8, 2), jnp.concatenate(sides, axis=0).astype(B16)],
        axis=0,
    )
    for j in range(3):
        out = weighted(lhs, weights, flipped, j)
        for n, row in enumerate((0, 1, 8, 9)):
            put(prod, j, row, out[n * COLS : (n + 1) * COLS])
        for n, start in enumerate((6, 7, 72, 73)):
            at = 4 * COLS + 16 * n
            place_column(prod, j, start, out[at : at + 10])


def columns(prod, start):
    parts = [
        prod[0, h, pl.ds(start, 10, stride=PITCH), :]
        + prod[1, h, pl.ds(start + 1, 10, stride=PITCH), :]
        + prod[2, h, pl.ds(start + 2, 10, stride=PITCH), :]
        for h in range(2)
    ]
    return jnp.concatenate(parts, axis=1)


def silu_parts(x):
    sigma = 1.0 / (1.0 + jnp.exp(-x))
    return x * sigma, sigma * (1.0 + x * (1.0 - sigma))


def gathered(prod, start, count):
    parts = [
        prod[0, h, start : start + count]
        + prod[1, h, start + 1 : start + 1 + count]
        + prod[2, h, start + 2 : start + 2 + count]
        for h in range(2)
    ]
    return jnp.concatenate(parts, axis=1)


def pack(field, packs):
    sub = iota((16, CH), 0)
    west = jnp.zeros((16, CH), F32)
    east = jnp.zeros((16, CH), F32)
    for r in range(ROWS):
        here = (sub == 2 * r) | (sub == 2 * r + 1)
        x = field[2 + r, 0:16].astype(F32)
        west = jnp.where(here, x if r == 0 else pltpu.roll(x, 2 * r, 0), west)
        x = field[2 + r, 48:64].astype(F32)
        east = jnp.where(here, x if r == 7 else pltpu.roll(x, (2 * r - 14) % 16, 0), east)
    packs[0] = west.astype(B16)
    packs[1] = east.astype(B16)


def assemble(edge, parts, north, south):
    for n, (a, b) in enumerate(CORNERS):
        x = parts[n]
        side = 0 if b < 0 else 1
        for h in range(2):
            y = x[:, h * 128 : (h + 1) * 128]
            if a < 0:
                edge[side, h, 0:4] = jnp.where(north, y[12:16], 0.0)
            elif a == 0:
                edge[side, h, 4:20] = y
            else:
                edge[side, h, 20:24] = jnp.where(south, y[0:4], 0.0)


def kernel(
    ids_in, taps_in, wts_in, vals_in, prec_in, probe_in, state, background, conv_in, conv_out,
    grad, innov,
    ids, taps, wts, vals, prec, probe, edge, sx, mx, ax, bg, w1, w2, slope, slope_side, hx, side, mb, prod, dt, rank_s,
    packs, arrived, sbuf, r2, qbuf, q2, zs, zr,
    load_sem, row_sem, pack_sem, out_sem, back_sem, z_sem, own_sem, ready,
):
    la = lax.axis_index("lat")
    lo = lax.axis_index("lon")

    def near(a, b):
        return place(a, b)[1]

    def send(src, dst, sems, to):
        return pltpu.make_async_remote_copy(
            src_ref=src, dst_ref=dst, send_sem=sems[0], recv_sem=sems[1],
            device_id=to, device_id_type=MESH,
        )

    me = la * LONS + lo
    barrier = pltpu.get_barrier_semaphore()

    def place(a, b):
        to = (lax.bitwise_and(la + a, LATS - 1), lax.bitwise_and(lo + b, LONS - 1))
        return to[0] * LONS + to[1], to

    ins = [(ids_in, ids), (prec_in, prec), (taps_in, taps), (wts_in, wts), (vals_in, vals)]
    ins += [(state, sx.at[2:10]), (conv_in, w1), (conv_out, w2), (background, bg)]
    ins += [(probe_in, probe)]
    loads = [pltpu.make_async_copy(a, b, load_sem.at[n]) for n, (a, b) in enumerate(ins)]
    for c in loads[:5]:
        c.start()

    def greet(a, b):
        pl.semaphore_signal(barrier, inc=1, device_id=place(a, b)[1], device_id_type=MESH)

    def where(a, run, things):
        def body():
            for t in things:
                run(t)

        if a == 0:
            body()
        else:
            pl.when(la > 0 if a < 0 else la < LATS - 1)(body)

    for a in (-1, 1):
        where(a, lambda b: greet(a, b), (-1, 1))
    for a, b in LINES:
        greet(a, b)
    for c in loads[5:]:
        c.start()

    def each(copies, act):
        for a in (-1, 1, 0):
            where(a, act, [c for s, c in copies if s[0] == a])

    def give(src, dst, sems, row, b):
        to = (row, lax.bitwise_and(lo + b, LONS - 1))
        send(src.at[row * LONS + to[1]], dst.at[me], (sems.at[0], sems.at[1]), to).start()

    def depart(src, dst, sems, offsets):
        for a, b in offsets:
            t, to = place(a, b)
            send(src.at[t], dst.at[me], (sems.at[0], sems.at[1]), to).start()

    def stay(src, dst, n):
        own = pltpu.make_async_copy(src.at[me], dst.at[me], own_sem.at[n])
        own.start()
        return own

    def settle(src, dst, sems, which):
        some = slice(0, TILES - 1)
        pltpu.make_async_copy(src.at[some], dst.at[some], sems.at[which]).wait()

    def halo(field, which):
        copies = [
            ((-1, 0), send(field.at[2:4], field.at[10:12],
                           (row_sem.at[which, 0, 0], row_sem.at[which, 1, 1]), near(-1, 0))),
            ((1, 0), send(field.at[8:10], field.at[0:2],
                          (row_sem.at[which, 1, 0], row_sem.at[which, 0, 1]), near(1, 0))),
        ]
        for n, (a, b) in enumerate(CORNERS):
            m = CORNERS.index((-a, -b))
            copies.append(
                ((a, b), send(packs.at[which, 0 if b < 0 else 1], arrived.at[which, m],
                              (pack_sem.at[which, n, 0], pack_sem.at[which, m, 1]), near(a, b)))
            )
        return copies

    def arrive(copies):
        back = {s: c for s, c in copies}
        each([(s, back[-s[0], -s[1]]) for s in back], lambda c: c.wait_recv())

    inside = {-1: la > 0, 0: True, 1: la < LATS - 1}

    def kept_in(r, x):
        a = -1 if r < 1 else (1 if r > 8 else 0)
        return jnp.where(inside[a], x, 0.0) if a else x

    for c in loads[:5]:
        c.wait()
    upper = jnp.where(iota((128, 128), 0) <= iota((128, 128), 1), 1.0, 0.0).astype(B16)
    carry = jnp.zeros((128, 1), F32)
    ranks = []
    for c in range(16):
        hit = iota((128, 128), 0) == ids[0:1, c * 128 : (c + 1) * 128]
        one = jnp.where(hit, 1.0, 0.0).astype(B16)
        dt[:, c * 128 : (c + 1) * 128] = one
        run = jnp.dot(one, upper, preferred_element_type=F32) + carry
        ranks.append(jnp.sum(jnp.where(hit, run, 0.0), axis=0, keepdims=True) - 1.0)
        carry = run[:, 127:128]
    rank = jnp.concatenate(ranks, axis=1)
    rank_s[...] = rank
    acc = jnp.zeros((128, 512), F32)
    for c in range(8):
        cut = slice(c * 256, (c + 1) * 256)
        own = iota((CAP, 256), 0) == rank[:, cut].astype(I32)
        p = prec[0:1, cut]
        rows = [taps[k : k + 1, cut].astype(F32) - 256.0 for k in range(4)]
        scaled = [wts[k : k + 1, cut] * p for k in range(4)] + [vals[0:1, cut] * p]
        tops = [s.astype(B16).astype(F32) for s in scaled]
        lows = [s - t for s, t in zip(scaled, tops)]
        rows += tops[:4] + lows[:4] + [tops[4], lows[4]]
        spots = [jnp.where(own, r, 0.0).astype(B16) for r in rows]
        spots.append(jnp.zeros((64, 256), B16))
        x = jnp.concatenate(spots, axis=0)
        acc = acc + lax.dot_general(dt[:, cut], x, NT, preferred_element_type=F32)
    sbuf[:, 0, 0:128] = acc[:, 0:128]
    sbuf[:, 0, 128:256] = acc[:, 128:256] + acc[:, 256:384]
    sbuf[:, 0, 256:384] = acc[:, 384:512]

    loads[5].wait()
    pack(sx, packs.at[0])
    ends = jnp.where((la == 0) | (la == LATS - 1), 2, 4)
    pl.semaphore_wait(barrier, len(LINES) + ends)
    for a in range(1, LATS):
        pl.semaphore_signal(
            ready.at[la], inc=1, device_id=place(a, 0)[1], device_id_type=MESH
        )
    first = halo(sx, 0)
    each(first, lambda c: c.start())
    loads[6].wait()
    for j in range(3):
        inner(sx, w1, False, prod, j)
    for row in range(LATS):

        @pl.when(la != row)
        def _(row=row):
            pl.semaphore_wait(ready.at[row], 1)
            give(sbuf, r2, out_sem, row, 0)

        for b in ROUND:
            give(sbuf, r2, out_sem, row, b)
    kept = stay(sbuf, r2, 0)

    arrive(first)
    assemble(edge, [arrived[0, n].astype(F32) for n in range(6)], la > 0, la < LATS - 1)
    sx[0:2] = jnp.where(inside[-1], sx[0:2], jnp.zeros((2, COLS, CH), B16))
    sx[10:12] = jnp.where(inside[1], sx[10:12], jnp.zeros((2, COLS, CH), B16))
    border(sx, edge, w1, False, prod)
    for r in range(10):
        y, slope[r] = silu_parts(gathered(prod, r * PITCH + 7, COLS))
        hx[r] = kept_in(r, y).astype(B16)
    row10 = iota((10, CH), 0)
    outside = ((row10 == 0) & (la == 0)) | ((row10 == 9) & (la == LATS - 1))
    for b in range(2):
        y, slope_side[b, 0:10] = silu_parts(columns(prod, 71 * b + 6 * (1 - b)))
        side[b, 0:10] = jnp.where(outside, 0.0, y)

    for c in loads[7:]:
        c.wait()
    products(hx, side, w2, False, prod)
    pr = probe[...]
    ph, plow = halves(pr)
    sub16 = iota((16, CH), 0)
    readout = jnp.where(
        sub16 == 0, ph.astype(F32), jnp.where(sub16 == 1, plow.astype(F32), 0.0)
    ).astype(B16)
    highs, lows = [], []
    for r in range(ROWS):
        m = gathered(prod, r * PITCH + 7, COLS) + sx[2 + r].astype(F32)
        high, low = halves(m)
        highs.append(high)
        lows.append(low)
        d = m - bg[r].astype(F32)
        mb[r] = d
        mx[2 + r] = d.astype(B16)
    pack(mx, packs.at[1])
    second = halo(mx, 1)
    each(second, lambda c: c.start())
    s = lax.dot_general(readout, jnp.concatenate(highs, axis=0), NT, preferred_element_type=F32)
    t = lax.dot_general(readout, jnp.concatenate(lows, axis=0), NT, preferred_element_type=F32)
    scalar = s[0:1] + s[1:2] + t[0:1]
    tables = [jnp.broadcast_to(scalar[:, q * 128 : (q + 1) * 128], (8, 128)) for q in range(4)]

    kept.wait()
    settle(sbuf, r2, out_sem, 1)
    cells, shares = [], []
    for t in range(TILES // 8):
        own = slice(8 * t, 8 * t + 8)
        cell = r2[own, 0, 0:128].astype(I32) + 256
        w = r2[own, 0, 128:256]
        lane = lax.bitwise_and(cell, 127)
        page = lax.shift_right_logical(cell, 7)
        got = jnp.zeros((8, 128), F32)
        for q in range(4):
            look = jnp.take_along_axis(tables[q], lane, axis=1, mode="promise_in_bounds")
            got = jnp.where(page == q, look, got)
        res = w * got - r2[own, 0, 256:384]
        res = res + pltpu.roll(res, 64, 1)
        res = res + pltpu.roll(res, 32, 1)
        qbuf[own, 0, :] = res
        cells.append(cell)
        shares.append(w * res)

    total = jnp.zeros((128, 256), F32)
    for t in range(0, TILES // 8, 2):
        cell = jnp.concatenate(cells[t : t + 2], axis=1)
        share = jnp.concatenate(shares[t : t + 2], axis=1)
        upper_cell = lax.shift_right_logical(cell, 5)
        lower_cell = lax.bitwise_and(cell, 31)
        tops, marks = [], []
        for g in range(8):
            hit = iota((16, 256), 0) == upper_cell[g : g + 1]
            tops.append(jnp.where(hit, share[g : g + 1], 0.0).astype(B16))
            marks.append(
                jnp.where(iota((32, 256), 0) == lower_cell[g : g + 1], 1.0, 0.0).astype(B16)
            )
        lhs = jnp.concatenate(tops, axis=0)
        rhs = jnp.concatenate(marks, axis=0)
        total = total + lax.dot_general(lhs, rhs, NT, preferred_element_type=F32)
    total = jnp.where(iota((128, 256), 0) // 16 == iota((128, 256), 1) // 32, total, 0.0)
    fold = total[0:16]
    for g in range(1, 8):
        fold = fold + total[g * 16 : (g + 1) * 16]
    fold = fold[:, 0:128] + fold[:, 128:256]
    fold = fold + pltpu.roll(fold, 64, 1)
    fold = fold + pltpu.roll(fold, 32, 1)
    zs[...] = fold
    out4 = []
    for n, (a, b) in enumerate(SIDES):
        m = SIDES.index((-a, -b))
        out4.append(((a, b), send(zs, zr.at[m], (z_sem.at[n, 0], z_sem.at[m, 1]), near(a, b))))
    each(out4, lambda c: c.start())

    group = iota((16, 128), 1) // 32
    base = jnp.where(iota((128, CH), 0) // 64 == 0, ph.astype(F32), plow.astype(F32)).astype(B16)
    sub = iota((16, 128), 0)
    odd = lax.bitwise_and(sub, 1)
    spot = lax.bitwise_and(iota((16, 128), 1), 31)
    marks = [spot == sub, spot == sub + 16]

    def parted(z):
        top = z.astype(B16).astype(F32)
        return jnp.where(lax.bitwise_and(group, 1) == 0, top, z - top)

    def outer(blocks):
        lhs = jnp.concatenate(
            [
                jnp.where(marks[c % 2], z[2 * r + c // 2 : 2 * r + c // 2 + 1], 0.0).astype(B16)
                for z, r, c in blocks
            ],
            axis=0,
        )
        return jnp.dot(lhs, base, preferred_element_type=F32)

    center = parted(fold)
    for r in range(ROWS):
        local = outer([(center, r, c) for c in range(4)])
        ax[2 + r] = (mb[r] + local).astype(B16)
    depart(qbuf, q2, back_sem, OTHERS)
    kept = stay(qbuf, q2, 1)
    for j in range(3):
        inner(ax, w2, True, prod, j)

    arrive(second)
    arrive(out4)
    around = {s: parted(zr[n]) for n, s in enumerate(SIDES)}
    for a, rows in ((-1, (6, 7)), (1, (0, 1))):
        piece = outer([(around[a, 0], r, c) for r in rows for c in range(4)])
        for n, r in enumerate(rows):
            row = r + 2 + a * 8
            x = mx[row].astype(F32) + piece[n * 64 : (n + 1) * 64]
            ax[row] = jnp.where(inside[a], x, 0.0).astype(B16)
    strips = []
    for a, b in CORNERS:
        z = around[a, b]
        if b < 0:
            z = jnp.where(odd == 1, z, pltpu.roll(z, 15, 0))
            hit = spot == odd + 30
        else:
            z = jnp.where(odd == 0, z, pltpu.roll(z, 1, 0))
            hit = spot == odd
        strips.append(jnp.where(hit, z, 0.0).astype(B16))
    piece = jnp.dot(jnp.concatenate(strips, axis=0), base, preferred_element_type=F32)
    parts = [
        (arrived[1, n].astype(F32) + piece[16 * n : 16 * n + 16]).astype(B16).astype(F32)
        for n in range(6)
    ]
    assemble(edge, parts, la > 0, la < LATS - 1)

    border(ax, edge, w2, True, prod)
    for r in range(10):
        hx[r] = kept_in(r, gathered(prod, r * PITCH + 7, COLS) * slope[r]).astype(B16)
    for b in range(2):
        y = columns(prod, 71 * b + 6 * (1 - b)) * slope_side[b, 0:10]
        side[b, 0:10] = jnp.where(outside, 0.0, y)
    products(hx, side, w1, True, prod)
    each(first + second + out4, lambda c: c.wait_send())
    settle(sbuf, r2, out_sem, 0)
    kept.wait()
    settle(qbuf, q2, back_sem, 1)
    back = q2[:, 0, :].T[0:CAP]
    one = back.astype(B16)
    rest = back - one.astype(F32)
    two = rest.astype(B16)
    lhs = jnp.concatenate([one, two], axis=0)
    for r in range(ROWS):
        y = gathered(prod, r * PITCH + 7, COLS) + ax[2 + r].astype(F32)
        grad[r] = y.astype(B16)
    for c in range(4):
        cut = slice(c * 512, (c + 1) * 512)
        got = jnp.dot(lhs, dt[:, cut], preferred_element_type=F32)
        got = got[0:32] + got[32:64]
        own = iota((CAP, 512), 0) == rank_s[0:1, cut].astype(I32)
        innov[0:1, cut] = jnp.sum(jnp.where(own, got, 0.0), axis=0, keepdims=True)

    settle(qbuf, q2, back_sem, 0)


def on_device(
    state, background, conv_in, conv_out, probe,
    tile_ids, cell_taps, tap_weights, obs_values, obs_precision,
):
    vmem = pl.BlockSpec(memory_space=pltpu.VMEM)
    hbm = pl.BlockSpec(memory_space=pl.ANY)
    dma = pltpu.SemaphoreType.DMA
    wide = pltpu.VMEM((12, COLS, CH), B16)
    kshape = (3, 3, CH, CH)
    grad, innov = pl.pallas_call(
        kernel,
        out_shape=(
            pltpu.VMEM((ROWS, COLS, CH), B16),
            pltpu.VMEM((1, COUNT), F32),
        ),
        in_specs=[hbm] * 10,
        out_specs=(vmem, vmem),
        scratch_shapes=[
            pltpu.VMEM((1, COUNT), I32),
            pltpu.VMEM((4, COUNT), I32),
            pltpu.VMEM((4, COUNT), F32),
            pltpu.VMEM((1, COUNT), F32),
            pltpu.VMEM((1, COUNT), F32),
            pltpu.VMEM((1, CH), F32),
            pltpu.VMEM((2, 2, 40, 128), F32),
            wide, wide, wide,
            pltpu.VMEM((ROWS, COLS, CH), B16),
            pltpu.VMEM(kshape, B16),
            pltpu.VMEM(kshape, B16),
            pltpu.VMEM((10, COLS, CH), F32),
            pltpu.VMEM((2, 16, CH), F32),
            pltpu.VMEM((10, COLS, CH), B16),
            pltpu.VMEM((2, 16, CH), F32),
            pltpu.VMEM((ROWS, COLS, CH), F32),
            pltpu.VMEM((3, 2, 10 * PITCH + 64, 128), F32),
            pltpu.VMEM((TILES, COUNT), B16),
            pltpu.VMEM((1, COUNT), F32),
            pltpu.VMEM((2, 2, 16, CH), B16),
            pltpu.VMEM((2, len(CORNERS), 16, CH), B16),
            pltpu.VMEM((TILES, 1, 384), F32),
            pltpu.VMEM((TILES, 1, 384), F32),
            pltpu.VMEM((TILES, 1, 128), F32),
            pltpu.VMEM((TILES, 1, 128), F32),
            pltpu.VMEM((16, 128), F32),
            pltpu.VMEM((len(SIDES), 16, 128), F32),
            dma((10,)),
            dma((2, 2, 2)),
            dma((2, len(CORNERS), 2)),
            dma((2,)),
            dma((2,)),
            dma((len(SIDES), 2)),
            dma((2,)),
            pltpu.SemaphoreType.REGULAR((LATS,)),
        ],
        compiler_params=pltpu.CompilerParams(
            collective_id=0, has_side_effects=True, vmem_limit_bytes=56 * 2**20
        ),
    )(
        tile_ids.reshape(1, COUNT),
        cell_taps,
        tap_weights,
        obs_values.reshape(1, COUNT),
        obs_precision.reshape(1, COUNT),
        probe.reshape(1, CH),
        state,
        background,
        conv_in,
        conv_out,
    )
    return grad, innov.reshape(COUNT)


def solution(mesh):
    in_specs = (
        P("lat", "lon", None),
        P("lat", "lon", None),
        P(),
        P(),
        P(),
        P(("lat", "lon"), None),
        P(None, ("lat", "lon")),
        P(None, ("lat", "lon")),
        P(("lat", "lon")),
        P(("lat", "lon")),
    )
    out_specs = (P("lat", "lon", None), P(("lat", "lon")))
    return jax.shard_map(
        on_device, mesh=mesh, in_specs=in_specs, out_specs=out_specs, check_vma=False
    )
```
